32 devices in a mesh: bricks: 32 (over z, y, x, core).
Axes of the slice: x: 2, y: 2, z: 4, core: 2. Of those that a mesh axis runs over, the one named last changes fastest.
Arguments:
- calcium: float32 [64, 32, 1024], P('bricks'), may hold values from 0.2 to 1.5
- buffer: float32 [64, 32, 1024], P('bricks'), may hold values from 0.1 to 1.5
- fraction: float32 [64, 32, 1024], P('bricks'), may hold values from 0.1 to 0.4
- rates: float32 [64, 3, 2], P('bricks'), may hold values from 2 to 64
- inverses: float32 [64, 3, 2, 32, 32], P('bricks'), as said below
- neighbors: int32 [3, 2, 64], replicated, may hold values from -1 to 63, as said below
- ranks: int32 [3, 64], replicated, may hold values from 0 to 31, as said below
Outputs:
- calcium_next: float32 [64, 32, 1024], P('bricks')
- buffer_next: float32 [64, 32, 1024], P('bricks')
The draws below stay inside these ranges and needn't reach their ends.
Inputs may be any that keep to these rules, and one draw needn't show every extreme that they name: neighbors[d, 0, s] and neighbors[d, 1, s] are the slots of the active bricks adjacent to slot s before and after it along dimension d of a block of 32 x 16 x 2 brick positions, -1 where that position is inactive or outside; active bricks fill whole rows along the first dimension. ranks[d, s] is the number of consecutive active bricks before slot s along dimension d. inverses[s, d, k] is the inverse of I + rates[s, d, k] K, K the 32 x 32 second difference with diagonal 1, 2, ..., 2, 1 and off-diagonals -1.
All inputs are finite; a program needn't handle non-finite values.
Results may differ from the reference program's by a relative error of at most 0.00015.
Values sent between devices are 32-bit elements; how exact they have to be, the bound alone decides.
No kernel may reach another device: no remote copies, remote signals or barrier semaphores. Data moves between devices by JAX's collectives and lax.ppermute only.
A program may use at most 128 MiB of HBM per device.

```python
import math
import jax
import jax.numpy as jnp
from jax import lax

BS = 32
GX = 32
GY = 16
NB = 64
ROWS = 2
GZ = 2


def chain_tables(key):
    key_start, key_cells, key_slots = jax.random.split(jax.random.fold_in(key, 7), 3)
    cells_all = GY * GZ
    run_length = max(2, 3 * ROWS // 4)
    y_start = jax.random.randint(key_start, (), 0, GY).astype(jnp.int32)
    cell_id = jnp.arange(cells_all, dtype=jnp.int32)
    along = (cell_id - y_start * GZ) % cells_all
    shuffled = jax.random.permutation(key_cells, cells_all).astype(jnp.int32)
    score = jnp.where(along < run_length, along, run_length + shuffled)
    cells = jnp.argsort(score)[:ROWS].astype(jnp.int32)
    brick = jnp.arange(NB, dtype=jnp.int32)
    cell = cells[brick // GX].astype(jnp.int32)
    position = jnp.stack([brick % GX, cell // GZ, cell % GZ], 0)
    slot = jax.random.permutation(key_slots, NB).astype(jnp.int32)
    grid = jnp.full((GX, GY, GZ), -1, jnp.int32).at[position[0], position[1], position[2]].set(slot)
    extent = [GX, GY, GZ]
    near_rows = []
    rank_rows = []
    for d in range(3):
        sides = []
        for delta in (-1, 1):
            moved = position.at[d].add(delta)
            inside = (moved[d] >= 0) & (moved[d] < extent[d])
            clipped = [jnp.clip(moved[a], 0, extent[a] - 1) for a in range(3)]
            sides.append(jnp.where(inside, grid[clipped[0], clipped[1], clipped[2]], -1))
        near_rows.append(jnp.stack(sides, 0))
        alive = jnp.ones((NB,), jnp.int32)
        run = jnp.zeros((NB,), jnp.int32)
        for step in range(1, extent[d]):
            moved = position.at[d].add(-step)
            inside = moved[d] >= 0
            clipped = [jnp.clip(moved[a], 0, extent[a] - 1) for a in range(3)]
            occupied = jnp.where(inside & (grid[clipped[0], clipped[1], clipped[2]] >= 0), 1, 0)
            alive = alive * occupied
            run = run + alive
        rank_rows.append(run)
    near = jnp.stack(near_rows, 0)
    rank = jnp.stack(rank_rows, 0)
    near_slot = jnp.zeros((3, 2, NB), jnp.int32).at[:, :, slot].set(near)
    rank_slot = jnp.zeros((3, NB), jnp.int32).at[:, slot].set(rank)
    return (near_slot, rank_slot)


def rate_tables(key):
    inner = jax.random.fold_in(key, 11)
    rate = jnp.exp(jax.random.uniform(inner, (NB, 3, 2), jnp.float32, jnp.log(2.0), jnp.log(64.0)))
    order = jnp.arange(BS, dtype=jnp.float32)
    wave = order[:, None]
    place = order[None, :]
    basis = jnp.where(wave == 0, jnp.sqrt(1.0 / BS), jnp.sqrt(2.0 / BS) * jnp.cos(jnp.pi * wave * (place + 0.5) / BS))
    eigen = 2.0 - 2.0 * jnp.cos(jnp.pi * order / BS)
    weight = 1.0 / (1.0 + rate[..., None] * eigen)
    inverse = jnp.einsum('ja,bdsj,jc->bdsac', basis, weight, basis, precision=lax.Precision.HIGHEST)
    return (rate, inverse)


def draw_rates(key, part):
    return rate_tables(key)[0]


def draw_inverses(key, part):
    return rate_tables(key)[1]


def draw_neighbors(key, part):
    return chain_tables(key)[0]


def draw_ranks(key, part):
    return chain_tables(key)[1]


def block_levels(key, shape, cuts, smallest, top_value):
    factor_of = 1.0
    for dim, blocks in cuts:
        steps = jax.random.uniform(jax.random.fold_in(jax.random.fold_in(key, 6), dim), (blocks,), jnp.float32, smallest / len(cuts), top_value / len(cuts))
        factor_of = factor_of * jnp.repeat(jnp.exp(steps), shape[dim] // blocks).reshape((-1,) + (1,) * (len(shape) - 1 - dim))
    return factor_of


def setup_inputs(seed: int = 0) -> dict:
    streams_of = jax.random.split(jax.random.key(seed), 8)
    calcium = jnp.clip(0.2 + 1.3 * jax.random.uniform(streams_of[0], (NB, BS, BS * BS), jnp.float32) ** block_levels(streams_of[0], (NB, BS, BS * BS), ((0, 32),), -0.2, 0.2), 0.2, 1.5)
    buffer = jnp.clip(0.1 + 1.4 * jax.random.uniform(streams_of[1], (NB, BS, BS * BS), jnp.float32) ** block_levels(streams_of[1], (NB, BS, BS * BS), ((0, 32),), -0.2, 0.2), 0.1, 1.5)
    fraction = jnp.clip(jnp.exp(math.log(0.4) - 1.3862944 * jax.random.uniform(streams_of[2], (NB, BS, BS * BS), jnp.float32) ** block_levels(streams_of[2], (NB, BS, BS * BS), ((0, 32),), -0.2, 0.2)), 0.1, 0.4)
    rates = draw_rates(jax.random.fold_in(streams_of[7], 71), 0)
    inverses = draw_inverses(jax.random.fold_in(streams_of[7], 71), 0)
    neighbors = draw_neighbors(jax.random.fold_in(streams_of[7], 71), 0)
    ranks = draw_ranks(jax.random.fold_in(streams_of[7], 71), 0)
    return dict(calcium=calcium, buffer=buffer, fraction=fraction, rates=rates, inverses=inverses, neighbors=neighbors, ranks=ranks)


KON = 0.5
KOFF = 0.3
BTOT = 2.0
INFLUX = 0.1


def fetch(table, index):
    rows = jnp.take(table, jnp.maximum(index, 0), axis=0)
    has = (index >= 0).reshape((-1,) + (1,) * (rows.ndim - 1))
    return jnp.where(has, rows, jnp.zeros_like(rows))


def lookup(planes, before, after):
    sides = []
    for d in range(3):
        lower = fetch(planes[:, d, 1], before[d])
        upper = fetch(planes[:, d, 0], after[d])
        sides.append(jnp.stack([lower, upper], 1))
    return jnp.stack(sides, 1)


def coupling(rate_all, neighbors):
    per_dim = []
    for d in range(3):
        mine = rate_all[:, d]
        sides = []
        for side in range(2):
            other = fetch(mine, neighbors[d, side])
            has = (neighbors[d, side] >= 0)[:, None]
            sides.append(jnp.where(has, 2.0 * mine * other / (mine + other), jnp.zeros_like(mine)))
        per_dim.append(jnp.stack(sides, 1))
    return jnp.stack(per_dim, 1)


def end_planes(field):
    count, edge = field.shape[0], field.shape[2]
    per_dim = []
    for d in range(3):
        first = lax.index_in_dim(field, 0, 2 + d, False).reshape(count, 2, edge * edge)
        last = lax.index_in_dim(field, edge - 1, 2 + d, False).reshape(count, 2, edge * edge)
        per_dim.append(jnp.stack([first, last], 1))
    return jnp.stack(per_dim, 1)


def operator(field, d, rate, glow, gup, hlow, hup):
    axis = 2 + d
    edge = field.shape[axis]
    plane_shape = lax.index_in_dim(field, 0, axis, False).shape
    lower_face = jnp.expand_dims(hlow.reshape(plane_shape), axis)
    upper_face = jnp.expand_dims(hup.reshape(plane_shape), axis)
    upper = jnp.concatenate([lax.slice_in_dim(field, 1, edge, axis=axis), upper_face], axis)
    lower = jnp.concatenate([lower_face, lax.slice_in_dim(field, 0, edge - 1, axis=axis)], axis)
    place = lax.broadcasted_iota(jnp.int32, field.shape, axis)
    inner = rate[:, :, None, None, None]
    c_up = jnp.where(place == edge - 1, gup[:, :, None, None, None], inner)
    c_down = jnp.where(place == 0, glow[:, :, None, None, None], inner)
    return c_up * (upper - field) + c_down * (lower - field)


def reaction(field, fraction):
    count, edge = field.shape[0], field.shape[2]
    alpha = fraction.reshape(count, edge, edge, edge)
    calc, bound = field[:, 0], field[:, 1]
    bind = KON * calc * (BTOT - bound) - KOFF * bound
    return jnp.stack([-bind + INFLUX * (1.0 - alpha) / alpha, bind], 1)


def apply_inverse(block, field, d):
    forms = ["psab,psbjk->psajk", "psab,psibk->psiak", "psab,psijb->psija"]
    return jnp.einsum(forms[d], block, field, precision=lax.Precision.HIGHEST)


def line_ends(field, d):
    count, edge = field.shape[0], field.shape[2]
    first = lax.index_in_dim(field, 0, 2 + d, False).reshape(count, 2, edge * edge)
    last = lax.index_in_dim(field, edge - 1, 2 + d, False).reshape(count, 2, edge * edge)
    return jnp.stack([first, last], 2)


def reduced_solve(ends, glow, gup, corner, before, after, rank, levels):
    v_first, v_last, w_first, w_last = corner[..., 0], corner[..., 1], corner[..., 2], corner[..., 3]
    a00 = 1.0 + glow * v_first
    a01 = gup * w_first
    a10 = glow * v_last
    a11 = 1.0 + gup * w_last
    lq0 = -glow * v_first
    lq1 = -glow * v_last
    up0 = -gup * w_first
    up1 = -gup * w_last
    y0 = ends[:, :, 0]
    y1 = ends[:, :, 1]
    has_b = before >= 0
    has_a = after >= 0
    idx_b = jnp.maximum(before, 0)
    idx_a = jnp.maximum(after, 0)

    def forward(t, carry):
        e0, e1, f0, f1 = carry
        fq = jnp.where(has_b[:, None], jnp.take(f1, idx_b, axis=0), jnp.zeros_like(f1))
        eq = jnp.where(has_b[:, None, None], jnp.take(e1, idx_b, axis=0), jnp.zeros_like(e1))
        b00 = a00 - lq0 * fq
        b10 = a10 - lq1 * fq
        z0 = y0 - lq0[:, :, None] * eq
        z1 = y1 - lq1[:, :, None] * eq
        det = b00 * a11 - a01 * b10
        n_e0 = (a11[:, :, None] * z0 - a01[:, :, None] * z1) / det[:, :, None]
        n_e1 = (b00[:, :, None] * z1 - b10[:, :, None] * z0) / det[:, :, None]
        n_f0 = (a11 * up0 - a01 * up1) / det
        n_f1 = (b00 * up1 - b10 * up0) / det
        now = rank == t
        return (jnp.where(now[:, None, None], n_e0, e0), jnp.where(now[:, None, None], n_e1, e1),
                jnp.where(now[:, None], n_f0, f0), jnp.where(now[:, None], n_f1, f1))

    start = (jnp.zeros_like(y0), jnp.zeros_like(y1), jnp.zeros_like(a00), jnp.zeros_like(a00))
    e0, e1, f0, f1 = lax.fori_loop(0, levels, forward, start)

    def backward(step, carry):
        t = levels - 1 - step
        zp, zq = carry
        pn = jnp.where(has_a[:, None, None], jnp.take(zp, idx_a, axis=0), jnp.zeros_like(zp))
        new_p = e0 - f0[:, :, None] * pn
        new_q = e1 - f1[:, :, None] * pn
        now = (rank == t)[:, None, None]
        return (jnp.where(now, new_p, zp), jnp.where(now, new_q, zq))

    zp, zq = lax.fori_loop(0, levels, backward, (jnp.zeros_like(y0), jnp.zeros_like(y1)))
    low = jnp.where(has_b[:, None, None], zp - jnp.take(zq, idx_b, axis=0), jnp.zeros_like(zp))
    high = jnp.where(has_a[:, None, None], zq - jnp.take(zp, idx_a, axis=0), jnp.zeros_like(zq))
    return jnp.stack([low, high], 2)


def correct(local, block, glow, gup, jumps, d):
    axis = 2 + d
    count, edge = local.shape[0], local.shape[2]
    shape_v = [count, 2, 1, 1, 1]
    shape_v[axis] = edge
    first_col = block[..., 0].reshape(shape_v)
    last_col = block[..., edge - 1].reshape(shape_v)
    plane_shape = lax.index_in_dim(local, 0, axis, False).shape
    low = jnp.expand_dims(jumps[:, :, 0].reshape(plane_shape), axis)
    high = jnp.expand_dims(jumps[:, :, 1].reshape(plane_shape), axis)
    return local - glow[:, :, None, None, None] * low * first_col - gup[:, :, None, None, None] * high * last_col


def reference(calcium, buffer, fraction, rates, inverses, neighbors, ranks):
    count, edge = calcium.shape[0], calcium.shape[1]
    levels = [GX, GY, GZ]
    couple = coupling(rates, neighbors)
    corner = jnp.stack([inverses[..., 0, 0], inverses[..., edge - 1, 0], inverses[..., 0, edge - 1], inverses[..., edge - 1, edge - 1]], -1)
    field = jnp.stack([calcium, buffer], 1).reshape(count, 2, edge, edge, edge)
    halos = lookup(end_planes(field), neighbors[:, 0], neighbors[:, 1])
    lams = [operator(field, d, rates[:, d], couple[:, d, 0], couple[:, d, 1], halos[:, d, 0], halos[:, d, 1]) for d in range(3)]
    rhs = field + lams[0] + 2.0 * lams[1] + 2.0 * lams[2] + reaction(field, fraction)

    def solve(right, d):
        block = inverses[:, d]
        local = apply_inverse(block, right, d)
        jumps = reduced_solve(line_ends(local, d), couple[:, d, 0], couple[:, d, 1], corner[:, d], neighbors[d, 0], neighbors[d, 1], ranks[d], levels[d])
        return correct(local, block, couple[:, d, 0], couple[:, d, 1], jumps, d)

    first = solve(rhs, 0)
    second = solve(first - lams[1], 1)
    third = solve(second - lams[2], 2)
    result = third.reshape(count, 2, edge, edge * edge)
    return result[:, 0], result[:, 1]
```

```python
from functools import partial
import math

import jax
import jax.numpy as jnp
import numpy as np
from jax import lax
from jax.experimental import pallas as pl
from jax.experimental.pallas import tpu as pltpu
from jax.sharding import PartitionSpec as P

GX = 32


KON = 0.5
KOFF = 0.3
BTOT = 2.0
INFLUX = 0.1


def fetch(table, index):
    rows = jnp.take(table, jnp.maximum(index, 0), axis=0)
    has = (index >= 0).reshape((-1,) + (1,) * (rows.ndim - 1))
    return jnp.where(has, rows, jnp.zeros_like(rows))


def lookup(planes, before, after):
    sides = []
    for d in range(3):
        lower = fetch(planes[:, d, 1], before[d])
        upper = fetch(planes[:, d, 0], after[d])
        sides.append(jnp.stack([lower, upper], 1))
    return jnp.stack(sides, 1)


def coupling(rate_all, neighbors):
    per_dim = []
    for d in range(3):
        mine = rate_all[:, d]
        sides = []
        for side in range(2):
            other = fetch(mine, neighbors[d, side])
            has = (neighbors[d, side] >= 0)[:, None]
            sides.append(jnp.where(has, 2.0 * mine * other / (mine + other), jnp.zeros_like(mine)))
        per_dim.append(jnp.stack(sides, 1))
    return jnp.stack(per_dim, 1)


def end_planes(field):
    count, edge = (field.shape[0], field.shape[2])
    per_dim = []
    for d in range(3):
        first = lax.index_in_dim(field, 0, 2 + d, False).reshape(count, 2, edge * edge)
        last = lax.index_in_dim(field, edge - 1, 2 + d, False).reshape(count, 2, edge * edge)
        per_dim.append(jnp.stack([first, last], 1))
    return jnp.stack(per_dim, 1)


def operator(field, d, rate, glow, gup, hlow, hup):
    axis = 2 + d
    edge = field.shape[axis]
    plane_shape = lax.index_in_dim(field, 0, axis, False).shape
    lower_face = jnp.expand_dims(hlow.reshape(plane_shape), axis)
    upper_face = jnp.expand_dims(hup.reshape(plane_shape), axis)
    upper = jnp.concatenate([lax.slice_in_dim(field, 1, edge, axis=axis), upper_face], axis)
    lower = jnp.concatenate([lower_face, lax.slice_in_dim(field, 0, edge - 1, axis=axis)], axis)
    place = lax.broadcasted_iota(jnp.int32, field.shape, axis)
    inner = rate[:, :, None, None, None]
    c_up = jnp.where(place == edge - 1, gup[:, :, None, None, None], inner)
    c_down = jnp.where(place == 0, glow[:, :, None, None, None], inner)
    return c_up * (upper - field) + c_down * (lower - field)


def reaction(field, fraction):
    count, edge = (field.shape[0], field.shape[2])
    alpha = fraction.reshape(count, edge, edge, edge)
    calc, bound = (field[:, 0], field[:, 1])
    bind = KON * calc * (BTOT - bound) - KOFF * bound
    return jnp.stack([-bind + INFLUX * (1.0 - alpha) / alpha, bind], 1)


def apply_inverse(block, field, d):
    forms = ["psab,psbjk->psajk", "psab,psibk->psiak", "psab,psijb->psija"]
    return jnp.einsum(forms[d], block, field, precision=lax.Precision.HIGHEST)


def line_ends(field, d):
    count, edge = (field.shape[0], field.shape[2])
    first = lax.index_in_dim(field, 0, 2 + d, False).reshape(count, 2, edge * edge)
    last = lax.index_in_dim(field, edge - 1, 2 + d, False).reshape(count, 2, edge * edge)
    return jnp.stack([first, last], 2)


def block_terms(glow, gup, corner):
    v_first, v_last, w_first, w_last = (
        corner[..., 0],
        corner[..., 1],
        corner[..., 2],
        corner[..., 3],
    )
    a00 = 1.0 + glow * v_first
    a01 = gup * w_first
    a10 = glow * v_last
    a11 = 1.0 + gup * w_last
    lq0 = -glow * v_first
    lq1 = -glow * v_last
    up0 = -gup * w_first
    up1 = -gup * w_last
    return (a00, a01, a10, a11, lq0, lq1, up0, up1)


def chain_order(before, rank):
    slots = jnp.arange(before.shape[0], dtype=jnp.int32)
    pointer = jnp.where(before >= 0, before, slots)
    for step in range(GX.bit_length()):
        pointer = jnp.take(pointer, pointer, axis=0)
    sort_key = pointer * GX + rank
    order = jnp.argsort(sort_key)
    inverse_order = jnp.argsort(order)
    return (order, inverse_order)


def shift_down(values):
    return jnp.concatenate([jnp.zeros_like(values[:1]), values[:-1]], 0)


def shift_up(values):
    return jnp.concatenate([values[1:], jnp.zeros_like(values[:1])], 0)


def compose_maps(first_map, second_map):
    e00, e01, e10, e11 = first_map
    l00, l01, l10, l11 = second_map
    n00 = l00 * e00 + l01 * e10
    n01 = l00 * e01 + l01 * e11
    n10 = l10 * e00 + l11 * e10
    n11 = l10 * e01 + l11 * e11
    scale = jnp.abs(n00) + jnp.abs(n01) + jnp.abs(n10) + jnp.abs(n11)
    return (n00 / scale, n01 / scale, n10 / scale, n11 / scale)


def compose_affine(first_map, second_map):
    first_q, first_p = first_map
    second_q, second_p = second_map
    return (first_q * second_q, second_p + second_q * first_p)


def sorted_solve(glow, gup, corner, before, after, order, inverse_order, ends):
    glow = jnp.take(glow, order, axis=0)
    gup = jnp.take(gup, order, axis=0)
    corner = jnp.take(corner, order, axis=0)
    has_b = jnp.take(before, order, axis=0) >= 0
    has_a = jnp.take(after, order, axis=0) >= 0
    arranged = jnp.take(ends, order, axis=0)
    y0 = arranged[:, :, 0]
    y1 = arranged[:, :, 1]
    a00, a01, a10, a11, lq0, lq1, up0, up1 = block_terms(glow, gup, corner)
    maps = (
        -(lq0 * up1 - lq1 * up0),
        a00 * up1 - a10 * up0,
        -(lq0 * a11 - a01 * lq1),
        a00 * a11 - a01 * a10,
    )
    summed = lax.associative_scan(compose_maps, maps, axis=0)
    f1_prev = summed[1] / summed[3]
    fq = shift_down(f1_prev)
    b00 = a00 - lq0 * fq
    b10 = a10 - lq1 * fq
    det = b00 * a11 - a01 * b10
    f0 = (a11 * up0 - a01 * up1) / det
    f1 = (b00 * up1 - b10 * up0) / det
    slope = (-(b00 * lq1 - b10 * lq0) / det)[:, :, None]
    offset = (b00[:, :, None] * y1 - b10[:, :, None] * y0) / det[:, :, None]
    e1 = lax.associative_scan(compose_affine, (slope, offset), axis=0)[1]
    eq = shift_down(e1)
    e0 = (
        a11[:, :, None] * y0 - a01[:, :, None] * y1 - (a11 * lq0 - a01 * lq1)[:, :, None] * eq
    ) / det[:, :, None]
    zp = lax.associative_scan(compose_affine, (-f0[:, :, None], e0), reverse=True, axis=0)[1]
    pn = shift_up(zp)
    zq = e1 - f1[:, :, None] * pn
    low = jnp.where(has_b[:, None, None], zp - shift_down(zq), jnp.zeros_like(zp))
    high = jnp.where(has_a[:, None, None], zq - pn, jnp.zeros_like(zq))
    return jnp.take(jnp.stack([low, high], 2), inverse_order, axis=0)


def correct(local, block, glow, gup, jumps, d):
    axis = 2 + d
    count, edge = (local.shape[0], local.shape[2])
    shape_v = [count, 2, 1, 1, 1]
    shape_v[axis] = edge
    first_col = block[..., 0].reshape(shape_v)
    last_col = block[..., edge - 1].reshape(shape_v)
    plane_shape = lax.index_in_dim(local, 0, axis, False).shape
    low = jnp.expand_dims(jumps[:, :, 0].reshape(plane_shape), axis)
    high = jnp.expand_dims(jumps[:, :, 1].reshape(plane_shape), axis)
    return (
        local
        - glow[:, :, None, None, None] * low * first_col
        - gup[:, :, None, None, None] * high * last_col
    )


def general_body(calcium, buffer, fraction, rates, inverses, neighbors, ranks):
    count, edge = (calcium.shape[0], calcium.shape[1])
    devices = lax.axis_size("bricks")
    square = edge * edge
    per_device = square // devices
    start = lax.axis_index("bricks") * count
    corners = jnp.stack(
        [
            inverses[..., 0, 0],
            inverses[..., edge - 1, 0],
            inverses[..., 0, edge - 1],
            inverses[..., edge - 1, edge - 1],
        ],
        -1,
    )
    rate_all, corner_all = (
        lax.all_gather(rates, "bricks", axis=0, tiled=True),
        lax.all_gather(corners, "bricks", axis=0, tiled=True),
    )
    couple_all = coupling(rate_all, neighbors)
    couple = lax.dynamic_slice_in_dim(couple_all, start, count, 0)
    field = jnp.stack([calcium, buffer], 1).reshape(count, 2, edge, edge, edge)
    planes = end_planes(field).reshape(count, 3, 2, 2, devices, per_device)
    lined = lookup(
        lax.all_to_all(planes, "bricks", split_axis=4, concat_axis=0, tiled=True),
        neighbors[:, 0],
        neighbors[:, 1],
    )
    halos = lax.all_to_all(lined, "bricks", split_axis=0, concat_axis=4, tiled=True).reshape(
        count, 3, 2, 2, square
    )
    lams = [
        operator(
            field, d, rates[:, d], couple[:, d, 0], couple[:, d, 1], halos[:, d, 0], halos[:, d, 1]
        )
        for d in range(3)
    ]
    rhs = field + lams[0] + 2.0 * lams[1] + 2.0 * lams[2] + reaction(field, fraction)

    def solve(right, d):
        block = inverses[:, d]
        local = apply_inverse(block, right, d)
        ends = line_ends(local, d).reshape(count, 2, 2, devices, per_device)
        order, inverse_order = chain_order(neighbors[d, 0], ranks[d])
        chain_fn = partial(
            sorted_solve,
            couple_all[:, d, 0],
            couple_all[:, d, 1],
            corner_all[:, d],
            neighbors[d, 0],
            neighbors[d, 1],
            order,
            inverse_order,
        )
        lined_jumps = chain_fn(
            lax.all_to_all(ends, "bricks", split_axis=3, concat_axis=0, tiled=True)[:, :, :, 0]
        )[:, :, :, None]
        jumps = lax.all_to_all(
            lined_jumps, "bricks", split_axis=0, concat_axis=3, tiled=True
        ).reshape(count, 2, 2, square)
        return correct(local, block, couple[:, d, 0], couple[:, d, 1], jumps, d)

    first = solve(rhs, 0)
    second = solve(first - lams[1], 1)
    third = solve(second - lams[2], 2)
    result = third.reshape(count, 2, edge, edge * edge)
    return (result[:, 0], result[:, 1])


LANES = 128


def cosine_basis(edge):
    wave = np.arange(edge)[:, None]
    place = np.arange(edge)[None, :]
    basis = np.sqrt(2.0 / edge) * np.cos(np.pi * wave * (place + 0.5) / edge)
    basis[0] = math.sqrt(1.0 / edge)
    eigen = 2.0 - 2.0 * np.cos(np.pi * np.arange(edge) / edge)
    return basis, eigen


def dot(a, b):
    return jnp.dot(a, b, precision=lax.Precision.HIGHEST, preferred_element_type=jnp.float32)


def dot_lanes(a, b):
    return lax.dot_general(
        a, b, (((1,), (1,)), ((), ())), precision=lax.Precision.HIGHEST, preferred_element_type=jnp.float32
    )


def lane_of(shape):
    return lax.broadcasted_iota(jnp.int32, shape, len(shape) - 1)


def swap_blocks(four):
    x0, x1, x2, x3 = four
    lane = lane_of(x0.shape)
    low = (lane & 64) == 0
    y0, y2 = jnp.where(low, x0, pltpu.roll(x2, 64, 1)), jnp.where(low, pltpu.roll(x0, 64, 1), x2)
    y1, y3 = jnp.where(low, x1, pltpu.roll(x3, 64, 1)), jnp.where(low, pltpu.roll(x1, 64, 1), x3)
    even = (lane & 32) == 0
    z0, z1 = jnp.where(even, y0, pltpu.roll(y1, 32, 1)), jnp.where(even, pltpu.roll(y0, 96, 1), y1)
    z2, z3 = jnp.where(even, y2, pltpu.roll(y3, 32, 1)), jnp.where(even, pltpu.roll(y2, 96, 1), y3)
    return [z0, z1, z2, z3]


def swap_rows(source, base, scratch, at, edge):
    tiles = edge // 4
    for c in range(tiles):
        rows = [source[pl.ds(base + edge * c + g, tiles, stride=4), :] for g in range(4)]
        for t4, row in enumerate(swap_blocks(rows)):
            scratch[pl.ds(at + 4 * c + t4, tiles, stride=edge), :] = row


def tile_rows(x, edge):
    tiles = edge // 4
    return jnp.concatenate([x[:, LANES * c : LANES * (c + 1)] for c in range(tiles)], 0)


def wide(ref, at, edge):
    tiles = edge // 4
    return jnp.concatenate([ref[pl.ds(at + edge * c, edge), :] for c in range(tiles)], 1)


def swap_inner(ref, edge):
    tiles = edge // 4
    size = tiles * edge
    count = ref.shape[0] // size
    fields = [ref[pl.ds(size * f, size), :] for f in range(count)]
    whole = [
        jnp.concatenate([field[edge * c : edge * (c + 1)] for field in fields], 0) for c in range(tiles)
    ]
    row = lax.broadcasted_iota(jnp.int32, (LANES, LANES), 0)
    lane = lane_of((LANES, LANES))
    for to in range(tiles):
        total = jnp.zeros((count * edge, LANES), jnp.float32)
        for c in range(tiles):
            hit = ((row & (edge - 1)) == 4 * to + lane // edge) & ((lane & (edge - 1)) == 4 * c + row // edge)
            total = total + dot(whole[c], hit.astype(jnp.float32))
        for f in range(count):
            ref[pl.ds(size * f + edge * to, edge), :] = total[edge * f : edge * (f + 1)]


def normal_of(near, slot):
    along_j = (near[1, 0, slot] >= 0) | (near[1, 1, slot] >= 0)
    return jnp.where(along_j, 1, 2)


def local_kernel(near, rates, calcium, buffer, fraction, inverses, ends_of, faces_of, msg, base, us, al, work, other):
    count, edge = calcium.shape[0], calcium.shape[1]
    tiles = edge // 4
    size = tiles * edge
    first_slot = lax.axis_index("bricks") * count
    normal = normal_of(near, first_slot)
    closed = 3 - normal
    for b in range(count):
        us[pl.ds(size * 2 * b, size), :] = tile_rows(calcium[b], edge)
        us[pl.ds(size * (2 * b + 1), size), :] = tile_rows(buffer[b], edge)
        al[pl.ds(size * b, size), :] = tile_rows(fraction[b], edge)

    @pl.when(normal == 1)
    def _():
        swap_inner(us, edge)
        swap_inner(al, edge)

    lane = lane_of((edge, LANES))
    inner = lane & (edge - 1)
    square_row = lax.broadcasted_iota(jnp.int32, (LANES, LANES), 0)
    square_lane = lane_of((LANES, LANES))
    on_block = (square_row // edge) == (square_lane // edge)
    faces_u, faces_y, ends0, ends1 = [], [], [], []
    for b in range(count):
        slot = first_slot + b
        face = jnp.where(near[normal, 1, slot] >= 0, edge - 1, 0)
        calc = [us[pl.ds(size * 2 * b + edge * c, edge), :] for c in range(tiles)]
        bound = [us[pl.ds(size * (2 * b + 1) + edge * c, edge), :] for c in range(tiles)]
        alpha = [al[pl.ds(size * b + edge * c, edge), :] for c in range(tiles)]
        bind = [KON * x * (BTOT - y) - KOFF * y for x, y in zip(calc, bound)]
        source_calc = [-w + INFLUX * (1.0 - a) / a for w, a in zip(bind, alpha)]
        for q, (u, source) in enumerate(((calc, source_calc), (bound, bind))):
            at = size * (2 * b + q)
            rate_t, rate_n = rates[b, closed, q], rates[b, normal, q]
            ahead = [pltpu.roll(x, LANES - edge, 1) for x in u]
            behind = [pltpu.roll(x, edge, 1) for x in u]
            f = []
            for c in range(tiles):
                x = u[c]
                next_t = jnp.where(lane < LANES - edge, ahead[c], ahead[c + 1] if c + 1 < tiles else x)
                last_t = jnp.where(lane >= edge, behind[c], behind[c - 1] if c else x)
                next_n = jnp.where(inner == edge - 1, x, pltpu.roll(x, LANES - 1, 1))
                last_n = jnp.where(inner == 0, x, pltpu.roll(x, 1, 1))
                along = rate_t * (next_t + last_t - 2.0 * x) + rate_n * (next_n + last_n - 2.0 * x)
                f.append(2.0 * x + 2.0 * along + source[c])
            g = dot(inverses[b, 0, q], jnp.concatenate(f, 1))
            for c in range(tiles):
                work[pl.ds(edge * c, edge), :] = g[:, LANES * c : LANES * (c + 1)]
            ends0.append(work[pl.ds(0, tiles, stride=edge), :])
            ends1.append(work[pl.ds(edge - 1, tiles, stride=edge), :])
            w = tile_rows(g, edge) - 2.0 * us[pl.ds(at, size), :]
            block = inverses[b, normal, q]
            block = jnp.concatenate([block] * 4, 1)
            block = jnp.where(on_block, jnp.concatenate([block] * 4, 0), 0.0)
            y = dot(w, block)
            work[pl.ds(0, size), :] = y
            face_u = jnp.zeros((edge, LANES), jnp.float32)
            face_y = jnp.zeros((edge, LANES), jnp.float32)
            for c in range(tiles):
                shift = (c - face) & (LANES - 1)
                face_u = face_u + jnp.where(inner == c, pltpu.roll(u[c], shift, 1), 0.0)
                face_y = face_y + jnp.where(inner == c, pltpu.roll(y[edge * c : edge * (c + 1)], shift, 1), 0.0)
            faces_u.append(face_u)
            faces_y.append(face_y)
            swap_rows(work, 0, other, 0, edge)
            solved = dot(inverses[b, closed, q], wide(other, 0, edge))
            for c in range(tiles):
                other[pl.ds(edge * c, edge), :] = solved[:, LANES * c : LANES * (c + 1)]
            swap_rows(other, 0, work, 0, edge)
            base[pl.ds(at, size), :] = us[pl.ds(at, size), :] + work[pl.ds(0, size), :]

    stack0 = jnp.concatenate(swap_blocks(ends0), 0)
    stack1 = jnp.concatenate(swap_blocks(ends1), 0)
    both = dot(ends_of[...], jnp.concatenate([stack0, stack1], 1))
    part_u = dot_lanes(faces_of[...], jnp.concatenate(faces_u, 0))
    part_y = dot_lanes(faces_of[...], jnp.concatenate(faces_y, 0))
    fields = swap_blocks([both[:, :LANES], both[:, LANES:], part_u, part_y])
    for x, part in enumerate(fields):
        msg[pl.ds(x, edge, stride=8), :] = part
    for b in range(count):
        for q in range(2):
            row = jnp.where(
                lane == 0,
                rates[b, 0, q],
                jnp.where(lane == 1, rates[b, closed, q], jnp.where(lane == 2, rates[b, normal, q], 0.0)),
            )
            msg[pl.ds(4 + 2 * b + q, edge, stride=8), :] = row


def owner_kernel(near, eigen_of, recv, basis, turned, eigen, out, rows, tail, order):
    edge = basis.shape[0]
    slots = near.shape[2]
    me = lax.axis_index("bricks")

    def find(s, heads):
        is_head = near[0, 0, s] < 0
        low, high = heads
        return jnp.where(is_head & (low < 0), s, low), jnp.where(is_head, s, high)

    low, high = lax.fori_loop(0, slots, find, (jnp.int32(-1), jnp.int32(-1)))

    def walk(x, at):
        for row in range(2):
            slot = at[row]
            place = row * edge + x
            order[place] = slot
            start = 8 * (slot // 2) + 2 * (slot % 2)
            rows[pl.ds(place, 2, stride=2 * edge), :] = recv[pl.ds(start, 2), :]
            tail[pl.ds(place, 2, stride=2 * edge), :] = recv[pl.ds(start + 4, 2), :]
        return tuple(jnp.maximum(near[0, 1, slot], 0) for slot in at)

    lax.fori_loop(0, edge, walk, (low, high))
    normal = normal_of(near, low)
    up = near[normal, 1, low] >= 0
    touch = up | (near[normal, 0, low] >= 0)
    face0 = jnp.where(up, edge - 1, 0)
    face1 = jnp.where(up, 0, edge - 1)

    parts = rows[...].T
    y0, y1, face_u, face_y = (parts[edge * x : edge * (x + 1)] for x in range(4))
    params = tail[...].T
    rate_0, rate_t, rate_n = params[0:1], params[1:2], params[2:3]

    lane = lane_of((1, LANES))
    place = lane & (edge - 1)
    first_row = (lane & edge) == 0
    face = jnp.where(first_row, face0, face1)
    v = basis[...]
    vt = turned[...]
    lam = eigen[...]

    def partner(x):
        return jnp.where(first_row, pltpu.roll(x, LANES - edge, 1), pltpu.roll(x, edge, 1))

    def after(x, s=1):
        return pltpu.roll(x, LANES - s, 1)

    def before(x, s=1):
        return pltpu.roll(x, s, 1)

    damp_0 = 1.0 / (1.0 + lam * rate_0)
    damp_n = 1.0 / (1.0 + lam * rate_n)
    damp_t = 1.0 / (1.0 + eigen_of[me] * rate_t)
    other_n = partner(rate_n)
    g = jnp.where(touch, 2.0 * rate_n * other_n / (rate_n + other_n), 0.0)
    cross = 2.0 * g * (partner(face_u) - face_u)
    first_vec = vt[0:edge, 0:1]
    last_vec = vt[edge - 1 : edge, :]
    v_first, v_last = v[:, 0:1], v[:, edge - 1 : edge]
    pieces = dot(
        vt,
        jnp.concatenate(
            [
                damp_0 * dot(v, cross),
                damp_0 * v_first,
                damp_0 * v_last,
                damp_n * jnp.where(face == 0, v_first, v_last),
            ],
            1,
        ),
    )
    spread, col_0, col_1, col_n = (pieces[:, LANES * x : LANES * (x + 1)] for x in range(4))
    depth = lax.broadcasted_iota(jnp.int32, (edge, LANES), 0)
    at_face = depth == face
    y0 = y0 + jnp.where(at_face, spread[0:1], 0.0)
    y1 = y1 + jnp.where(at_face, spread[edge - 1 : edge], 0.0)

    near_c, far_c = col_0[0:1], col_0[edge - 1 : edge]
    inv_rate = 1.0 / rate_0
    open_face = place < edge - 1
    diag = jnp.where(open_face, 0.5 * (inv_rate + after(inv_rate)) + near_c + after(near_c), 1.0)
    lower = jnp.where(open_face & (place > 0), -far_c, 0.0)
    upper = jnp.where(place < edge - 2, -after(far_c), 0.0)
    right = jnp.where(open_face, y1 - after(y0), 0.0)
    step = 1
    while step < edge:
        back = -lower / before(diag, step)
        fore = -upper / after(diag, step)
        diag = diag + back * before(upper, step) + fore * after(lower, step)
        right = right + back * before(right, step) + fore * after(right, step)
        lower = back * before(lower, step)
        upper = fore * after(upper, step)
        step *= 2
    flux_up = right / diag
    flux_down = jnp.where(place > 0, before(flux_up), 0.0)

    end_n = jnp.where(face == 0, col_n[0:1], col_n[edge - 1 : edge])
    weight_down = jnp.sum(col_n * flux_down, 0, keepdims=True)
    weight_up = jnp.sum(col_n * flux_up, 0, keepdims=True)
    reach = face_y
    halo = end_n * spread + col_0 * weight_down - col_1 * weight_up
    reach_t = jnp.where(normal == 2, damp_t, 1.0)
    ends = reach_t * (reach + halo)
    jump = g * (ends - partner(ends)) / (1.0 + g * (end_n + partner(end_n)))
    face_out = jnp.where(normal == 2, damp_t * spread - jump, damp_t * (spread - jump))
    lines = dot(v, jnp.concatenate([flux_down, flux_up], 1))
    lines = jnp.concatenate([damp_n, damp_n], 1) * lines
    lines = dot(vt, lines)
    packed = jnp.concatenate(
        [
            damp_t * lines[:, :LANES],
            damp_t * lines[:, LANES:],
            face_out,
            jnp.zeros((edge, LANES), jnp.float32),
        ],
        0,
    )
    rows[...] = packed.T

    def hand_out(x, carry):
        slot = order[x]
        out[pl.ds(4 * (slot // 2) + 2 * (slot % 2), 2), :] = rows[pl.ds(x, 2, stride=2 * edge), :]
        return carry

    lax.fori_loop(0, slots, hand_out, 0)


def update_kernel(near, recv, base, inverses, spread_of, calcium_next, buffer_next, work):
    count, edge = calcium_next.shape[0], calcium_next.shape[1]
    tiles = edge // 4
    size = tiles * edge
    first_slot = lax.axis_index("bricks") * count
    normal = normal_of(near, first_slot)
    lane = lane_of((edge, LANES))
    fields = [recv[pl.ds(x, edge, stride=2 * count), :] for x in range(2 * count)]
    low, high, face_part, _ = swap_blocks(fields)
    turn = jnp.concatenate([face_part, jnp.zeros((LANES - edge, LANES), jnp.float32)], 0).T[:, :edge]
    expand = wide(spread_of, 0, edge)
    face_wide = dot(turn, expand)
    group = lane // edge

    def repeat(x, at):
        x = jnp.where(group == at, x, 0.0)
        x = x + pltpu.roll(x, 64, 1)
        return x + pltpu.roll(x, 32, 1)

    for b in range(count):
        slot = first_slot + b
        face = jnp.where(near[normal, 1, slot] >= 0, edge - 1, 0)
        for q in range(2):
            x = 2 * b + q
            at = size * x
            low_x, high_x = repeat(low, x), repeat(high, x)
            col_0 = inverses[b, 0, q, :, 0:1]
            col_1 = inverses[b, 0, q, :, edge - 1 : edge]
            row_n = inverses[b, normal, q, pl.ds(face, 1), :]
            row_n = jnp.concatenate([row_n] * 4, 1)
            for c in range(tiles):
                basis_c = spread_of[pl.ds(edge * c, edge), :]
                row_low = jnp.sum(basis_c * low_x, 0, keepdims=True)
                row_high = jnp.sum(basis_c * high_x, 0, keepdims=True)
                add = face_wide[edge * x : edge * (x + 1), LANES * c : LANES * (c + 1)] * row_n
                work[pl.ds(at + edge * c, edge), :] = (
                    base[pl.ds(at + edge * c, edge), :] + col_0 * row_low - col_1 * row_high + add
                )

    @pl.when(normal == 1)
    def _():
        swap_inner(work, edge)

    for b in range(count):
        for q, ref in enumerate((calcium_next, buffer_next)):
            for c in range(tiles):
                ref[b, :, LANES * c : LANES * (c + 1)] = work[pl.ds(size * (2 * b + q) + edge * c, edge), :]


def fast_body(calcium, buffer, fraction, rates, inverses, neighbors, ranks):
    count, edge = calcium.shape[0], calcium.shape[1]
    devices = lax.axis_size("bricks")
    tiles = edge // 4
    size = tiles * edge
    f32 = jnp.float32
    basis, eigen = cosine_basis(edge)
    place = np.arange(edge)
    ends_of = np.zeros((edge, edge))
    ends_of[:, (place % 4) * tiles + place // 4] = basis
    faces_of = np.zeros((edge, LANES))
    faces_of[:, (place % 4) * edge + place // 4] = basis
    spread_of = np.repeat(basis, edge, 1).reshape(edge, tiles, LANES).transpose(1, 0, 2).reshape(size, LANES)
    smem = pl.BlockSpec(memory_space=pltpu.SMEM)
    vmem = pl.BlockSpec(memory_space=pltpu.VMEM)
    params = pltpu.CompilerParams(vmem_limit_bytes=48 * 2**20)
    const = lambda x: jnp.asarray(x, f32)

    msg, base = pl.pallas_call(
        local_kernel,
        out_shape=(
            jax.ShapeDtypeStruct((devices * 8, LANES), f32),
            jax.ShapeDtypeStruct((2 * count * size, LANES), f32),
        ),
        in_specs=[smem, smem] + [vmem] * 6,
        out_specs=(vmem, vmem),
        scratch_shapes=[
            pltpu.VMEM((2 * count * size, LANES), f32),
            pltpu.VMEM((count * size, LANES), f32),
            pltpu.VMEM((size, LANES), f32),
            pltpu.VMEM((size, LANES), f32),
        ],
        compiler_params=params,
        name="local_solutions",
    )(neighbors, rates, calcium, buffer, fraction, inverses, const(ends_of), const(faces_of))
    recv = lax.all_to_all(msg.reshape(devices, 8, LANES), "bricks", 0, 0, tiled=True)
    reply = pl.pallas_call(
        owner_kernel,
        out_shape=jax.ShapeDtypeStruct((devices * 2 * count, LANES), f32),
        in_specs=[smem, smem] + [vmem] * 4,
        out_specs=vmem,
        scratch_shapes=[
            pltpu.VMEM((LANES, LANES), f32),
            pltpu.VMEM((LANES, LANES), f32),
            pltpu.SMEM((devices * count,), jnp.int32),
        ],
        compiler_params=params,
        name="chain_and_face_solves",
    )(
        neighbors,
        const(eigen),
        recv.reshape(devices * 8, LANES),
        const(basis),
        const(basis.T),
        const(np.tile(eigen[:, None], (1, LANES))),
    )
    back = lax.all_to_all(reply.reshape(devices, 2 * count, LANES), "bricks", 0, 0, tiled=True)
    return pl.pallas_call(
        update_kernel,
        out_shape=(
            jax.ShapeDtypeStruct(calcium.shape, f32),
            jax.ShapeDtypeStruct(buffer.shape, f32),
        ),
        in_specs=[smem] + [vmem] * 4,
        out_specs=(vmem, vmem),
        scratch_shapes=[pltpu.VMEM((2 * count * size, LANES), f32)],
        compiler_params=params,
        name="rank_three_update",
    )(neighbors, back.reshape(devices * 2 * count, LANES), base, inverses, const(spread_of))


def body(calcium, buffer, fraction, rates, inverses, neighbors, ranks):
    count, edge = calcium.shape[0], calcium.shape[1]
    devices = lax.axis_size("bricks")
    if edge == GX and devices == edge and count == 2 and 4 * edge == LANES:
        return fast_body(calcium, buffer, fraction, rates, inverses, neighbors, ranks)
    return general_body(calcium, buffer, fraction, rates, inverses, neighbors, ranks)


def solution(mesh):
    in_specs = (
        P("bricks", None, None),
        P("bricks", None, None),
        P("bricks", None, None),
        P("bricks", None, None),
        P("bricks", None, None, None, None),
        P(),
        P(),
    )
    out_specs = (P("bricks", None, None), P("bricks", None, None))
    return jax.shard_map(body, mesh=mesh, in_specs=in_specs, out_specs=out_specs, check_vma=False)
```

```python
from functools import partial
import math

import jax
import jax.numpy as jnp
import numpy as np
from jax import lax
from jax.experimental import pallas as pl
from jax.experimental.pallas import tpu as pltpu
from jax.sharding import PartitionSpec as P

GX = 32


KON = 0.5
KOFF = 0.3
BTOT = 2.0
INFLUX = 0.1


def fetch(table, index):
    rows = jnp.take(table, jnp.maximum(index, 0), axis=0)
    has = (index >= 0).reshape((-1,) + (1,) * (rows.ndim - 1))
    return jnp.where(has, rows, jnp.zeros_like(rows))


def lookup(planes, before, after):
    sides = []
    for d in range(3):
        lower = fetch(planes[:, d, 1], before[d])
        upper = fetch(planes[:, d, 0], after[d])
        sides.append(jnp.stack([lower, upper], 1))
    return jnp.stack(sides, 1)


def coupling(rate_all, neighbors):
    per_dim = []
    for d in range(3):
        mine = rate_all[:, d]
        sides = []
        for side in range(2):
            other = fetch(mine, neighbors[d, side])
            has = (neighbors[d, side] >= 0)[:, None]
            sides.append(jnp.where(has, 2.0 * mine * other / (mine + other), jnp.zeros_like(mine)))
        per_dim.append(jnp.stack(sides, 1))
    return jnp.stack(per_dim, 1)


def end_planes(field):
    count, edge = (field.shape[0], field.shape[2])
    per_dim = []
    for d in range(3):
        first = lax.index_in_dim(field, 0, 2 + d, False).reshape(count, 2, edge * edge)
        last = lax.index_in_dim(field, edge - 1, 2 + d, False).reshape(count, 2, edge * edge)
        per_dim.append(jnp.stack([first, last], 1))
    return jnp.stack(per_dim, 1)


def operator(field, d, rate, glow, gup, hlow, hup):
    axis = 2 + d
    edge = field.shape[axis]
    plane_shape = lax.index_in_dim(field, 0, axis, False).shape
    lower_face = jnp.expand_dims(hlow.reshape(plane_shape), axis)
    upper_face = jnp.expand_dims(hup.reshape(plane_shape), axis)
    upper = jnp.concatenate([lax.slice_in_dim(field, 1, edge, axis=axis), upper_face], axis)
    lower = jnp.concatenate([lower_face, lax.slice_in_dim(field, 0, edge - 1, axis=axis)], axis)
    place = lax.broadcasted_iota(jnp.int32, field.shape, axis)
    inner = rate[:, :, None, None, None]
    c_up = jnp.where(place == edge - 1, gup[:, :, None, None, None], inner)
    c_down = jnp.where(place == 0, glow[:, :, None, None, None], inner)
    return c_up * (upper - field) + c_down * (lower - field)


def reaction(field, fraction):
    count, edge = (field.shape[0], field.shape[2])
    alpha = fraction.reshape(count, edge, edge, edge)
    calc, bound = (field[:, 0], field[:, 1])
    bind = KON * calc * (BTOT - bound) - KOFF * bound
    return jnp.stack([-bind + INFLUX * (1.0 - alpha) / alpha, bind], 1)


def apply_inverse(block, field, d):
    forms = ["psab,psbjk->psajk", "psab,psibk->psiak", "psab,psijb->psija"]
    return jnp.einsum(forms[d], block, field, precision=lax.Precision.HIGHEST)


def line_ends(field, d):
    count, edge = (field.shape[0], field.shape[2])
    first = lax.index_in_dim(field, 0, 2 + d, False).reshape(count, 2, edge * edge)
    last = lax.index_in_dim(field, edge - 1, 2 + d, False).reshape(count, 2, edge * edge)
    return jnp.stack([first, last], 2)


def block_terms(glow, gup, corner):
    v_first, v_last, w_first, w_last = (
        corner[..., 0],
        corner[..., 1],
        corner[..., 2],
        corner[..., 3],
    )
    a00 = 1.0 + glow * v_first
    a01 = gup * w_first
    a10 = glow * v_last
    a11 = 1.0 + gup * w_last
    lq0 = -glow * v_first
    lq1 = -glow * v_last
    up0 = -gup * w_first
    up1 = -gup * w_last
    return (a00, a01, a10, a11, lq0, lq1, up0, up1)


def chain_order(before, rank):
    slots = jnp.arange(before.shape[0], dtype=jnp.int32)
    pointer = jnp.where(before >= 0, before, slots)
    for step in range(GX.bit_length()):
        pointer = jnp.take(pointer, pointer, axis=0)
    sort_key = pointer * GX + rank
    order = jnp.argsort(sort_key)
    inverse_order = jnp.argsort(order)
    return (order, inverse_order)


def shift_down(values):
    return jnp.concatenate([jnp.zeros_like(values[:1]), values[:-1]], 0)


def shift_up(values):
    return jnp.concatenate([values[1:], jnp.zeros_like(values[:1])], 0)


def compose_maps(first_map, second_map):
    e00, e01, e10, e11 = first_map
    l00, l01, l10, l11 = second_map
    n00 = l00 * e00 + l01 * e10
    n01 = l00 * e01 + l01 * e11
    n10 = l10 * e00 + l11 * e10
    n11 = l10 * e01 + l11 * e11
    scale = jnp.abs(n00) + jnp.abs(n01) + jnp.abs(n10) + jnp.abs(n11)
    return (n00 / scale, n01 / scale, n10 / scale, n11 / scale)


def compose_affine(first_map, second_map):
    first_q, first_p = first_map
    second_q, second_p = second_map
    return (first_q * second_q, second_p + second_q * first_p)


def sorted_solve(glow, gup, corner, before, after, order, inverse_order, ends):
    glow = jnp.take(glow, order, axis=0)
    gup = jnp.take(gup, order, axis=0)
    corner = jnp.take(corner, order, axis=0)
    has_b = jnp.take(before, order, axis=0) >= 0
    has_a = jnp.take(after, order, axis=0) >= 0
    arranged = jnp.take(ends, order, axis=0)
    y0 = arranged[:, :, 0]
    y1 = arranged[:, :, 1]
    a00, a01, a10, a11, lq0, lq1, up0, up1 = block_terms(glow, gup, corner)
    maps = (
        -(lq0 * up1 - lq1 * up0),
        a00 * up1 - a10 * up0,
        -(lq0 * a11 - a01 * lq1),
        a00 * a11 - a01 * a10,
    )
    summed = lax.associative_scan(compose_maps, maps, axis=0)
    f1_prev = summed[1] / summed[3]
    fq = shift_down(f1_prev)
    b00 = a00 - lq0 * fq
    b10 = a10 - lq1 * fq
    det = b00 * a11 - a01 * b10
    f0 = (a11 * up0 - a01 * up1) / det
    f1 = (b00 * up1 - b10 * up0) / det
    slope = (-(b00 * lq1 - b10 * lq0) / det)[:, :, None]
    offset = (b00[:, :, None] * y1 - b10[:, :, None] * y0) / det[:, :, None]
    e1 = lax.associative_scan(compose_affine, (slope, offset), axis=0)[1]
    eq = shift_down(e1)
    e0 = (
        a11[:, :, None] * y0 - a01[:, :, None] * y1 - (a11 * lq0 - a01 * lq1)[:, :, None] * eq
    ) / det[:, :, None]
    zp = lax.associative_scan(compose_affine, (-f0[:, :, None], e0), reverse=True, axis=0)[1]
    pn = shift_up(zp)
    zq = e1 - f1[:, :, None] * pn
    low = jnp.where(has_b[:, None, None], zp - shift_down(zq), jnp.zeros_like(zp))
    high = jnp.where(has_a[:, None, None], zq - pn, jnp.zeros_like(zq))
    return jnp.take(jnp.stack([low, high], 2), inverse_order, axis=0)


def correct(local, block, glow, gup, jumps, d):
    axis = 2 + d
    count, edge = (local.shape[0], local.shape[2])
    shape_v = [count, 2, 1, 1, 1]
    shape_v[axis] = edge
    first_col = block[..., 0].reshape(shape_v)
    last_col = block[..., edge - 1].reshape(shape_v)
    plane_shape = lax.index_in_dim(local, 0, axis, False).shape
    low = jnp.expand_dims(jumps[:, :, 0].reshape(plane_shape), axis)
    high = jnp.expand_dims(jumps[:, :, 1].reshape(plane_shape), axis)
    return (
        local
        - glow[:, :, None, None, None] * low * first_col
        - gup[:, :, None, None, None] * high * last_col
    )


def general_body(calcium, buffer, fraction, rates, inverses, neighbors, ranks):
    count, edge = (calcium.shape[0], calcium.shape[1])
    devices = lax.axis_size("bricks")
    square = edge * edge
    per_device = square // devices
    start = lax.axis_index("bricks") * count
    corners = jnp.stack(
        [
            inverses[..., 0, 0],
            inverses[..., edge - 1, 0],
            inverses[..., 0, edge - 1],
            inverses[..., edge - 1, edge - 1],
        ],
        -1,
    )
    rate_all, corner_all = (
        lax.all_gather(rates, "bricks", axis=0, tiled=True),
        lax.all_gather(corners, "bricks", axis=0, tiled=True),
    )
    couple_all = coupling(rate_all, neighbors)
    couple = lax.dynamic_slice_in_dim(couple_all, start, count, 0)
    field = jnp.stack([calcium, buffer], 1).reshape(count, 2, edge, edge, edge)
    planes = end_planes(field).reshape(count, 3, 2, 2, devices, per_device)
    lined = lookup(
        lax.all_to_all(planes, "bricks", split_axis=4, concat_axis=0, tiled=True),
        neighbors[:, 0],
        neighbors[:, 1],
    )
    halos = lax.all_to_all(lined, "bricks", split_axis=0, concat_axis=4, tiled=True).reshape(
        count, 3, 2, 2, square
    )
    lams = [
        operator(
            field, d, rates[:, d], couple[:, d, 0], couple[:, d, 1], halos[:, d, 0], halos[:, d, 1]
        )
        for d in range(3)
    ]
    rhs = field + lams[0] + 2.0 * lams[1] + 2.0 * lams[2] + reaction(field, fraction)

    def solve(right, d):
        block = inverses[:, d]
        local = apply_inverse(block, right, d)
        ends = line_ends(local, d).reshape(count, 2, 2, devices, per_device)
        order, inverse_order = chain_order(neighbors[d, 0], ranks[d])
        chain_fn = partial(
            sorted_solve,
            couple_all[:, d, 0],
            couple_all[:, d, 1],
            corner_all[:, d],
            neighbors[d, 0],
            neighbors[d, 1],
            order,
            inverse_order,
        )
        lined_jumps = chain_fn(
            lax.all_to_all(ends, "bricks", split_axis=3, concat_axis=0, tiled=True)[:, :, :, 0]
        )[:, :, :, None]
        jumps = lax.all_to_all(
            lined_jumps, "bricks", split_axis=0, concat_axis=3, tiled=True
        ).reshape(count, 2, 2, square)
        return correct(local, block, couple[:, d, 0], couple[:, d, 1], jumps, d)

    first = solve(rhs, 0)
    second = solve(first - lams[1], 1)
    third = solve(second - lams[2], 2)
    result = third.reshape(count, 2, edge, edge * edge)
    return (result[:, 0], result[:, 1])


LANES = 128


def cosine_basis(edge):
    wave = np.arange(edge)[:, None]
    place = np.arange(edge)[None, :]
    basis = np.sqrt(2.0 / edge) * np.cos(np.pi * wave * (place + 0.5) / edge)
    basis[0] = math.sqrt(1.0 / edge)
    eigen = 2.0 - 2.0 * np.cos(np.pi * np.arange(edge) / edge)
    return basis, eigen


def parts_of(x):
    high = x.astype(jnp.bfloat16).astype(jnp.float32)
    return high, (x - high).astype(jnp.bfloat16).astype(jnp.float32)


def left_of(x):
    high, low = parts_of(x)
    return jnp.concatenate([high, low, high], 1).astype(jnp.bfloat16)


def right_of(x, axis=0):
    high = x.astype(jnp.bfloat16)
    low = (x - high.astype(jnp.float32)).astype(jnp.bfloat16)
    return jnp.concatenate([high, high, low], axis)


def right_of_swapped(x):
    high = x.astype(jnp.bfloat16)
    low = (x - high.astype(jnp.float32)).astype(jnp.bfloat16)
    return jnp.concatenate([high, low, high], 0)


def exact_of(x):
    high = x.astype(jnp.bfloat16)
    rest = x - high.astype(jnp.float32)
    middle = rest.astype(jnp.bfloat16)
    return jnp.concatenate([high, middle, (rest - middle.astype(jnp.float32)).astype(jnp.bfloat16)], 1)


def dot(a, b):
    return jnp.dot(a, b, preferred_element_type=jnp.float32)


def dot_lanes(a, b):
    return lax.dot_general(a, b, (((1,), (1,)), ((), ())), preferred_element_type=jnp.float32)


def host_left(x):
    high = x.astype(jnp.bfloat16).astype(np.float64)
    low = (x - high).astype(jnp.bfloat16).astype(np.float64)
    return np.concatenate([high, low, high], 1)


def host_right(x):
    high = x.astype(jnp.bfloat16).astype(np.float64)
    low = (x - high).astype(jnp.bfloat16).astype(np.float64)
    return np.concatenate([high, high, low], 0)


def lane_of(shape):
    return lax.broadcasted_iota(jnp.int32, shape, len(shape) - 1)


def swap_blocks(four):
    x0, x1, x2, x3 = four
    lane = lane_of(x0.shape)
    low = (lane & 64) == 0
    y0, y2 = jnp.where(low, x0, pltpu.roll(x2, 64, 1)), jnp.where(low, pltpu.roll(x0, 64, 1), x2)
    y1, y3 = jnp.where(low, x1, pltpu.roll(x3, 64, 1)), jnp.where(low, pltpu.roll(x1, 64, 1), x3)
    even = (lane & 32) == 0
    z0, z1 = jnp.where(even, y0, pltpu.roll(y1, 32, 1)), jnp.where(even, pltpu.roll(y0, 96, 1), y1)
    z2, z3 = jnp.where(even, y2, pltpu.roll(y3, 32, 1)), jnp.where(even, pltpu.roll(y2, 96, 1), y3)
    return [z0, z1, z2, z3]


def swap_rows(source, base, scratch, at, edge):
    tiles = edge // 4
    for c in range(tiles):
        rows = [source[pl.ds(base + edge * c + g, tiles, stride=4), :] for g in range(4)]
        for t4, row in enumerate(swap_blocks(rows)):
            scratch[pl.ds(at + 4 * c + t4, tiles, stride=edge), :] = row


def tile_rows(x, edge):
    tiles = edge // 4
    return jnp.concatenate([x[:, LANES * c : LANES * (c + 1)] for c in range(tiles)], 0)


def wide(ref, at, edge):
    tiles = edge // 4
    return jnp.concatenate([ref[pl.ds(at + edge * c, edge), :] for c in range(tiles)], 1)


def swap_inner(refs, edge):
    tiles = edge // 4
    fields = [(ref, b) for ref in refs for b in range(ref.shape[0])]
    whole = [
        exact_of(jnp.concatenate([ref[b, :, LANES * c : LANES * (c + 1)] for ref, b in fields], 0))
        for c in range(tiles)
    ]
    row = lax.broadcasted_iota(jnp.int32, (LANES, LANES), 0)
    lane = lane_of((LANES, LANES))
    for to in range(tiles):
        total = jnp.zeros((len(fields) * edge, LANES), jnp.float32)
        for c in range(tiles):
            hit = ((row & (edge - 1)) == 4 * to + lane // edge) & ((lane & (edge - 1)) == 4 * c + row // edge)
            hit = hit.astype(jnp.float32).astype(jnp.bfloat16)
            total = total + dot(whole[c], jnp.concatenate([hit] * 3, 0))
        for f, (ref, b) in enumerate(fields):
            ref[b, :, LANES * to : LANES * (to + 1)] = total[edge * f : edge * (f + 1)]


def normal_of(near, slot):
    along_j = (near[1, 0, slot] >= 0) | (near[1, 1, slot] >= 0)
    return jnp.where(along_j, 1, 2)


def message_kernel(
    near_in, rates_in, calcium_in, buffer_in, fraction_in, inverses_in, const_in,
    msg, solved,
    near, rates, calcium, buffer, fraction, inverses, const, work, sems,
):
    count, edge = calcium.shape[0], calcium.shape[1]
    tiles = edge // 4
    size = tiles * edge
    copies = [
        pltpu.make_async_copy(source, target, sems.at[x])
        for x, (source, target) in enumerate(
            (
                (near_in, near),
                (rates_in, rates),
                (calcium_in, calcium),
                (buffer_in, buffer),
                (fraction_in, fraction),
                (inverses_in, inverses),
                (const_in, const),
            )
        )
    ]
    for copy in copies:
        copy.start()
    first_slot = lax.axis_index("bricks") * count
    for copy in copies:
        copy.wait()
    normal = normal_of(near, first_slot)
    closed = 3 - normal

    @pl.when(normal == 1)
    def _():
        swap_inner((calcium, buffer, fraction), edge)

    lane = lane_of((edge, LANES))
    inner = lane & (edge - 1)
    square_row = lax.broadcasted_iota(jnp.int32, (LANES, LANES), 0)
    square_lane = lane_of((LANES, LANES))
    on_block = (square_row // edge) == (square_lane // edge)
    faces_u, faces_y, ends0, ends1 = [], [], [], []
    for b in range(count):
        face = jnp.where(near[normal, 1, first_slot + b] >= 0, edge - 1, 0)
        calc = [calcium[b, :, LANES * c : LANES * (c + 1)] for c in range(tiles)]
        bound = [buffer[b, :, LANES * c : LANES * (c + 1)] for c in range(tiles)]
        alpha = [fraction[b, :, LANES * c : LANES * (c + 1)] for c in range(tiles)]
        bind = [KON * x * (BTOT - y) - KOFF * y for x, y in zip(calc, bound)]
        source_calc = [-w + INFLUX * (1.0 - a) / a for w, a in zip(bind, alpha)]
        for q, (u, source) in enumerate(((calc, source_calc), (bound, bind))):
            at = size * (2 * b + q)
            rate_t, rate_n = 2.0 * rates[b, q, closed], 2.0 * rates[b, q, normal]
            ahead = [pltpu.roll(x, LANES - edge, 1) for x in u]
            behind = [pltpu.roll(x, edge, 1) for x in u]
            f = []
            for c in range(tiles):
                x = u[c]
                next_t = jnp.where(lane < LANES - edge, ahead[c], ahead[c + 1] if c + 1 < tiles else x)
                last_t = jnp.where(lane >= edge, behind[c], behind[c - 1] if c else x)
                next_n = jnp.where(inner == edge - 1, x, pltpu.roll(x, LANES - 1, 1))
                last_n = jnp.where(inner == 0, x, pltpu.roll(x, 1, 1))
                twice = x + x
                along = rate_t * (next_t + last_t - twice) + rate_n * (next_n + last_n - twice)
                f.append(twice + along + source[c])
            g = dot(left_of(inverses[b, 0, q]), right_of(jnp.concatenate(f, 1)))
            for c in range(tiles):
                work[pl.ds(edge * c, edge), :] = g[:, LANES * c : LANES * (c + 1)]
            ends0.append(work[pl.ds(0, tiles, stride=edge), :])
            ends1.append(work[pl.ds(edge - 1, tiles, stride=edge), :])
            w = jnp.concatenate([g[:, LANES * c : LANES * (c + 1)] - 2.0 * u[c] for c in range(tiles)], 0)
            block = jnp.concatenate([inverses[b, normal, q]] * 4, 1)
            block = jnp.where(on_block, jnp.concatenate([block] * 4, 0), 0.0)
            high = w.astype(jnp.bfloat16)
            low = (w - high.astype(jnp.float32)).astype(jnp.bfloat16)
            y = dot(jnp.concatenate([high, high, low], 1), right_of_swapped(block))
            solved[pl.ds(at, size), :] = y
            face_u = jnp.zeros((edge, LANES), jnp.float32)
            face_y = jnp.zeros((edge, LANES), jnp.float32)
            for c in range(tiles):
                shift = (c - face) & (LANES - 1)
                face_u = jnp.where(inner == c, pltpu.roll(u[c], shift, 1), face_u)
                face_y = jnp.where(inner == c, pltpu.roll(y[edge * c : edge * (c + 1)], shift, 1), face_y)
            faces_u.append(face_u)
            faces_y.append(face_y)

    stack0 = jnp.concatenate(swap_blocks(ends0), 0)
    stack1 = jnp.concatenate(swap_blocks(ends1), 0)
    ends_of = const[:, : 3 * edge].astype(jnp.bfloat16)
    faces_of = const[:, LANES:].astype(jnp.bfloat16)
    both = dot(ends_of, right_of(jnp.concatenate([stack0, stack1], 1)))
    part_u = dot_lanes(faces_of, right_of(jnp.concatenate(faces_u, 0), 1))
    part_y = dot_lanes(faces_of, right_of(jnp.concatenate(faces_y, 0), 1))
    fields = swap_blocks([both[:, :LANES], both[:, LANES:], part_u, part_y])
    for x, part in enumerate(fields):
        msg[pl.ds(x, edge, stride=8), :] = part
    for b in range(count):
        for q in range(2):
            row = jnp.where(
                lane == 0,
                rates[b, q, 0],
                jnp.where(lane == 1, rates[b, q, closed], jnp.where(lane == 2, rates[b, q, normal], 0.0)),
            )
            msg[pl.ds(4 + 2 * b + q, edge, stride=8), :] = row


def local_kernel(
    near_in, solved_in, inverses_in,
    base, pick, flags, edges,
    near, table, solved, inverses, work, other, sems,
):
    count, edge = inverses.shape[0], inverses.shape[3]
    tiles = edge // 4
    size = tiles * edge
    slots = near.shape[2]
    copies = [
        pltpu.make_async_copy(source, target, sems.at[x])
        for x, (source, target) in enumerate(
            (
                (near_in, near),
                (near_in, table),
                (solved_in, solved),
                (inverses_in, inverses),
            )
        )
    ]
    for copy in copies:
        copy.start()
    for copy in copies[:2]:
        copy.wait()
    normal = normal_of(near, 0)
    closed = 3 - normal
    up = near[normal, 1, 0] >= 0
    touch = up | (near[normal, 0, 0] >= 0)

    lane = lane_of((8, LANES))
    back = jnp.broadcast_to(table[0, 0:1, :], (8, slots))
    back = jnp.concatenate([back] * (LANES // slots), 1)
    pointer = jnp.where(back >= 0, back, lane & (slots - 1))
    place = jnp.where(back >= 0, 1, 0)

    def pull(values, index):
        return jnp.take_along_axis(values, index, axis=1, mode="promise_in_bounds")

    reach = 1
    while reach < edge:
        place = place + pull(place, pointer)
        pointer = pull(pointer, pointer)
        reach *= 2
    chain = jnp.where(pointer == pointer[:, 0:1], 0, edge) + place
    goal = pull(chain, (lane & (edge - 1)) * count + lane // (2 * edge)) + 2 * (lane & edge)
    hit = lax.broadcasted_iota(jnp.int32, (LANES, LANES), 0) == goal[0:1]
    pick[...] = hit.astype(jnp.float32).T
    face = jnp.where(((lane & edge) == 0) == up, edge - 1, 0).astype(jnp.float32)
    depth = lax.broadcasted_iota(jnp.int32, (8, LANES), 0)
    angle = jnp.full((8, LANES), lax.axis_index("bricks")).astype(jnp.float32) * (0.5 * math.pi / edge)
    half = jnp.sin(angle)
    flags[...] = jnp.where(
        depth == 0,
        face,
        jnp.where(
            depth == 1,
            jnp.where(touch, 1.0, 0.0),
            jnp.where(depth == 2, jnp.where(normal == 2, 1.0, 0.0), 4.0 * half * half),
        ),
    )

    for copy in copies[2:]:
        copy.wait()
    first_slot = lax.axis_index("bricks") * count
    for b in range(count):
        face = jnp.where(near[normal, 1, first_slot + b] >= 0, edge - 1, 0)
        for q in range(2):
            x = 2 * b + q
            at = size * x
            swap_rows(solved, at, other, 0, edge)
            whole = dot(left_of(inverses[b, closed, q]), right_of(wide(other, 0, edge)))
            for c in range(tiles):
                other[pl.ds(edge * c, edge), :] = whole[:, LANES * c : LANES * (c + 1)]
            swap_rows(other, 0, work, 0, edge)
            base[pl.ds(at, size), :] = work[...]
            row_n = jnp.concatenate([inverses[b, normal, q, pl.ds(face, 1), :]] * 4, 1)
            edges[x, 0] = jnp.broadcast_to(inverses[b, 0, q, :, 0:1], (edge, LANES))
            edges[x, 1] = jnp.broadcast_to(inverses[b, 0, q, :, edge - 1 : edge], (edge, LANES))
            edges[x, 2] = jnp.broadcast_to(row_n, (edge, LANES))


def owner_kernel(recv, pick, flags, const, out):
    edge = const.shape[0]
    basis = const[:, 0 : 3 * edge].astype(jnp.bfloat16)
    turned = const[:, LANES : LANES + 3 * edge].astype(jnp.bfloat16)
    lam = const[:, 2 * LANES : 3 * LANES]
    v_first = const[:, 3 * LANES : 4 * LANES]
    v_last = const[:, 4 * LANES : 5 * LANES]
    face, touch, normal_2, my_lam = flags[0:1], flags[1:2], flags[2:3], flags[3:4]

    hit = pick[...].astype(jnp.bfloat16)
    data = jnp.concatenate([recv[pl.ds(x, edge, stride=8), :] for x in range(4)], 0).T
    tail = jnp.concatenate([recv[pl.ds(4 + x, edge, stride=8), :] for x in range(4)], 0).T[:16]
    parts = dot(exact_of(jnp.concatenate([tail, data], 0)), jnp.concatenate([hit] * 3, 0))
    rate_0, rate_t, rate_n = parts[0:1], parts[1:2], parts[2:3]
    y0, y1, face_u, face_y = (parts[16 + edge * x : 16 + edge * (x + 1)] for x in range(4))

    lane = lane_of((1, LANES))
    place = lane & (edge - 1)
    first_row = (lane & edge) == 0

    def partner(x):
        return jnp.where(first_row, pltpu.roll(x, LANES - edge, 1), pltpu.roll(x, edge, 1))

    def after(x, s=1):
        return pltpu.roll(x, LANES - s, 1)

    def before(x, s=1):
        return pltpu.roll(x, s, 1)

    damp_0 = 1.0 / (1.0 + lam * rate_0)
    damp_n = 1.0 / (1.0 + lam * rate_n)
    damp_t = 1.0 / (1.0 + my_lam * rate_t)
    other_n = partner(rate_n)
    g = jnp.where(touch > 0.5, 2.0 * rate_n * other_n / (rate_n + other_n), 0.0)
    cross = 2.0 * g * (partner(face_u) - face_u)
    near_c = jnp.sum(damp_0 * v_first * v_first, 0, keepdims=True)
    far_c = jnp.sum(damp_0 * v_first * v_last, 0, keepdims=True)
    end_n = jnp.sum(damp_n * v_first * v_first, 0, keepdims=True)
    pieces = dot(
        turned,
        right_of(
            jnp.concatenate(
                [
                    damp_0 * dot(basis, right_of(cross)),
                    damp_0 * v_first,
                    damp_0 * v_last,
                    damp_n * jnp.where(face < 0.5, v_first, v_last),
                ],
                1,
            )
        ),
    )
    spread, col_0, col_1, col_n = (pieces[:, LANES * x : LANES * (x + 1)] for x in range(4))
    depth = lax.broadcasted_iota(jnp.int32, (edge, LANES), 0).astype(jnp.float32)
    at_face = depth == face
    y0 = y0 + jnp.where(at_face, spread[0:1], 0.0)
    y1 = y1 + jnp.where(at_face, spread[edge - 1 : edge], 0.0)

    inv_rate = 1.0 / rate_0
    open_face = place < edge - 1
    diag = jnp.where(open_face, 0.5 * (inv_rate + after(inv_rate)) + near_c + after(near_c), 1.0)
    lower = jnp.where(open_face & (place > 0), -far_c, 0.0)
    upper = jnp.where(place < edge - 2, -after(far_c), 0.0)
    right = jnp.where(open_face, y1 - after(y0), 0.0)
    step = 1
    while step < edge:
        inverse = 1.0 / diag
        back = -lower * before(inverse, step)
        fore = -upper * after(inverse, step)
        diag = diag + back * before(upper, step) + fore * after(lower, step)
        right = right + back * before(right, step) + fore * after(right, step)
        lower = back * before(lower, step)
        upper = fore * after(upper, step)
        step *= 2
    flux_up = right / diag
    flux_down = jnp.where(place > 0, before(flux_up), 0.0)

    weight_down = jnp.sum(col_n * flux_down, 0, keepdims=True)
    weight_up = jnp.sum(col_n * flux_up, 0, keepdims=True)
    ends = face_y + end_n * spread + col_0 * weight_down - col_1 * weight_up
    ends = jnp.where(normal_2 > 0.5, damp_t, 1.0) * ends
    jump = g / (1.0 + g * (end_n + partner(end_n))) * (ends - partner(ends))
    face_out = jnp.where(normal_2 > 0.5, damp_t * spread - jump, damp_t * (spread - jump))
    lines = dot(basis, right_of(jnp.concatenate([flux_down, flux_up], 1)))
    lines = dot(turned, right_of(jnp.concatenate([damp_n * damp_t] * 2, 1) * lines))
    packed = jnp.concatenate(
        [lines[:, :LANES], lines[:, LANES:], face_out, jnp.zeros((edge, LANES), jnp.float32)], 0
    )
    reply = dot_lanes(jnp.concatenate([hit] * 3, 1), exact_of(packed))
    for x in range(4):
        out[pl.ds(x, edge, stride=4), :] = reply[edge * x : edge * (x + 1)]


def update_kernel(
    recv, base, edges, flags, calcium, buffer, const,
    calcium_out, buffer_out,
    calcium_next, buffer_next, work, sems,
):
    count, edge = calcium.shape[0], calcium.shape[1]
    tiles = edge // 4
    size = tiles * edge
    swapped = flags[2, 0] < 0.5
    old = jnp.where(flags[2:3] < 0.5, 0.0, 1.0)
    fields = [recv[pl.ds(x, edge, stride=2 * count), :] for x in range(2 * count)]
    low, high, face_part, _ = swap_blocks(fields)
    high_s, low_s = parts_of(face_part)
    turn = jnp.concatenate([high_s, low_s, high_s, jnp.zeros_like(high_s)], 0).T.astype(jnp.bfloat16)
    face_wide = dot(turn, const[:, LANES:].astype(jnp.bfloat16))
    lines = dot(const[:edge, : 3 * edge].astype(jnp.bfloat16), right_of(jnp.concatenate([low, high], 1)))
    rows = []
    for e in range(2):
        work[pl.ds(edge * e, edge), :] = lines[:, LANES * e : LANES * (e + 1)]
        rows.append(swap_blocks([work[pl.ds(edge * e + t4, tiles, stride=4), :] for t4 in range(4)]))

    stores = [
        pltpu.make_async_copy(source.at[b], to.at[b], sems.at[2 * b + q])
        for b in range(count)
        for q, (source, to) in enumerate(((calcium_next, calcium_out), (buffer_next, buffer_out)))
    ]
    for b in range(count):
        for q, (ref, now) in enumerate(((calcium_next, calcium), (buffer_next, buffer))):
            x = 2 * b + q
            at = size * x
            col_0, col_1, row_n = edges[x, 0], edges[x, 1], edges[x, 2]
            for c in range(tiles):
                part = slice(LANES * c, LANES * (c + 1))
                ref[b, :, part] = (
                    (base[pl.ds(at + edge * c, edge), :] + old * now[b, :, part])
                    + face_wide[edge * x : edge * (x + 1), part] * row_n
                    + (col_0 * rows[0][x][c : c + 1] - col_1 * rows[1][x][c : c + 1])
                )
            stores[x].start()
    for store in stores:
        store.wait()

    @pl.when(swapped)
    def _():
        swap_inner((calcium_next, buffer_next), edge)
        calcium_next[...] = calcium_next[...] + calcium[...]
        buffer_next[...] = buffer_next[...] + buffer[...]
        for store in stores:
            store.start()
        for store in stores:
            store.wait()


def fast_body(calcium, buffer, fraction, rates, inverses, neighbors, ranks):
    count, edge = calcium.shape[0], calcium.shape[1]
    devices = lax.axis_size("bricks")
    tiles = edge // 4
    size = tiles * edge
    f32 = jnp.float32
    basis, eigen = cosine_basis(edge)
    place = np.arange(edge)
    ends_of = np.zeros((edge, edge))
    ends_of[:, (place % 4) * tiles + place // 4] = basis
    faces_of = np.zeros((edge, LANES))
    faces_of[:, (place % 4) * edge + place // 4] = basis
    pad = lambda x: np.pad(x, ((0, 0), (0, LANES - x.shape[1])))
    message_const = np.concatenate([pad(host_left(ends_of)), host_left(faces_of)], 1)
    lanes_of = lambda x: np.tile(x[:, None], (1, LANES))
    owner_const = np.concatenate(
        [pad(host_left(basis)), pad(host_left(basis.T))]
        + [lanes_of(x) for x in (eigen, basis[:, 0], basis[:, -1])],
        1,
    )
    expand = np.pad(host_right(np.repeat(basis, edge, 1)), ((0, LANES - 3 * edge), (0, 0)))
    back_const = np.pad(pad(host_left(basis.T)), ((0, LANES - edge), (0, 0)))
    update_const = np.concatenate([back_const, expand], 1)
    smem = pl.BlockSpec(memory_space=pltpu.SMEM)
    vmem = pl.BlockSpec(memory_space=pltpu.VMEM)
    hbm = pl.BlockSpec(memory_space=pltpu.HBM)
    params = pltpu.CompilerParams(vmem_limit_bytes=48 * 2**20)
    const = lambda x: jnp.asarray(x, f32)
    field = jax.ShapeDtypeStruct(calcium.shape, f32)
    tall = jax.ShapeDtypeStruct((2 * count * size, LANES), f32)

    stay = lambda x: pltpu.with_memory_space_constraint(x, pltpu.HBM)
    msg, solved = pl.pallas_call(
        message_kernel,
        out_shape=(jax.ShapeDtypeStruct((devices * 8, LANES), f32), tall),
        in_specs=[hbm] * 7,
        out_specs=(vmem, vmem),
        scratch_shapes=[
            pltpu.SMEM(neighbors.shape, jnp.int32),
            pltpu.SMEM((count, 2, 3), f32),
            pltpu.VMEM(calcium.shape, f32),
            pltpu.VMEM(calcium.shape, f32),
            pltpu.VMEM(fraction.shape, f32),
            pltpu.VMEM(inverses.shape, f32),
            pltpu.VMEM(message_const.shape, f32),
            pltpu.VMEM((size, LANES), f32),
            pltpu.SemaphoreType.DMA((7,)),
        ],
        compiler_params=pltpu.CompilerParams(vmem_limit_bytes=48 * 2**20),
        name="message",
    )(*(stay(x) for x in (neighbors, rates.transpose(0, 2, 1), calcium, buffer, fraction, inverses, const(message_const))))
    recv = lax.all_to_all(msg.reshape(devices, 8, LANES), "bricks", 0, 0, tiled=True)
    base, pick, flags, edges = pl.pallas_call(
        local_kernel,
        out_shape=(
            tall,
            jax.ShapeDtypeStruct((LANES, LANES), f32),
            jax.ShapeDtypeStruct((8, LANES), f32),
            jax.ShapeDtypeStruct((2 * count, 3, edge, LANES), f32),
        ),
        in_specs=[hbm] * 3,
        out_specs=(vmem,) * 4,
        scratch_shapes=[
            pltpu.SMEM(neighbors.shape, jnp.int32),
            pltpu.VMEM(neighbors.shape, jnp.int32),
            pltpu.VMEM(tall.shape, f32),
            pltpu.VMEM(inverses.shape, f32),
            pltpu.VMEM((size, LANES), f32),
            pltpu.VMEM((size, LANES), f32),
            pltpu.SemaphoreType.DMA((4,)),
        ],
        compiler_params=pltpu.CompilerParams(vmem_limit_bytes=48 * 2**20),
        cost_estimate=pl.CostEstimate(flops=2 * 10**7, bytes_accessed=4 * 10**6, transcendentals=0),
        name="local_solution",
    )(neighbors, solved, inverses)
    reply = pl.pallas_call(
        owner_kernel,
        out_shape=jax.ShapeDtypeStruct((devices * 2 * count, LANES), f32),
        in_specs=[vmem] * 4,
        out_specs=vmem,
        compiler_params=params,
        name="chain_and_face_solves",
    )(recv.reshape(devices * 8, LANES), pick, flags, const(owner_const))
    back = lax.all_to_all(reply.reshape(devices, 2 * count, LANES), "bricks", 0, 0, tiled=True)
    return pl.pallas_call(
        update_kernel,
        out_shape=(field, field),
        in_specs=[vmem] * 7,
        out_specs=(hbm, hbm),
        scratch_shapes=[
            pltpu.VMEM(calcium.shape, f32),
            pltpu.VMEM(buffer.shape, f32),
            pltpu.VMEM((2 * edge, LANES), f32),
            pltpu.SemaphoreType.DMA((2 * count,)),
        ],
        compiler_params=params,
        name="rank_three_update",
    )(back.reshape(devices * 2 * count, LANES), base, edges, flags, calcium, buffer, const(update_const))


def body(calcium, buffer, fraction, rates, inverses, neighbors, ranks):
    count, edge = calcium.shape[0], calcium.shape[1]
    devices = lax.axis_size("bricks")
    if edge == GX and devices == edge and count == 2 and 4 * edge == LANES:
        return fast_body(calcium, buffer, fraction, rates, inverses, neighbors, ranks)
    return general_body(calcium, buffer, fraction, rates, inverses, neighbors, ranks)


def solution(mesh):
    in_specs = (
        P("bricks", None, None),
        P("bricks", None, None),
        P("bricks", None, None),
        P("bricks", None, None),
        P("bricks", None, None, None, None),
        P(),
        P(),
    )
    out_specs = (P("bricks", None, None), P("bricks", None, None))
    return jax.shard_map(body, mesh=mesh, in_specs=in_specs, out_specs=out_specs, check_vma=False)
```

```python
from functools import partial
import math

import jax
import jax.numpy as jnp
import numpy as np
from jax import lax
from jax.experimental import pallas as pl
from jax.experimental.pallas import tpu as pltpu
from jax.sharding import PartitionSpec as P

GX = 32


KON = 0.5
KOFF = 0.3
BTOT = 2.0
INFLUX = 0.1


def fetch(table, index):
    rows = jnp.take(table, jnp.maximum(index, 0), axis=0)
    has = (index >= 0).reshape((-1,) + (1,) * (rows.ndim - 1))
    return jnp.where(has, rows, jnp.zeros_like(rows))


def lookup(planes, before, after):
    sides = []
    for d in range(3):
        lower = fetch(planes[:, d, 1], before[d])
        upper = fetch(planes[:, d, 0], after[d])
        sides.append(jnp.stack([lower, upper], 1))
    return jnp.stack(sides, 1)


def coupling(rate_all, neighbors):
    per_dim = []
    for d in range(3):
        mine = rate_all[:, d]
        sides = []
        for side in range(2):
            other = fetch(mine, neighbors[d, side])
            has = (neighbors[d, side] >= 0)[:, None]
            sides.append(jnp.where(has, 2.0 * mine * other / (mine + other), jnp.zeros_like(mine)))
        per_dim.append(jnp.stack(sides, 1))
    return jnp.stack(per_dim, 1)


def end_planes(field):
    count, edge = (field.shape[0], field.shape[2])
    per_dim = []
    for d in range(3):
        first = lax.index_in_dim(field, 0, 2 + d, False).reshape(count, 2, edge * edge)
        last = lax.index_in_dim(field, edge - 1, 2 + d, False).reshape(count, 2, edge * edge)
        per_dim.append(jnp.stack([first, last], 1))
    return jnp.stack(per_dim, 1)


def operator(field, d, rate, glow, gup, hlow, hup):
    axis = 2 + d
    edge = field.shape[axis]
    plane_shape = lax.index_in_dim(field, 0, axis, False).shape
    lower_face = jnp.expand_dims(hlow.reshape(plane_shape), axis)
    upper_face = jnp.expand_dims(hup.reshape(plane_shape), axis)
    upper = jnp.concatenate([lax.slice_in_dim(field, 1, edge, axis=axis), upper_face], axis)
    lower = jnp.concatenate([lower_face, lax.slice_in_dim(field, 0, edge - 1, axis=axis)], axis)
    place = lax.broadcasted_iota(jnp.int32, field.shape, axis)
    inner = rate[:, :, None, None, None]
    c_up = jnp.where(place == edge - 1, gup[:, :, None, None, None], inner)
    c_down = jnp.where(place == 0, glow[:, :, None, None, None], inner)
    return c_up * (upper - field) + c_down * (lower - field)


def reaction(field, fraction):
    count, edge = (field.shape[0], field.shape[2])
    alpha = fraction.reshape(count, edge, edge, edge)
    calc, bound = (field[:, 0], field[:, 1])
    bind = KON * calc * (BTOT - bound) - KOFF * bound
    return jnp.stack([-bind + INFLUX * (1.0 - alpha) / alpha, bind], 1)


def apply_inverse(block, field, d):
    forms = ["psab,psbjk->psajk", "psab,psibk->psiak", "psab,psijb->psija"]
    return jnp.einsum(forms[d], block, field, precision=lax.Precision.HIGHEST)


def line_ends(field, d):
    count, edge = (field.shape[0], field.shape[2])
    first = lax.index_in_dim(field, 0, 2 + d, False).reshape(count, 2, edge * edge)
    last = lax.index_in_dim(field, edge - 1, 2 + d, False).reshape(count, 2, edge * edge)
    return jnp.stack([first, last], 2)


def block_terms(glow, gup, corner):
    v_first, v_last, w_first, w_last = (
        corner[..., 0],
        corner[..., 1],
        corner[..., 2],
        corner[..., 3],
    )
    a00 = 1.0 + glow * v_first
    a01 = gup * w_first
    a10 = glow * v_last
    a11 = 1.0 + gup * w_last
    lq0 = -glow * v_first
    lq1 = -glow * v_last
    up0 = -gup * w_first
    up1 = -gup * w_last
    return (a00, a01, a10, a11, lq0, lq1, up0, up1)


def chain_order(before, rank):
    slots = jnp.arange(before.shape[0], dtype=jnp.int32)
    pointer = jnp.where(before >= 0, before, slots)
    for step in range(GX.bit_length()):
        pointer = jnp.take(pointer, pointer, axis=0)
    sort_key = pointer * GX + rank
    order = jnp.argsort(sort_key)
    inverse_order = jnp.argsort(order)
    return (order, inverse_order)


def shift_down(values):
    return jnp.concatenate([jnp.zeros_like(values[:1]), values[:-1]], 0)


def shift_up(values):
    return jnp.concatenate([values[1:], jnp.zeros_like(values[:1])], 0)


def compose_maps(first_map, second_map):
    e00, e01, e10, e11 = first_map
    l00, l01, l10, l11 = second_map
    n00 = l00 * e00 + l01 * e10
    n01 = l00 * e01 + l01 * e11
    n10 = l10 * e00 + l11 * e10
    n11 = l10 * e01 + l11 * e11
    scale = jnp.abs(n00) + jnp.abs(n01) + jnp.abs(n10) + jnp.abs(n11)
    return (n00 / scale, n01 / scale, n10 / scale, n11 / scale)


def compose_affine(first_map, second_map):
    first_q, first_p = first_map
    second_q, second_p = second_map
    return (first_q * second_q, second_p + second_q * first_p)


def sorted_solve(glow, gup, corner, before, after, order, inverse_order, ends):
    glow = jnp.take(glow, order, axis=0)
    gup = jnp.take(gup, order, axis=0)
    corner = jnp.take(corner, order, axis=0)
    has_b = jnp.take(before, order, axis=0) >= 0
    has_a = jnp.take(after, order, axis=0) >= 0
    arranged = jnp.take(ends, order, axis=0)
    y0 = arranged[:, :, 0]
    y1 = arranged[:, :, 1]
    a00, a01, a10, a11, lq0, lq1, up0, up1 = block_terms(glow, gup, corner)
    maps = (
        -(lq0 * up1 - lq1 * up0),
        a00 * up1 - a10 * up0,
        -(lq0 * a11 - a01 * lq1),
        a00 * a11 - a01 * a10,
    )
    summed = lax.associative_scan(compose_maps, maps, axis=0)
    f1_prev = summed[1] / summed[3]
    fq = shift_down(f1_prev)
    b00 = a00 - lq0 * fq
    b10 = a10 - lq1 * fq
    det = b00 * a11 - a01 * b10
    f0 = (a11 * up0 - a01 * up1) / det
    f1 = (b00 * up1 - b10 * up0) / det
    slope = (-(b00 * lq1 - b10 * lq0) / det)[:, :, None]
    offset = (b00[:, :, None] * y1 - b10[:, :, None] * y0) / det[:, :, None]
    e1 = lax.associative_scan(compose_affine, (slope, offset), axis=0)[1]
    eq = shift_down(e1)
    e0 = (
        a11[:, :, None] * y0 - a01[:, :, None] * y1 - (a11 * lq0 - a01 * lq1)[:, :, None] * eq
    ) / det[:, :, None]
    zp = lax.associative_scan(compose_affine, (-f0[:, :, None], e0), reverse=True, axis=0)[1]
    pn = shift_up(zp)
    zq = e1 - f1[:, :, None] * pn
    low = jnp.where(has_b[:, None, None], zp - shift_down(zq), jnp.zeros_like(zp))
    high = jnp.where(has_a[:, None, None], zq - pn, jnp.zeros_like(zq))
    return jnp.take(jnp.stack([low, high], 2), inverse_order, axis=0)


def correct(local, block, glow, gup, jumps, d):
    axis = 2 + d
    count, edge = (local.shape[0], local.shape[2])
    shape_v = [count, 2, 1, 1, 1]
    shape_v[axis] = edge
    first_col = block[..., 0].reshape(shape_v)
    last_col = block[..., edge - 1].reshape(shape_v)
    plane_shape = lax.index_in_dim(local, 0, axis, False).shape
    low = jnp.expand_dims(jumps[:, :, 0].reshape(plane_shape), axis)
    high = jnp.expand_dims(jumps[:, :, 1].reshape(plane_shape), axis)
    return (
        local
        - glow[:, :, None, None, None] * low * first_col
        - gup[:, :, None, None, None] * high * last_col
    )


def general_body(calcium, buffer, fraction, rates, inverses, neighbors, ranks):
    count, edge = (calcium.shape[0], calcium.shape[1])
    devices = lax.axis_size("bricks")
    square = edge * edge
    per_device = square // devices
    start = lax.axis_index("bricks") * count
    corners = jnp.stack(
        [
            inverses[..., 0, 0],
            inverses[..., edge - 1, 0],
            inverses[..., 0, edge - 1],
            inverses[..., edge - 1, edge - 1],
        ],
        -1,
    )
    rate_all, corner_all = (
        lax.all_gather(rates, "bricks", axis=0, tiled=True),
        lax.all_gather(corners, "bricks", axis=0, tiled=True),
    )
    couple_all = coupling(rate_all, neighbors)
    couple = lax.dynamic_slice_in_dim(couple_all, start, count, 0)
    field = jnp.stack([calcium, buffer], 1).reshape(count, 2, edge, edge, edge)
    planes = end_planes(field).reshape(count, 3, 2, 2, devices, per_device)
    lined = lookup(
        lax.all_to_all(planes, "bricks", split_axis=4, concat_axis=0, tiled=True),
        neighbors[:, 0],
        neighbors[:, 1],
    )
    halos = lax.all_to_all(lined, "bricks", split_axis=0, concat_axis=4, tiled=True).reshape(
        count, 3, 2, 2, square
    )
    lams = [
        operator(
            field, d, rates[:, d], couple[:, d, 0], couple[:, d, 1], halos[:, d, 0], halos[:, d, 1]
        )
        for d in range(3)
    ]
    rhs = field + lams[0] + 2.0 * lams[1] + 2.0 * lams[2] + reaction(field, fraction)

    def solve(right, d):
        block = inverses[:, d]
        local = apply_inverse(block, right, d)
        ends = line_ends(local, d).reshape(count, 2, 2, devices, per_device)
        order, inverse_order = chain_order(neighbors[d, 0], ranks[d])
        chain_fn = partial(
            sorted_solve,
            couple_all[:, d, 0],
            couple_all[:, d, 1],
            corner_all[:, d],
            neighbors[d, 0],
            neighbors[d, 1],
            order,
            inverse_order,
        )
        lined_jumps = chain_fn(
            lax.all_to_all(ends, "bricks", split_axis=3, concat_axis=0, tiled=True)[:, :, :, 0]
        )[:, :, :, None]
        jumps = lax.all_to_all(
            lined_jumps, "bricks", split_axis=0, concat_axis=3, tiled=True
        ).reshape(count, 2, 2, square)
        return correct(local, block, couple[:, d, 0], couple[:, d, 1], jumps, d)

    first = solve(rhs, 0)
    second = solve(first - lams[1], 1)
    third = solve(second - lams[2], 2)
    result = third.reshape(count, 2, edge, edge * edge)
    return (result[:, 0], result[:, 1])


LANES = 128


ROWS = 5


def cosine_basis(edge):
    wave = np.arange(edge)[:, None]
    place = np.arange(edge)[None, :]
    basis = np.sqrt(2.0 / edge) * np.cos(np.pi * wave * (place + 0.5) / edge)
    basis[0] = math.sqrt(1.0 / edge)
    eigen = 2.0 - 2.0 * np.cos(np.pi * np.arange(edge) / edge)
    return basis, eigen


def parts_of(x):
    high = x.astype(jnp.bfloat16).astype(jnp.float32)
    return high, (x - high).astype(jnp.bfloat16).astype(jnp.float32)


def left_of(x):
    high, low = parts_of(x)
    return jnp.concatenate([high, low, high], 1).astype(jnp.bfloat16)


def right_of(x, axis=0):
    high = x.astype(jnp.bfloat16)
    low = (x - high.astype(jnp.float32)).astype(jnp.bfloat16)
    return jnp.concatenate([high, high, low], axis)


def right_of_swapped(x):
    high = x.astype(jnp.bfloat16)
    low = (x - high.astype(jnp.float32)).astype(jnp.bfloat16)
    return jnp.concatenate([high, low, high], 0)


def exact_of(x):
    high = x.astype(jnp.bfloat16)
    rest = x - high.astype(jnp.float32)
    middle = rest.astype(jnp.bfloat16)
    return jnp.concatenate([high, middle, (rest - middle.astype(jnp.float32)).astype(jnp.bfloat16)], 1)


def dot(a, b):
    return jnp.dot(a, b, preferred_element_type=jnp.float32)


def dot_lanes(a, b):
    return lax.dot_general(a, b, (((1,), (1,)), ((), ())), preferred_element_type=jnp.float32)


def host_left(x):
    high = x.astype(jnp.bfloat16).astype(np.float64)
    low = (x - high).astype(jnp.bfloat16).astype(np.float64)
    return np.concatenate([high, low, high], 1)


def host_right(x):
    high = x.astype(jnp.bfloat16).astype(np.float64)
    low = (x - high).astype(jnp.bfloat16).astype(np.float64)
    return np.concatenate([high, high, low], 0)


def lane_of(shape):
    return lax.broadcasted_iota(jnp.int32, shape, len(shape) - 1)


def swap_blocks(four):
    x0, x1, x2, x3 = four
    lane = lane_of(x0.shape)
    low = (lane & 64) == 0
    y0, y2 = jnp.where(low, x0, pltpu.roll(x2, 64, 1)), jnp.where(low, pltpu.roll(x0, 64, 1), x2)
    y1, y3 = jnp.where(low, x1, pltpu.roll(x3, 64, 1)), jnp.where(low, pltpu.roll(x1, 64, 1), x3)
    even = (lane & 32) == 0
    z0, z1 = jnp.where(even, y0, pltpu.roll(y1, 32, 1)), jnp.where(even, pltpu.roll(y0, 96, 1), y1)
    z2, z3 = jnp.where(even, y2, pltpu.roll(y3, 32, 1)), jnp.where(even, pltpu.roll(y2, 96, 1), y3)
    return [z0, z1, z2, z3]


def swap_rows(source, base, scratch, at, edge):
    tiles = edge // 4
    for c in range(tiles):
        rows = [source[pl.ds(base + edge * c + g, tiles, stride=4), :] for g in range(4)]
        for t4, row in enumerate(swap_blocks(rows)):
            scratch[pl.ds(at + 4 * c + t4, tiles, stride=edge), :] = row


def tile_rows(x, edge):
    tiles = edge // 4
    return jnp.concatenate([x[:, LANES * c : LANES * (c + 1)] for c in range(tiles)], 0)


def wide(ref, at, edge):
    tiles = edge // 4
    return jnp.concatenate([ref[pl.ds(at + edge * c, edge), :] for c in range(tiles)], 1)


def swap_inner(refs, edge):
    tiles = edge // 4
    fields = [(ref, b) for ref in refs for b in range(ref.shape[0])]
    whole = [
        exact_of(jnp.concatenate([ref[b, :, LANES * c : LANES * (c + 1)] for ref, b in fields], 0))
        for c in range(tiles)
    ]
    row = lax.broadcasted_iota(jnp.int32, (LANES, LANES), 0)
    lane = lane_of((LANES, LANES))
    for to in range(tiles):
        total = jnp.zeros((len(fields) * edge, LANES), jnp.float32)
        for c in range(tiles):
            hit = ((row & (edge - 1)) == 4 * to + lane // edge) & ((lane & (edge - 1)) == 4 * c + row // edge)
            hit = hit.astype(jnp.float32).astype(jnp.bfloat16)
            total = total + dot(whole[c], jnp.concatenate([hit] * 3, 0))
        for f, (ref, b) in enumerate(fields):
            ref[b, :, LANES * to : LANES * (to + 1)] = total[edge * f : edge * (f + 1)]


def normal_of(near, slot):
    along_j = (near[1, 0, slot] >= 0) | (near[1, 1, slot] >= 0)
    return jnp.where(along_j, 1, 2)


def message_kernel(
    near_in, rates_in, calcium_in, buffer_in, fraction_in, inverses_in, const_in,
    msg, solved,
    near, rates, calcium, buffer, fraction, inverses, const, sems,
):
    count, edge = calcium.shape[0], calcium.shape[1]
    tiles = edge // 4
    size = tiles * edge
    copies = [
        pltpu.make_async_copy(source, target, sems.at[x])
        for x, (source, target) in enumerate(
            (
                (near_in, near),
                (rates_in, rates),
                (calcium_in, calcium),
                (buffer_in, buffer),
                (fraction_in, fraction),
                (inverses_in, inverses),
                (const_in, const),
            )
        )
    ]
    for copy in copies:
        copy.start()
    first_slot = lax.axis_index("bricks") * count
    for copy in copies:
        copy.wait()
    normal = normal_of(near, first_slot)
    closed = 3 - normal

    @pl.when(normal == 1)
    def _():
        swap_inner((calcium, buffer, fraction), edge)

    lane = lane_of((edge, LANES))
    inner = lane & (edge - 1)
    square_row = lax.broadcasted_iota(jnp.int32, (LANES, LANES), 0)
    square_lane = lane_of((LANES, LANES))
    on_block = (square_row // edge) == (square_lane // edge)
    faces_u, faces_y, ends0, ends1 = [], [], [], []
    for b in range(count):
        face = jnp.where(near[normal, 1, first_slot + b] >= 0, edge - 1, 0)
        calc = [calcium[b, :, LANES * c : LANES * (c + 1)] for c in range(tiles)]
        bound = [buffer[b, :, LANES * c : LANES * (c + 1)] for c in range(tiles)]
        alpha = [fraction[b, :, LANES * c : LANES * (c + 1)] for c in range(tiles)]
        bind = [KON * x * (BTOT - y) - KOFF * y for x, y in zip(calc, bound)]
        source_calc = [-w + INFLUX * (1.0 - a) / a for w, a in zip(bind, alpha)]
        for q, (u, source) in enumerate(((calc, source_calc), (bound, bind))):
            at = size * (2 * b + q)
            rate_t, rate_n = 2.0 * rates[b, q, closed], 2.0 * rates[b, q, normal]
            ahead = [pltpu.roll(x, LANES - edge, 1) for x in u]
            behind = [pltpu.roll(x, edge, 1) for x in u]
            f = []
            for c in range(tiles):
                x = u[c]
                next_t = jnp.where(lane < LANES - edge, ahead[c], ahead[c + 1] if c + 1 < tiles else x)
                last_t = jnp.where(lane >= edge, behind[c], behind[c - 1] if c else x)
                next_n = jnp.where(inner == edge - 1, x, pltpu.roll(x, LANES - 1, 1))
                last_n = jnp.where(inner == 0, x, pltpu.roll(x, 1, 1))
                twice = x + x
                along = rate_t * (next_t + last_t - twice) + rate_n * (next_n + last_n - twice)
                f.append(twice + along + source[c])
            g = dot(left_of(inverses[b, 0, q]), right_of(jnp.concatenate(f, 1)))
            ends0.append(jnp.concatenate([g[0:1, LANES * c : LANES * (c + 1)] for c in range(tiles)], 0))
            ends1.append(jnp.concatenate([g[edge - 1 : edge, LANES * c : LANES * (c + 1)] for c in range(tiles)], 0))
            w = jnp.concatenate([g[:, LANES * c : LANES * (c + 1)] - 2.0 * u[c] for c in range(tiles)], 0)
            block = jnp.concatenate([inverses[b, normal, q]] * 4, 1)
            block = jnp.where(on_block, jnp.concatenate([block] * 4, 0), 0.0)
            high = w.astype(jnp.bfloat16)
            low = (w - high.astype(jnp.float32)).astype(jnp.bfloat16)
            y = dot(jnp.concatenate([high, high, low], 1), right_of_swapped(block))
            solved[pl.ds(at, size), :] = y
            face_u = jnp.zeros((edge, LANES), jnp.float32)
            face_y = jnp.zeros((edge, LANES), jnp.float32)
            for c in range(tiles):
                shift = (c - face) & (LANES - 1)
                face_u = jnp.where(inner == c, pltpu.roll(u[c], shift, 1), face_u)
                face_y = jnp.where(inner == c, pltpu.roll(y[edge * c : edge * (c + 1)], shift, 1), face_y)
            faces_u.append(face_u)
            faces_y.append(face_y)

    stack = jnp.concatenate(swap_blocks(ends0) + swap_blocks(ends1), 0)
    ends_of = const[:, : 3 * edge].astype(jnp.bfloat16)
    faces_of = const[:, LANES : 4 * LANES].astype(jnp.bfloat16)
    turn = right_of_swapped(jnp.where(on_block, jnp.concatenate([const[:, 4 * LANES :]] * 4, 0), 0.0))
    stack = dot(right_of(stack, 1), turn)
    both = dot(ends_of, right_of(jnp.concatenate([stack[:edge], stack[edge:]], 1)))
    part_u = dot_lanes(faces_of, right_of(jnp.concatenate(faces_u, 0), 1))
    part_u = dot(right_of(part_u, 1), turn)
    part_y = dot_lanes(faces_of, right_of(jnp.concatenate(faces_y, 0), 1))
    fields = swap_blocks([both[:, :LANES], both[:, LANES:], part_u, part_y])
    for x, part in enumerate(fields):
        msg[pl.ds(x, edge, stride=ROWS), :] = part
    row = jnp.zeros((edge, LANES), jnp.float32)
    for b in range(count):
        for q in range(2):
            for x, rate in enumerate((rates[b, q, 0], rates[b, q, closed], rates[b, q, normal])):
                row = jnp.where(lane == (2 * b + q) * edge + x, rate, row)
    msg[pl.ds(4, edge, stride=ROWS), :] = row


def local_kernel(
    near_in, solved_in, inverses_in,
    base, pick, flags, edges,
    near, table, solved, inverses, work, other, sems,
):
    count, edge = inverses.shape[0], inverses.shape[3]
    tiles = edge // 4
    size = tiles * edge
    slots = near.shape[2]
    copies = [
        pltpu.make_async_copy(source, target, sems.at[x])
        for x, (source, target) in enumerate(
            (
                (near_in, near),
                (near_in, table),
                (solved_in, solved),
                (inverses_in, inverses),
            )
        )
    ]
    for copy in copies:
        copy.start()
    for copy in copies[:2]:
        copy.wait()
    normal = normal_of(near, 0)
    closed = 3 - normal
    up = near[normal, 1, 0] >= 0
    touch = up | (near[normal, 0, 0] >= 0)

    lane = lane_of((8, LANES))
    back = jnp.broadcast_to(table[0, 0:1, :], (8, slots))
    back = jnp.concatenate([back] * (LANES // slots), 1)
    pointer = jnp.where(back >= 0, back, lane & (slots - 1))
    place = jnp.where(back >= 0, 1, 0)

    def pull(values, index):
        return jnp.take_along_axis(values, index, axis=1, mode="promise_in_bounds")

    reach = 1
    while reach < edge:
        place = place + pull(place, pointer)
        pointer = pull(pointer, pointer)
        reach *= 2
    chain = jnp.where(pointer == pointer[:, 0:1], 0, edge) + place
    goal = pull(chain, (lane & (edge - 1)) * count + lane // (2 * edge)) + 2 * (lane & edge)
    hit = lax.broadcasted_iota(jnp.int32, (LANES, LANES), 0) == goal[0:1]
    pick[...] = hit.astype(jnp.float32).T
    face = jnp.where(((lane & edge) == 0) == up, edge - 1, 0).astype(jnp.float32)
    depth = lax.broadcasted_iota(jnp.int32, (8, LANES), 0)
    angle = jnp.full((8, LANES), lax.axis_index("bricks")).astype(jnp.float32) * (0.5 * math.pi / edge)
    half = jnp.sin(angle)
    flags[...] = jnp.where(
        depth == 0,
        face,
        jnp.where(
            depth == 1,
            jnp.where(touch, 1.0, 0.0),
            jnp.where(depth == 2, jnp.where(normal == 2, 1.0, 0.0), 4.0 * half * half),
        ),
    )

    for copy in copies[2:]:
        copy.wait()
    first_slot = lax.axis_index("bricks") * count
    for b in range(count):
        face = jnp.where(near[normal, 1, first_slot + b] >= 0, edge - 1, 0)
        for q in range(2):
            x = 2 * b + q
            at = size * x
            swap_rows(solved, at, other, 0, edge)
            whole = dot(left_of(inverses[b, closed, q]), right_of(wide(other, 0, edge)))
            for c in range(tiles):
                other[pl.ds(edge * c, edge), :] = whole[:, LANES * c : LANES * (c + 1)]
            swap_rows(other, 0, work, 0, edge)
            base[pl.ds(at, size), :] = work[...]
            row_n = jnp.concatenate([inverses[b, normal, q, pl.ds(face, 1), :]] * 4, 1)
            edges[x, 0] = jnp.broadcast_to(inverses[b, 0, q, :, 0:1], (edge, LANES))
            edges[x, 1] = jnp.broadcast_to(inverses[b, 0, q, :, edge - 1 : edge], (edge, LANES))
            edges[x, 2] = jnp.broadcast_to(row_n, (edge, LANES))


def owner_kernel(recv, pick, flags, const, out):
    edge = const.shape[0]
    turned = const[:, : 3 * edge].astype(jnp.bfloat16)
    lam = const[:, LANES : 2 * LANES]
    v_first = const[:, 2 * LANES : 3 * LANES]
    v_last = const[:, 3 * LANES : 4 * LANES]
    face, touch, normal_2, my_lam = flags[0:1], flags[1:2], flags[2:3], flags[3:4]

    hit = pick[...].astype(jnp.bfloat16)
    data = jnp.concatenate([recv[pl.ds(x, edge, stride=ROWS), :] for x in range(4)], 0).T
    tail = recv[pl.ds(4, edge, stride=ROWS), :]
    tail = jnp.concatenate([tail] + [pltpu.roll(tail, LANES - edge * x, 1) for x in range(1, 4)], 0).T[:16]
    parts = dot(exact_of(jnp.concatenate([tail, data], 0)), jnp.concatenate([hit] * 3, 0))
    rate_0, rate_t, rate_n = parts[0:1], parts[1:2], parts[2:3]
    y0, y1, face_u, face_y = (parts[16 + edge * x : 16 + edge * (x + 1)] for x in range(4))

    lane = lane_of((1, LANES))
    place = lane & (edge - 1)
    first_row = (lane & edge) == 0

    def partner(x):
        return jnp.where(first_row, pltpu.roll(x, LANES - edge, 1), pltpu.roll(x, edge, 1))

    def after(x, s=1):
        return pltpu.roll(x, LANES - s, 1)

    def before(x, s=1):
        return pltpu.roll(x, s, 1)

    damp_0 = 1.0 / (1.0 + lam * rate_0)
    damp_n = 1.0 / (1.0 + lam * rate_n)
    damp_t = 1.0 / (1.0 + my_lam * rate_t)
    other_n = partner(rate_n)
    g = jnp.where(touch > 0.5, 2.0 * rate_n * other_n / (rate_n + other_n), 0.0)
    cross = 2.0 * g * (partner(face_u) - face_u)
    near_c = jnp.sum(damp_0 * v_first * v_first, 0, keepdims=True)
    far_c = jnp.sum(damp_0 * v_first * v_last, 0, keepdims=True)
    end_n = jnp.sum(damp_n * v_first * v_first, 0, keepdims=True)
    damped = damp_0 * cross
    pieces = dot(turned, right_of(jnp.concatenate([damped, damp_0 * v_first, damp_0 * v_last], 1)))
    spread, col_0, col_1 = (pieces[:, LANES * x : LANES * (x + 1)] for x in range(3))
    v_face = jnp.where(face < 0.5, v_first, v_last)
    y0 = y0 + v_face * jnp.sum(v_first * damped, 0, keepdims=True)
    y1 = y1 + v_face * jnp.sum(v_last * damped, 0, keepdims=True)

    inv_rate = 1.0 / rate_0
    open_face = place < edge - 1
    diag = jnp.where(open_face, 0.5 * (inv_rate + after(inv_rate)) + near_c + after(near_c), 1.0)
    lower = jnp.where(open_face & (place > 0), -far_c, 0.0)
    upper = jnp.where(place < edge - 2, -after(far_c), 0.0)
    right = jnp.where(open_face, y1 - after(y0), 0.0)
    step = 1
    while step < edge:
        inverse = 1.0 / diag
        back = -lower * before(inverse, step)
        fore = -upper * after(inverse, step)
        diag = diag + back * before(upper, step) + fore * after(lower, step)
        right = right + back * before(right, step) + fore * after(right, step)
        lower = back * before(lower, step)
        upper = fore * after(upper, step)
        step *= 2
    flux_up = right / diag
    flux_down = jnp.where(place > 0, before(flux_up), 0.0)

    weight_down = jnp.sum(damp_n * v_face * flux_down, 0, keepdims=True)
    weight_up = jnp.sum(damp_n * v_face * flux_up, 0, keepdims=True)
    ends = face_y + end_n * spread + col_0 * weight_down - col_1 * weight_up
    ends = jnp.where(normal_2 > 0.5, damp_t, 1.0) * ends
    jump = g / (1.0 + g * (end_n + partner(end_n))) * (ends - partner(ends))
    face_out = jnp.where(normal_2 > 0.5, damp_t * spread - jump, damp_t * (spread - jump))
    damp_nt = damp_n * damp_t
    lines = dot(turned, right_of(jnp.concatenate([damp_nt * flux_down, damp_nt * flux_up], 1)))
    packed = jnp.concatenate(
        [lines[:, :LANES], lines[:, LANES:], face_out, jnp.zeros((edge, LANES), jnp.float32)], 0
    )
    reply = dot_lanes(jnp.concatenate([hit] * 3, 1), exact_of(packed))
    kinds = swap_blocks([reply[edge * x : edge * (x + 1)] for x in range(4)])
    for x in range(3):
        out[pl.ds(x, edge, stride=3), :] = kinds[x]


def update_kernel(
    recv, base, edges, flags, calcium, buffer, const,
    calcium_out, buffer_out,
    calcium_next, buffer_next, work, sems,
):
    count, edge = calcium.shape[0], calcium.shape[1]
    tiles = edge // 4
    size = tiles * edge
    swapped = flags[2, 0] < 0.5
    old = jnp.where(flags[2:3] < 0.5, 0.0, 1.0)
    low, high, face_part = (recv[pl.ds(x, edge, stride=3), :] for x in range(3))
    high_s, low_s = parts_of(face_part)
    turn = jnp.concatenate([high_s, low_s, high_s, jnp.zeros_like(high_s)], 0).T.astype(jnp.bfloat16)
    face_wide = dot(turn, const[:, LANES:].astype(jnp.bfloat16))
    lines = dot(const[:edge, : 3 * edge].astype(jnp.bfloat16), right_of(jnp.concatenate([low, high], 1)))
    rows = []
    for e in range(2):
        work[pl.ds(edge * e, edge), :] = lines[:, LANES * e : LANES * (e + 1)]
        rows.append(swap_blocks([work[pl.ds(edge * e + t4, tiles, stride=4), :] for t4 in range(4)]))

    stores = [
        pltpu.make_async_copy(source.at[b], to.at[b], sems.at[2 * b + q])
        for b in range(count)
        for q, (source, to) in enumerate(((calcium_next, calcium_out), (buffer_next, buffer_out)))
    ]
    for b in range(count):
        for q, (ref, now) in enumerate(((calcium_next, calcium), (buffer_next, buffer))):
            x = 2 * b + q
            at = size * x
            col_0, col_1, row_n = edges[x, 0], edges[x, 1], edges[x, 2]
            for c in range(tiles):
                part = slice(LANES * c, LANES * (c + 1))
                ref[b, :, part] = (
                    (base[pl.ds(at + edge * c, edge), :] + old * now[b, :, part])
                    + face_wide[edge * x : edge * (x + 1), part] * row_n
                    + (col_0 * rows[0][x][c : c + 1] - col_1 * rows[1][x][c : c + 1])
                )
            stores[x].start()
    for store in stores:
        store.wait()

    @pl.when(swapped)
    def _():
        swap_inner((calcium_next, buffer_next), edge)
        calcium_next[...] = calcium_next[...] + calcium[...]
        buffer_next[...] = buffer_next[...] + buffer[...]
        for store in stores:
            store.start()
        for store in stores:
            store.wait()


def fast_body(calcium, buffer, fraction, rates, inverses, neighbors, ranks):
    count, edge = calcium.shape[0], calcium.shape[1]
    devices = lax.axis_size("bricks")
    tiles = edge // 4
    size = tiles * edge
    f32 = jnp.float32
    basis, eigen = cosine_basis(edge)
    place = np.arange(edge)
    ends_of = np.zeros((edge, edge))
    ends_of[:, (place % 4) * tiles + place // 4] = basis
    faces_of = np.zeros((edge, LANES))
    faces_of[:, (place % 4) * edge + place // 4] = basis
    pad = lambda x: np.pad(x, ((0, 0), (0, LANES - x.shape[1])))
    message_const = np.concatenate([pad(host_left(ends_of)), host_left(faces_of), np.tile(basis.T, (1, 4))], 1)
    lanes_of = lambda x: np.tile(x[:, None], (1, LANES))
    owner_const = np.concatenate(
        [pad(host_left(basis.T))]
        + [lanes_of(x) for x in (eigen, basis[:, 0], basis[:, -1])],
        1,
    )
    expand = np.pad(host_right(np.repeat(basis, edge, 1)), ((0, LANES - 3 * edge), (0, 0)))
    back_const = np.pad(pad(host_left(basis.T)), ((0, LANES - edge), (0, 0)))
    update_const = np.concatenate([back_const, expand], 1)
    smem = pl.BlockSpec(memory_space=pltpu.SMEM)
    vmem = pl.BlockSpec(memory_space=pltpu.VMEM)
    hbm = pl.BlockSpec(memory_space=pltpu.HBM)
    params = pltpu.CompilerParams(vmem_limit_bytes=48 * 2**20)
    const = lambda x: jnp.asarray(x, f32)
    field = jax.ShapeDtypeStruct(calcium.shape, f32)
    tall = jax.ShapeDtypeStruct((2 * count * size, LANES), f32)

    stay = lambda x: pltpu.with_memory_space_constraint(x, pltpu.HBM)
    msg, solved = pl.pallas_call(
        message_kernel,
        out_shape=(jax.ShapeDtypeStruct((devices * ROWS, LANES), f32), tall),
        in_specs=[hbm] * 7,
        out_specs=(vmem, vmem),
        scratch_shapes=[
            pltpu.SMEM(neighbors.shape, jnp.int32),
            pltpu.SMEM((count, 2, 3), f32),
            pltpu.VMEM(calcium.shape, f32),
            pltpu.VMEM(calcium.shape, f32),
            pltpu.VMEM(fraction.shape, f32),
            pltpu.VMEM(inverses.shape, f32),
            pltpu.VMEM(message_const.shape, f32),
            pltpu.SemaphoreType.DMA((7,)),
        ],
        compiler_params=pltpu.CompilerParams(vmem_limit_bytes=48 * 2**20),
        name="message",
    )(*(stay(x) for x in (neighbors, rates.transpose(0, 2, 1), calcium, buffer, fraction, inverses, const(message_const))))
    recv = lax.all_to_all(msg.reshape(devices * ROWS, 1, LANES), "bricks", 0, 0, tiled=True).reshape(devices * ROWS, LANES)
    base, pick, flags, edges = pl.pallas_call(
        local_kernel,
        out_shape=(
            tall,
            jax.ShapeDtypeStruct((LANES, LANES), f32),
            jax.ShapeDtypeStruct((8, LANES), f32),
            jax.ShapeDtypeStruct((2 * count, 3, edge, LANES), f32),
        ),
        in_specs=[hbm] * 3,
        out_specs=(vmem,) * 4,
        scratch_shapes=[
            pltpu.SMEM(neighbors.shape, jnp.int32),
            pltpu.VMEM(neighbors.shape, jnp.int32),
            pltpu.VMEM(tall.shape, f32),
            pltpu.VMEM(inverses.shape, f32),
            pltpu.VMEM((size, LANES), f32),
            pltpu.VMEM((size, LANES), f32),
            pltpu.SemaphoreType.DMA((4,)),
        ],
        compiler_params=pltpu.CompilerParams(vmem_limit_bytes=48 * 2**20),
        cost_estimate=pl.CostEstimate(flops=2 * 10**7, bytes_accessed=4 * 10**6, transcendentals=0),
        name="local_solution",
    )(neighbors, solved, inverses)
    reply = pl.pallas_call(
        owner_kernel,
        out_shape=jax.ShapeDtypeStruct((devices * 3, LANES), f32),
        in_specs=[vmem] * 4,
        out_specs=vmem,
        compiler_params=params,
        name="chain_and_face_solves",
    )(recv, pick, flags, const(owner_const))
    back = lax.all_to_all(reply.reshape(devices * 3, 1, LANES), "bricks", 0, 0, tiled=True)
    return pl.pallas_call(
        update_kernel,
        out_shape=(field, field),
        in_specs=[vmem] * 7,
        out_specs=(hbm, hbm),
        scratch_shapes=[
            pltpu.VMEM(calcium.shape, f32),
            pltpu.VMEM(buffer.shape, f32),
            pltpu.VMEM((2 * edge, LANES), f32),
            pltpu.SemaphoreType.DMA((2 * count,)),
        ],
        compiler_params=params,
        name="rank_three_update",
    )(back.reshape(devices * 3, LANES), base, edges, flags, calcium, buffer, const(update_const))


def body(calcium, buffer, fraction, rates, inverses, neighbors, ranks):
    count, edge = calcium.shape[0], calcium.shape[1]
    devices = lax.axis_size("bricks")
    if edge == GX and devices == edge and count == 2 and 4 * edge == LANES:
        return fast_body(calcium, buffer, fraction, rates, inverses, neighbors, ranks)
    return general_body(calcium, buffer, fraction, rates, inverses, neighbors, ranks)


def solution(mesh):
    in_specs = (
        P("bricks", None, None),
        P("bricks", None, None),
        P("bricks", None, None),
        P("bricks", None, None),
        P("bricks", None, None, None, None),
        P(),
        P(),
    )
    out_specs = (P("bricks", None, None), P("bricks", None, None))
    return jax.shard_map(body, mesh=mesh, in_specs=in_specs, out_specs=out_specs, check_vma=False)
```

```python
from functools import partial
import math

import jax
import jax.numpy as jnp
import numpy as np
from jax import lax
from jax.experimental import pallas as pl
from jax.experimental.pallas import tpu as pltpu
from jax.sharding import PartitionSpec as P

GX = 32


KON = 0.5
KOFF = 0.3
BTOT = 2.0
INFLUX = 0.1


def fetch(table, index):
    rows = jnp.take(table, jnp.maximum(index, 0), axis=0)
    has = (index >= 0).reshape((-1,) + (1,) * (rows.ndim - 1))
    return jnp.where(has, rows, jnp.zeros_like(rows))


def lookup(planes, before, after):
    sides = []
    for d in range(3):
        lower = fetch(planes[:, d, 1], before[d])
        upper = fetch(planes[:, d, 0], after[d])
        sides.append(jnp.stack([lower, upper], 1))
    return jnp.stack(sides, 1)


def coupling(rate_all, neighbors):
    per_dim = []
    for d in range(3):
        mine = rate_all[:, d]
        sides = []
        for side in range(2):
            other = fetch(mine, neighbors[d, side])
            has = (neighbors[d, side] >= 0)[:, None]
            sides.append(jnp.where(has, 2.0 * mine * other / (mine + other), jnp.zeros_like(mine)))
        per_dim.append(jnp.stack(sides, 1))
    return jnp.stack(per_dim, 1)


def end_planes(field):
    count, edge = (field.shape[0], field.shape[2])
    per_dim = []
    for d in range(3):
        first = lax.index_in_dim(field, 0, 2 + d, False).reshape(count, 2, edge * edge)
        last = lax.index_in_dim(field, edge - 1, 2 + d, False).reshape(count, 2, edge * edge)
        per_dim.append(jnp.stack([first, last], 1))
    return jnp.stack(per_dim, 1)


def operator(field, d, rate, glow, gup, hlow, hup):
    axis = 2 + d
    edge = field.shape[axis]
    plane_shape = lax.index_in_dim(field, 0, axis, False).shape
    lower_face = jnp.expand_dims(hlow.reshape(plane_shape), axis)
    upper_face = jnp.expand_dims(hup.reshape(plane_shape), axis)
    upper = jnp.concatenate([lax.slice_in_dim(field, 1, edge, axis=axis), upper_face], axis)
    lower = jnp.concatenate([lower_face, lax.slice_in_dim(field, 0, edge - 1, axis=axis)], axis)
    place = lax.broadcasted_iota(jnp.int32, field.shape, axis)
    inner = rate[:, :, None, None, None]
    c_up = jnp.where(place == edge - 1, gup[:, :, None, None, None], inner)
    c_down = jnp.where(place == 0, glow[:, :, None, None, None], inner)
    return c_up * (upper - field) + c_down * (lower - field)


def reaction(field, fraction):
    count, edge = (field.shape[0], field.shape[2])
    alpha = fraction.reshape(count, edge, edge, edge)
    calc, bound = (field[:, 0], field[:, 1])
    bind = KON * calc * (BTOT - bound) - KOFF * bound
    return jnp.stack([-bind + INFLUX * (1.0 - alpha) / alpha, bind], 1)


def apply_inverse(block, field, d):
    forms = ["psab,psbjk->psajk", "psab,psibk->psiak", "psab,psijb->psija"]
    return jnp.einsum(forms[d], block, field, precision=lax.Precision.HIGHEST)


def line_ends(field, d):
    count, edge = (field.shape[0], field.shape[2])
    first = lax.index_in_dim(field, 0, 2 + d, False).reshape(count, 2, edge * edge)
    last = lax.index_in_dim(field, edge - 1, 2 + d, False).reshape(count, 2, edge * edge)
    return jnp.stack([first, last], 2)


def block_terms(glow, gup, corner):
    v_first, v_last, w_first, w_last = (
        corner[..., 0],
        corner[..., 1],
        corner[..., 2],
        corner[..., 3],
    )
    a00 = 1.0 + glow * v_first
    a01 = gup * w_first
    a10 = glow * v_last
    a11 = 1.0 + gup * w_last
    lq0 = -glow * v_first
    lq1 = -glow * v_last
    up0 = -gup * w_first
    up1 = -gup * w_last
    return (a00, a01, a10, a11, lq0, lq1, up0, up1)


def chain_order(before, rank):
    slots = jnp.arange(before.shape[0], dtype=jnp.int32)
    pointer = jnp.where(before >= 0, before, slots)
    for step in range(GX.bit_length()):
        pointer = jnp.take(pointer, pointer, axis=0)
    sort_key = pointer * GX + rank
    order = jnp.argsort(sort_key)
    inverse_order = jnp.argsort(order)
    return (order, inverse_order)


def shift_down(values):
    return jnp.concatenate([jnp.zeros_like(values[:1]), values[:-1]], 0)


def shift_up(values):
    return jnp.concatenate([values[1:], jnp.zeros_like(values[:1])], 0)


def compose_maps(first_map, second_map):
    e00, e01, e10, e11 = first_map
    l00, l01, l10, l11 = second_map
    n00 = l00 * e00 + l01 * e10
    n01 = l00 * e01 + l01 * e11
    n10 = l10 * e00 + l11 * e10
    n11 = l10 * e01 + l11 * e11
    scale = jnp.abs(n00) + jnp.abs(n01) + jnp.abs(n10) + jnp.abs(n11)
    return (n00 / scale, n01 / scale, n10 / scale, n11 / scale)


def compose_affine(first_map, second_map):
    first_q, first_p = first_map
    second_q, second_p = second_map
    return (first_q * second_q, second_p + second_q * first_p)


def sorted_solve(glow, gup, corner, before, after, order, inverse_order, ends):
    glow = jnp.take(glow, order, axis=0)
    gup = jnp.take(gup, order, axis=0)
    corner = jnp.take(corner, order, axis=0)
    has_b = jnp.take(before, order, axis=0) >= 0
    has_a = jnp.take(after, order, axis=0) >= 0
    arranged = jnp.take(ends, order, axis=0)
    y0 = arranged[:, :, 0]
    y1 = arranged[:, :, 1]
    a00, a01, a10, a11, lq0, lq1, up0, up1 = block_terms(glow, gup, corner)
    maps = (
        -(lq0 * up1 - lq1 * up0),
        a00 * up1 - a10 * up0,
        -(lq0 * a11 - a01 * lq1),
        a00 * a11 - a01 * a10,
    )
    summed = lax.associative_scan(compose_maps, maps, axis=0)
    f1_prev = summed[1] / summed[3]
    fq = shift_down(f1_prev)
    b00 = a00 - lq0 * fq
    b10 = a10 - lq1 * fq
    det = b00 * a11 - a01 * b10
    f0 = (a11 * up0 - a01 * up1) / det
    f1 = (b00 * up1 - b10 * up0) / det
    slope = (-(b00 * lq1 - b10 * lq0) / det)[:, :, None]
    offset = (b00[:, :, None] * y1 - b10[:, :, None] * y0) / det[:, :, None]
    e1 = lax.associative_scan(compose_affine, (slope, offset), axis=0)[1]
    eq = shift_down(e1)
    e0 = (
        a11[:, :, None] * y0 - a01[:, :, None] * y1 - (a11 * lq0 - a01 * lq1)[:, :, None] * eq
    ) / det[:, :, None]
    zp = lax.associative_scan(compose_affine, (-f0[:, :, None], e0), reverse=True, axis=0)[1]
    pn = shift_up(zp)
    zq = e1 - f1[:, :, None] * pn
    low = jnp.where(has_b[:, None, None], zp - shift_down(zq), jnp.zeros_like(zp))
    high = jnp.where(has_a[:, None, None], zq - pn, jnp.zeros_like(zq))
    return jnp.take(jnp.stack([low, high], 2), inverse_order, axis=0)


def correct(local, block, glow, gup, jumps, d):
    axis = 2 + d
    count, edge = (local.shape[0], local.shape[2])
    shape_v = [count, 2, 1, 1, 1]
    shape_v[axis] = edge
    first_col = block[..., 0].reshape(shape_v)
    last_col = block[..., edge - 1].reshape(shape_v)
    plane_shape = lax.index_in_dim(local, 0, axis, False).shape
    low = jnp.expand_dims(jumps[:, :, 0].reshape(plane_shape), axis)
    high = jnp.expand_dims(jumps[:, :, 1].reshape(plane_shape), axis)
    return (
        local
        - glow[:, :, None, None, None] * low * first_col
        - gup[:, :, None, None, None] * high * last_col
    )


def general_body(calcium, buffer, fraction, rates, inverses, neighbors, ranks):
    count, edge = (calcium.shape[0], calcium.shape[1])
    devices = lax.axis_size("bricks")
    square = edge * edge
    per_device = square // devices
    start = lax.axis_index("bricks") * count
    corners = jnp.stack(
        [
            inverses[..., 0, 0],
            inverses[..., edge - 1, 0],
            inverses[..., 0, edge - 1],
            inverses[..., edge - 1, edge - 1],
        ],
        -1,
    )
    rate_all, corner_all = (
        lax.all_gather(rates, "bricks", axis=0, tiled=True),
        lax.all_gather(corners, "bricks", axis=0, tiled=True),
    )
    couple_all = coupling(rate_all, neighbors)
    couple = lax.dynamic_slice_in_dim(couple_all, start, count, 0)
    field = jnp.stack([calcium, buffer], 1).reshape(count, 2, edge, edge, edge)
    planes = end_planes(field).reshape(count, 3, 2, 2, devices, per_device)
    lined = lookup(
        lax.all_to_all(planes, "bricks", split_axis=4, concat_axis=0, tiled=True),
        neighbors[:, 0],
        neighbors[:, 1],
    )
    halos = lax.all_to_all(lined, "bricks", split_axis=0, concat_axis=4, tiled=True).reshape(
        count, 3, 2, 2, square
    )
    lams = [
        operator(
            field, d, rates[:, d], couple[:, d, 0], couple[:, d, 1], halos[:, d, 0], halos[:, d, 1]
        )
        for d in range(3)
    ]
    rhs = field + lams[0] + 2.0 * lams[1] + 2.0 * lams[2] + reaction(field, fraction)

    def solve(right, d):
        block = inverses[:, d]
        local = apply_inverse(block, right, d)
        ends = line_ends(local, d).reshape(count, 2, 2, devices, per_device)
        order, inverse_order = chain_order(neighbors[d, 0], ranks[d])
        chain_fn = partial(
            sorted_solve,
            couple_all[:, d, 0],
            couple_all[:, d, 1],
            corner_all[:, d],
            neighbors[d, 0],
            neighbors[d, 1],
            order,
            inverse_order,
        )
        lined_jumps = chain_fn(
            lax.all_to_all(ends, "bricks", split_axis=3, concat_axis=0, tiled=True)[:, :, :, 0]
        )[:, :, :, None]
        jumps = lax.all_to_all(
            lined_jumps, "bricks", split_axis=0, concat_axis=3, tiled=True
        ).reshape(count, 2, 2, square)
        return correct(local, block, couple[:, d, 0], couple[:, d, 1], jumps, d)

    first = solve(rhs, 0)
    second = solve(first - lams[1], 1)
    third = solve(second - lams[2], 2)
    result = third.reshape(count, 2, edge, edge * edge)
    return (result[:, 0], result[:, 1])


LANES = 128


ROWS = 5


def cosine_basis(edge):
    wave = np.arange(edge)[:, None]
    place = np.arange(edge)[None, :]
    basis = np.sqrt(2.0 / edge) * np.cos(np.pi * wave * (place + 0.5) / edge)
    basis[0] = math.sqrt(1.0 / edge)
    eigen = 2.0 - 2.0 * np.cos(np.pi * np.arange(edge) / edge)
    return basis, eigen


def parts_of(x):
    high = x.astype(jnp.bfloat16).astype(jnp.float32)
    return high, (x - high).astype(jnp.bfloat16).astype(jnp.float32)


def left_of(x):
    high, low = parts_of(x)
    return jnp.concatenate([high, low, high], 1).astype(jnp.bfloat16)


def right_of(x, axis=0):
    high = x.astype(jnp.bfloat16)
    low = (x - high.astype(jnp.float32)).astype(jnp.bfloat16)
    return jnp.concatenate([high, high, low], axis)


def right_of_swapped(x):
    high = x.astype(jnp.bfloat16)
    low = (x - high.astype(jnp.float32)).astype(jnp.bfloat16)
    return jnp.concatenate([high, low, high], 0)


def pair_of(x):
    high = x.astype(jnp.bfloat16)
    return jnp.concatenate([high, (x - high.astype(jnp.float32)).astype(jnp.bfloat16)], 1)


def exact_of(x):
    high = x.astype(jnp.bfloat16)
    rest = x - high.astype(jnp.float32)
    middle = rest.astype(jnp.bfloat16)
    return jnp.concatenate([high, middle, (rest - middle.astype(jnp.float32)).astype(jnp.bfloat16)], 1)


def dot(a, b):
    return jnp.dot(a, b, preferred_element_type=jnp.float32)


def dot_lanes(a, b):
    return lax.dot_general(a, b, (((1,), (1,)), ((), ())), preferred_element_type=jnp.float32)


def host_left(x):
    high = x.astype(jnp.bfloat16).astype(np.float64)
    low = (x - high).astype(jnp.bfloat16).astype(np.float64)
    return np.concatenate([high, low, high], 1)


def host_right(x):
    high = x.astype(jnp.bfloat16).astype(np.float64)
    low = (x - high).astype(jnp.bfloat16).astype(np.float64)
    return np.concatenate([high, high, low], 0)


def lane_of(shape):
    return lax.broadcasted_iota(jnp.int32, shape, len(shape) - 1)


def swap_blocks(four):
    x0, x1, x2, x3 = four
    lane = lane_of(x0.shape)
    low = (lane & 64) == 0
    y0, y2 = jnp.where(low, x0, pltpu.roll(x2, 64, 1)), jnp.where(low, pltpu.roll(x0, 64, 1), x2)
    y1, y3 = jnp.where(low, x1, pltpu.roll(x3, 64, 1)), jnp.where(low, pltpu.roll(x1, 64, 1), x3)
    even = (lane & 32) == 0
    z0, z1 = jnp.where(even, y0, pltpu.roll(y1, 32, 1)), jnp.where(even, pltpu.roll(y0, 96, 1), y1)
    z2, z3 = jnp.where(even, y2, pltpu.roll(y3, 32, 1)), jnp.where(even, pltpu.roll(y2, 96, 1), y3)
    return [z0, z1, z2, z3]


def swap_rows(source, base, scratch, at, edge):
    tiles = edge // 4
    for c in range(tiles):
        rows = [source[pl.ds(base + edge * c + g, tiles, stride=4), :] for g in range(4)]
        for t4, row in enumerate(swap_blocks(rows)):
            scratch[pl.ds(at + 4 * c + t4, tiles, stride=edge), :] = row


def tile_rows(x, edge):
    tiles = edge // 4
    return jnp.concatenate([x[:, LANES * c : LANES * (c + 1)] for c in range(tiles)], 0)


def wide(ref, at, edge):
    tiles = edge // 4
    return jnp.concatenate([ref[pl.ds(at + edge * c, edge), :] for c in range(tiles)], 1)


def swap_inner(refs, edge):
    tiles = edge // 4
    fields = [(ref, b) for ref in refs for b in range(ref.shape[0])]
    whole = [
        exact_of(jnp.concatenate([ref[b, :, LANES * c : LANES * (c + 1)] for ref, b in fields], 0))
        for c in range(tiles)
    ]
    row = lax.broadcasted_iota(jnp.int32, (LANES, LANES), 0)
    lane = lane_of((LANES, LANES))
    for to in range(tiles):
        total = jnp.zeros((len(fields) * edge, LANES), jnp.float32)
        for c in range(tiles):
            hit = ((row & (edge - 1)) == 4 * to + lane // edge) & ((lane & (edge - 1)) == 4 * c + row // edge)
            hit = hit.astype(jnp.float32).astype(jnp.bfloat16)
            total = total + dot(whole[c], jnp.concatenate([hit] * 3, 0))
        for f, (ref, b) in enumerate(fields):
            ref[b, :, LANES * to : LANES * (to + 1)] = total[edge * f : edge * (f + 1)]


def normal_of(near, slot):
    along_j = (near[1, 0, slot] >= 0) | (near[1, 1, slot] >= 0)
    return jnp.where(along_j, 1, 2)


def message_kernel(
    near_in, rates_in, calcium_in, buffer_in, fraction_in, inverses_in, const_in,
    msg, solved,
    near, rates, calcium, buffer, fraction, inverses, const, sems,
):
    count, edge = calcium.shape[0], calcium.shape[1]
    tiles = edge // 4
    size = tiles * edge
    copies = [
        pltpu.make_async_copy(source, target, sems.at[x])
        for x, (source, target) in enumerate(
            (
                (near_in, near),
                (rates_in, rates),
                (calcium_in, calcium),
                (buffer_in, buffer),
                (fraction_in, fraction),
                (inverses_in, inverses),
                (const_in, const),
            )
        )
    ]
    for copy in copies:
        copy.start()
    first_slot = lax.axis_index("bricks") * count
    for copy in copies:
        copy.wait()
    normal = normal_of(near, first_slot)
    closed = 3 - normal

    @pl.when(normal == 1)
    def _():
        swap_inner((calcium, buffer, fraction), edge)

    lane = lane_of((edge, LANES))
    inner = lane & (edge - 1)
    square_row = lax.broadcasted_iota(jnp.int32, (LANES, LANES), 0)
    square_lane = lane_of((LANES, LANES))
    on_block = (square_row // edge) == (square_lane // edge)
    faces_u, faces_y, ends0, ends1 = [], [], [], []
    for b in range(count):
        face = jnp.where(near[normal, 1, first_slot + b] >= 0, edge - 1, 0)
        calc = [calcium[b, :, LANES * c : LANES * (c + 1)] for c in range(tiles)]
        bound = [buffer[b, :, LANES * c : LANES * (c + 1)] for c in range(tiles)]
        alpha = [fraction[b, :, LANES * c : LANES * (c + 1)] for c in range(tiles)]
        bind = [KON * x * (BTOT - y) - KOFF * y for x, y in zip(calc, bound)]
        source_calc = [-w + INFLUX * (1.0 - a) / a for w, a in zip(bind, alpha)]
        for q, (u, source) in enumerate(((calc, source_calc), (bound, bind))):
            at = size * (2 * b + q)
            rate_t, rate_n = 2.0 * rates[b, q, closed], 2.0 * rates[b, q, normal]
            ahead = [pltpu.roll(x, LANES - edge, 1) for x in u]
            behind = [pltpu.roll(x, edge, 1) for x in u]
            f = []
            for c in range(tiles):
                x = u[c]
                next_t = jnp.where(lane < LANES - edge, ahead[c], ahead[c + 1] if c + 1 < tiles else x)
                last_t = jnp.where(lane >= edge, behind[c], behind[c - 1] if c else x)
                next_n = jnp.where(inner == edge - 1, x, pltpu.roll(x, LANES - 1, 1))
                last_n = jnp.where(inner == 0, x, pltpu.roll(x, 1, 1))
                twice = x + x
                along = rate_t * (next_t + last_t - twice) + rate_n * (next_n + last_n - twice)
                f.append(twice + along + source[c])
            g = dot(left_of(inverses[b, 0, q]), right_of(jnp.concatenate(f, 1)))
            ends0.append(jnp.concatenate([g[0:1, LANES * c : LANES * (c + 1)] for c in range(tiles)], 0))
            ends1.append(jnp.concatenate([g[edge - 1 : edge, LANES * c : LANES * (c + 1)] for c in range(tiles)], 0))
            w = jnp.concatenate([g[:, LANES * c : LANES * (c + 1)] - 2.0 * u[c] for c in range(tiles)], 0)
            block = jnp.concatenate([inverses[b, normal, q]] * 4, 1)
            block = jnp.where(on_block, jnp.concatenate([block] * 4, 0), 0.0)
            high = w.astype(jnp.bfloat16)
            low = (w - high.astype(jnp.float32)).astype(jnp.bfloat16)
            y = dot(jnp.concatenate([high, high, low], 1), right_of_swapped(block))
            solved[pl.ds(at, size), :] = y
            face_u = jnp.zeros((edge, LANES), jnp.float32)
            face_y = jnp.zeros((edge, LANES), jnp.float32)
            for c in range(tiles):
                shift = (c - face) & (LANES - 1)
                face_u = jnp.where(inner == c, pltpu.roll(u[c], shift, 1), face_u)
                face_y = jnp.where(inner == c, pltpu.roll(y[edge * c : edge * (c + 1)], shift, 1), face_y)
            faces_u.append(face_u)
            faces_y.append(face_y)

    stack = jnp.concatenate(swap_blocks(ends0) + swap_blocks(ends1), 0)
    ends_of = const[:, : 3 * edge].astype(jnp.bfloat16)
    faces_of = const[:, LANES:].astype(jnp.bfloat16)
    both = dot(ends_of, right_of(jnp.concatenate([stack[:edge], stack[edge:]], 1)))
    part_u = dot_lanes(faces_of, right_of(jnp.concatenate(faces_u, 0), 1))
    part_y = dot_lanes(faces_of, right_of(jnp.concatenate(faces_y, 0), 1))
    fields = swap_blocks([both[:, :LANES], both[:, LANES:], part_u, part_y])
    for x, part in enumerate(fields):
        msg[pl.ds(x, edge, stride=ROWS), :] = part
    row = jnp.zeros((edge, LANES), jnp.float32)
    for b in range(count):
        for q in range(2):
            for x, rate in enumerate((rates[b, q, 0], rates[b, q, closed], rates[b, q, normal])):
                row = jnp.where(lane == (2 * b + q) * edge + x, rate, row)
    msg[pl.ds(4, edge, stride=ROWS), :] = row


def local_kernel(
    near_in, solved_in, inverses_in,
    base, pick, flags, edges,
    near, table, solved, inverses, work, other, sems,
):
    count, edge = inverses.shape[0], inverses.shape[3]
    tiles = edge // 4
    size = tiles * edge
    slots = near.shape[2]
    copies = [
        pltpu.make_async_copy(source, target, sems.at[x])
        for x, (source, target) in enumerate(
            (
                (near_in, near),
                (near_in, table),
                (solved_in, solved),
                (inverses_in, inverses),
            )
        )
    ]
    for copy in copies:
        copy.start()
    for copy in copies[:2]:
        copy.wait()
    normal = normal_of(near, 0)
    closed = 3 - normal
    up = near[normal, 1, 0] >= 0
    touch = up | (near[normal, 0, 0] >= 0)

    lane = lane_of((8, LANES))
    back = jnp.broadcast_to(table[0, 0:1, :], (8, slots))
    back = jnp.concatenate([back] * (LANES // slots), 1)
    pointer = jnp.where(back >= 0, back, lane & (slots - 1))
    place = jnp.where(back >= 0, 1, 0)

    def pull(values, index):
        return jnp.take_along_axis(values, index, axis=1, mode="promise_in_bounds")

    reach = 1
    while reach < edge:
        place = place + pull(place, pointer)
        pointer = pull(pointer, pointer)
        reach *= 2
    chain = jnp.where(pointer == pointer[:, 0:1], 0, edge) + place
    goal = pull(chain, (lane & (edge - 1)) * count + lane // (2 * edge)) + 2 * (lane & edge)
    hit = lax.broadcasted_iota(jnp.int32, (LANES, LANES), 0) == goal[0:1]
    pick[...] = hit.astype(jnp.float32).T
    face = jnp.where(((lane & edge) == 0) == up, edge - 1, 0).astype(jnp.float32)
    depth = lax.broadcasted_iota(jnp.int32, (8, LANES), 0)
    angle = jnp.full((8, LANES), lax.axis_index("bricks")).astype(jnp.float32) * (0.5 * math.pi / edge)
    half = jnp.sin(angle)
    flags[...] = jnp.where(
        depth == 0,
        face,
        jnp.where(
            depth == 1,
            jnp.where(touch, 1.0, 0.0),
            jnp.where(depth == 2, jnp.where(normal == 2, 1.0, 0.0), 4.0 * half * half),
        ),
    )

    for copy in copies[2:]:
        copy.wait()
    first_slot = lax.axis_index("bricks") * count
    for b in range(count):
        face = jnp.where(near[normal, 1, first_slot + b] >= 0, edge - 1, 0)
        for q in range(2):
            x = 2 * b + q
            at = size * x
            swap_rows(solved, at, other, 0, edge)
            whole = dot(left_of(inverses[b, closed, q]), right_of(wide(other, 0, edge)))
            for c in range(tiles):
                other[pl.ds(edge * c, edge), :] = whole[:, LANES * c : LANES * (c + 1)]
            swap_rows(other, 0, work, 0, edge)
            base[pl.ds(at, size), :] = work[...]
            row_n = jnp.concatenate([inverses[b, normal, q, pl.ds(face, 1), :]] * 4, 1)
            edges[x, 0] = jnp.broadcast_to(inverses[b, 0, q, :, 0:1], (edge, LANES))
            edges[x, 1] = jnp.broadcast_to(inverses[b, 0, q, :, edge - 1 : edge], (edge, LANES))
            edges[x, 2] = jnp.broadcast_to(row_n, (edge, LANES))


def owner_kernel(recv, pick, flags, const, out):
    edge = const.shape[0]
    turned = const[:, : 3 * edge].astype(jnp.bfloat16)
    lam = const[:, LANES : 2 * LANES]
    v_first = const[:, 2 * LANES : 3 * LANES]
    v_last = const[:, 3 * LANES : 4 * LANES]
    basis = const[:, 4 * LANES : 4 * LANES + 3 * edge].astype(jnp.bfloat16)
    face, touch, normal_2, my_lam = flags[0:1], flags[1:2], flags[2:3], flags[3:4]

    hit = pick[...].astype(jnp.bfloat16)
    data = jnp.concatenate([recv[pl.ds(x, edge, stride=ROWS), :] for x in range(4)], 0).T
    tail = recv[pl.ds(4, edge, stride=ROWS), :]
    tail = jnp.concatenate([tail] + [pltpu.roll(tail, LANES - edge * x, 1) for x in range(1, 4)], 0).T[:16]
    parts = dot(pair_of(jnp.concatenate([tail, data], 0)), jnp.concatenate([hit] * 2, 0))
    rate_0, rate_t, rate_n = parts[0:1], parts[1:2], parts[2:3]
    y0, y1, face_u, face_y = (parts[16 + edge * x : 16 + edge * (x + 1)] for x in range(4))

    lane = lane_of((1, LANES))
    place = lane & (edge - 1)
    first_row = (lane & edge) == 0

    def partner(x):
        return jnp.where(first_row, pltpu.roll(x, LANES - edge, 1), pltpu.roll(x, edge, 1))

    def after(x, s=1):
        return pltpu.roll(x, LANES - s, 1)

    def before(x, s=1):
        return pltpu.roll(x, s, 1)

    damp_0 = 1.0 / (1.0 + lam * rate_0)
    damp_n = 1.0 / (1.0 + lam * rate_n)
    damp_t = 1.0 / (1.0 + my_lam * rate_t)
    other_n = partner(rate_n)
    g = jnp.where(touch > 0.5, 2.0 * rate_n * other_n / (rate_n + other_n), 0.0)
    cross = 2.0 * g * (partner(face_u) - face_u)
    near_c = jnp.sum(damp_0 * v_first * v_first, 0, keepdims=True)
    far_c = jnp.sum(damp_0 * v_first * v_last, 0, keepdims=True)
    end_n = jnp.sum(damp_n * v_first * v_first, 0, keepdims=True)
    open_face = place < edge - 1
    right = jnp.where(open_face, y1 - after(y0), 0.0)
    both = dot(basis, right_of(jnp.concatenate([cross, right], 1)))
    damped = damp_0 * both[:, :LANES]
    pieces = dot(turned, right_of(jnp.concatenate([damped, damp_0 * v_first, damp_0 * v_last], 1)))
    spread, col_0, col_1 = (pieces[:, LANES * x : LANES * (x + 1)] for x in range(3))
    v_face = jnp.where(face < 0.5, v_first, v_last)
    at_first = v_face * jnp.sum(v_first * damped, 0, keepdims=True)
    at_last = v_face * jnp.sum(v_last * damped, 0, keepdims=True)
    right = both[:, LANES:] + jnp.where(open_face, at_last - after(at_first), 0.0)

    inv_rate = 1.0 / rate_0
    diag = jnp.where(open_face, 0.5 * (inv_rate + after(inv_rate)) + near_c + after(near_c), 1.0)
    lower = jnp.where(open_face & (place > 0), -far_c, 0.0)
    upper = jnp.where(place < edge - 2, -after(far_c), 0.0)
    step = 1
    while step < edge:
        inverse = 1.0 / diag
        back = -lower * before(inverse, step)
        fore = -upper * after(inverse, step)
        diag = diag + back * before(upper, step) + fore * after(lower, step)
        right = right + back * before(right, step) + fore * after(right, step)
        lower = back * before(lower, step)
        upper = fore * after(upper, step)
        step *= 2
    flux_up = right / diag
    flux_down = jnp.where(place > 0, before(flux_up), 0.0)

    weight_down = jnp.sum(damp_n * v_face * flux_down, 0, keepdims=True)
    weight_up = jnp.sum(damp_n * v_face * flux_up, 0, keepdims=True)
    ends = face_y + end_n * spread + col_0 * weight_down - col_1 * weight_up
    ends = jnp.where(normal_2 > 0.5, damp_t, 1.0) * ends
    jump = g / (1.0 + g * (end_n + partner(end_n))) * (ends - partner(ends))
    face_out = jnp.where(normal_2 > 0.5, damp_t * spread - jump, damp_t * (spread - jump))
    damp_nt = damp_n * damp_t
    lines = dot(turned, right_of(jnp.concatenate([damp_nt * flux_down, damp_nt * flux_up], 1)))
    packed = jnp.concatenate(
        [lines[:, :LANES], lines[:, LANES:], face_out, jnp.zeros((edge, LANES), jnp.float32)], 0
    )
    reply = dot_lanes(jnp.concatenate([hit] * 2, 1), pair_of(packed))
    kinds = swap_blocks([reply[edge * x : edge * (x + 1)] for x in range(4)])
    for x in range(3):
        out[pl.ds(x, edge, stride=3), :] = kinds[x]


def update_kernel(
    recv, base, edges, flags, calcium, buffer, const,
    calcium_out, buffer_out,
    calcium_next, buffer_next, work, sems,
):
    count, edge = calcium.shape[0], calcium.shape[1]
    tiles = edge // 4
    size = tiles * edge
    swapped = flags[2, 0] < 0.5
    old = jnp.where(flags[2:3] < 0.5, 0.0, 1.0)
    low, high, face_part = (recv[pl.ds(x, edge, stride=3), :] for x in range(3))
    high_s, low_s = parts_of(face_part)
    turn = jnp.concatenate([high_s, low_s, high_s, jnp.zeros_like(high_s)], 0).T.astype(jnp.bfloat16)
    face_wide = dot(turn, const[:, LANES:].astype(jnp.bfloat16))
    lines = dot(const[:edge, : 3 * edge].astype(jnp.bfloat16), right_of(jnp.concatenate([low, high], 1)))
    rows = []
    for e in range(2):
        work[pl.ds(edge * e, edge), :] = lines[:, LANES * e : LANES * (e + 1)]
        rows.append(swap_blocks([work[pl.ds(edge * e + t4, tiles, stride=4), :] for t4 in range(4)]))

    stores = [
        pltpu.make_async_copy(source.at[b], to.at[b], sems.at[2 * b + q])
        for b in range(count)
        for q, (source, to) in enumerate(((calcium_next, calcium_out), (buffer_next, buffer_out)))
    ]
    for b in range(count):
        for q, (ref, now) in enumerate(((calcium_next, calcium), (buffer_next, buffer))):
            x = 2 * b + q
            at = size * x
            col_0, col_1, row_n = edges[x, 0], edges[x, 1], edges[x, 2]
            for c in range(tiles):
                part = slice(LANES * c, LANES * (c + 1))
                ref[b, :, part] = (
                    (base[pl.ds(at + edge * c, edge), :] + old * now[b, :, part])
                    + face_wide[edge * x : edge * (x + 1), part] * row_n
                    + (col_0 * rows[0][x][c : c + 1] - col_1 * rows[1][x][c : c + 1])
                )
            stores[x].start()
    for store in stores:
        store.wait()

    @pl.when(swapped)
    def _():
        swap_inner((calcium_next, buffer_next), edge)
        calcium_next[...] = calcium_next[...] + calcium[...]
        buffer_next[...] = buffer_next[...] + buffer[...]
        for store in stores:
            store.start()
        for store in stores:
            store.wait()


def fast_body(calcium, buffer, fraction, rates, inverses, neighbors, ranks):
    count, edge = calcium.shape[0], calcium.shape[1]
    devices = lax.axis_size("bricks")
    tiles = edge // 4
    size = tiles * edge
    f32 = jnp.float32
    basis, eigen = cosine_basis(edge)
    place = np.arange(edge)
    ends_of = np.zeros((edge, edge))
    ends_of[:, (place % 4) * tiles + place // 4] = basis
    faces_of = np.zeros((edge, LANES))
    faces_of[:, (place % 4) * edge + place // 4] = basis
    pad = lambda x: np.pad(x, ((0, 0), (0, LANES - x.shape[1])))
    message_const = np.concatenate([pad(host_left(ends_of)), host_left(faces_of)], 1)
    lanes_of = lambda x: np.tile(x[:, None], (1, LANES))
    owner_const = np.concatenate(
        [pad(host_left(basis.T))]
        + [lanes_of(x) for x in (eigen, basis[:, 0], basis[:, -1])]
        + [pad(host_left(basis))],
        1,
    )
    expand = np.pad(host_right(np.repeat(basis, edge, 1)), ((0, LANES - 3 * edge), (0, 0)))
    back_const = np.pad(pad(host_left(basis.T)), ((0, LANES - edge), (0, 0)))
    update_const = np.concatenate([back_const, expand], 1)
    smem = pl.BlockSpec(memory_space=pltpu.SMEM)
    vmem = pl.BlockSpec(memory_space=pltpu.VMEM)
    hbm = pl.BlockSpec(memory_space=pltpu.HBM)
    params = pltpu.CompilerParams(vmem_limit_bytes=48 * 2**20)
    const = lambda x: jnp.asarray(x, f32)
    field = jax.ShapeDtypeStruct(calcium.shape, f32)
    tall = jax.ShapeDtypeStruct((2 * count * size, LANES), f32)

    stay = lambda x: pltpu.with_memory_space_constraint(x, pltpu.HBM)
    msg, solved = pl.pallas_call(
        message_kernel,
        out_shape=(jax.ShapeDtypeStruct((devices * ROWS, LANES), f32), tall),
        in_specs=[hbm] * 7,
        out_specs=(vmem, vmem),
        scratch_shapes=[
            pltpu.SMEM(neighbors.shape, jnp.int32),
            pltpu.SMEM((count, 2, 3), f32),
            pltpu.VMEM(calcium.shape, f32),
            pltpu.VMEM(calcium.shape, f32),
            pltpu.VMEM(fraction.shape, f32),
            pltpu.VMEM(inverses.shape, f32),
            pltpu.VMEM(message_const.shape, f32),
            pltpu.SemaphoreType.DMA((7,)),
        ],
        compiler_params=pltpu.CompilerParams(vmem_limit_bytes=48 * 2**20),
        name="message",
    )(*(stay(x) for x in (neighbors, rates.transpose(0, 2, 1), calcium, buffer, fraction, inverses, const(message_const))))
    recv = lax.all_to_all(msg.reshape(devices * ROWS, 1, LANES), "bricks", 0, 0, tiled=True).reshape(devices * ROWS, LANES)
    base, pick, flags, edges = pl.pallas_call(
        local_kernel,
        out_shape=(
            tall,
            jax.ShapeDtypeStruct((LANES, LANES), f32),
            jax.ShapeDtypeStruct((8, LANES), f32),
            jax.ShapeDtypeStruct((2 * count, 3, edge, LANES), f32),
        ),
        in_specs=[hbm] * 3,
        out_specs=(vmem,) * 4,
        scratch_shapes=[
            pltpu.SMEM(neighbors.shape, jnp.int32),
            pltpu.VMEM(neighbors.shape, jnp.int32),
            pltpu.VMEM(tall.shape, f32),
            pltpu.VMEM(inverses.shape, f32),
            pltpu.VMEM((size, LANES), f32),
            pltpu.VMEM((size, LANES), f32),
            pltpu.SemaphoreType.DMA((4,)),
        ],
        compiler_params=pltpu.CompilerParams(vmem_limit_bytes=48 * 2**20),
        cost_estimate=pl.CostEstimate(flops=2 * 10**7, bytes_accessed=4 * 10**6, transcendentals=0),
        name="local_solution",
    )(neighbors, solved, inverses)
    reply = pl.pallas_call(
        owner_kernel,
        out_shape=jax.ShapeDtypeStruct((devices * 3, LANES), f32),
        in_specs=[vmem] * 4,
        out_specs=vmem,
        compiler_params=params,
        name="chain_and_face_solves",
    )(recv, pick, flags, const(owner_const))
    back = lax.all_to_all(reply.reshape(devices * 3, 1, LANES), "bricks", 0, 0, tiled=True)
    return pl.pallas_call(
        update_kernel,
        out_shape=(field, field),
        in_specs=[vmem] * 7,
        out_specs=(hbm, hbm),
        scratch_shapes=[
            pltpu.VMEM(calcium.shape, f32),
            pltpu.VMEM(buffer.shape, f32),
            pltpu.VMEM((2 * edge, LANES), f32),
            pltpu.SemaphoreType.DMA((2 * count,)),
        ],
        compiler_params=params,
        name="rank_three_update",
    )(back.reshape(devices * 3, LANES), base, edges, flags, calcium, buffer, const(update_const))


def body(calcium, buffer, fraction, rates, inverses, neighbors, ranks):
    count, edge = calcium.shape[0], calcium.shape[1]
    devices = lax.axis_size("bricks")
    if edge == GX and devices == edge and count == 2 and 4 * edge == LANES:
        return fast_body(calcium, buffer, fraction, rates, inverses, neighbors, ranks)
    return general_body(calcium, buffer, fraction, rates, inverses, neighbors, ranks)


def solution(mesh):
    in_specs = (
        P("bricks", None, None),
        P("bricks", None, None),
        P("bricks", None, None),
        P("bricks", None, None),
        P("bricks", None, None, None, None),
        P(),
        P(),
    )
    out_specs = (P("bricks", None, None), P("bricks", None, None))
    return jax.shard_map(body, mesh=mesh, in_specs=in_specs, out_specs=out_specs, check_vma=False)
```

```python
from functools import partial
import math

import jax
import jax.numpy as jnp
import numpy as np
from jax import lax
from jax.experimental import pallas as pl
from jax.experimental.pallas import tpu as pltpu
from jax.sharding import PartitionSpec as P

GX = 32


KON = 0.5
KOFF = 0.3
BTOT = 2.0
INFLUX = 0.1


def fetch(table, index):
    rows = jnp.take(table, jnp.maximum(index, 0), axis=0)
    has = (index >= 0).reshape((-1,) + (1,) * (rows.ndim - 1))
    return jnp.where(has, rows, jnp.zeros_like(rows))


def lookup(planes, before, after):
    sides = []
    for d in range(3):
        lower = fetch(planes[:, d, 1], before[d])
        upper = fetch(planes[:, d, 0], after[d])
        sides.append(jnp.stack([lower, upper], 1))
    return jnp.stack(sides, 1)


def coupling(rate_all, neighbors):
    per_dim = []
    for d in range(3):
        mine = rate_all[:, d]
        sides = []
        for side in range(2):
            other = fetch(mine, neighbors[d, side])
            has = (neighbors[d, side] >= 0)[:, None]
            sides.append(jnp.where(has, 2.0 * mine * other / (mine + other), jnp.zeros_like(mine)))
        per_dim.append(jnp.stack(sides, 1))
    return jnp.stack(per_dim, 1)


def end_planes(field):
    count, edge = (field.shape[0], field.shape[2])
    per_dim = []
    for d in range(3):
        first = lax.index_in_dim(field, 0, 2 + d, False).reshape(count, 2, edge * edge)
        last = lax.index_in_dim(field, edge - 1, 2 + d, False).reshape(count, 2, edge * edge)
        per_dim.append(jnp.stack([first, last], 1))
    return jnp.stack(per_dim, 1)


def operator(field, d, rate, glow, gup, hlow, hup):
    axis = 2 + d
    edge = field.shape[axis]
    plane_shape = lax.index_in_dim(field, 0, axis, False).shape
    lower_face = jnp.expand_dims(hlow.reshape(plane_shape), axis)
    upper_face = jnp.expand_dims(hup.reshape(plane_shape), axis)
    upper = jnp.concatenate([lax.slice_in_dim(field, 1, edge, axis=axis), upper_face], axis)
    lower = jnp.concatenate([lower_face, lax.slice_in_dim(field, 0, edge - 1, axis=axis)], axis)
    place = lax.broadcasted_iota(jnp.int32, field.shape, axis)
    inner = rate[:, :, None, None, None]
    c_up = jnp.where(place == edge - 1, gup[:, :, None, None, None], inner)
    c_down = jnp.where(place == 0, glow[:, :, None, None, None], inner)
    return c_up * (upper - field) + c_down * (lower - field)


def reaction(field, fraction):
    count, edge = (field.shape[0], field.shape[2])
    alpha = fraction.reshape(count, edge, edge, edge)
    calc, bound = (field[:, 0], field[:, 1])
    bind = KON * calc * (BTOT - bound) - KOFF * bound
    return jnp.stack([-bind + INFLUX * (1.0 - alpha) / alpha, bind], 1)


def apply_inverse(block, field, d):
    forms = ["psab,psbjk->psajk", "psab,psibk->psiak", "psab,psijb->psija"]
    return jnp.einsum(forms[d], block, field, precision=lax.Precision.HIGHEST)


def line_ends(field, d):
    count, edge = (field.shape[0], field.shape[2])
    first = lax.index_in_dim(field, 0, 2 + d, False).reshape(count, 2, edge * edge)
    last = lax.index_in_dim(field, edge - 1, 2 + d, False).reshape(count, 2, edge * edge)
    return jnp.stack([first, last], 2)


def block_terms(glow, gup, corner):
    v_first, v_last, w_first, w_last = (
        corner[..., 0],
        corner[..., 1],
        corner[..., 2],
        corner[..., 3],
    )
    a00 = 1.0 + glow * v_first
    a01 = gup * w_first
    a10 = glow * v_last
    a11 = 1.0 + gup * w_last
    lq0 = -glow * v_first
    lq1 = -glow * v_last
    up0 = -gup * w_first
    up1 = -gup * w_last
    return (a00, a01, a10, a11, lq0, lq1, up0, up1)


def chain_order(before, rank):
    slots = jnp.arange(before.shape[0], dtype=jnp.int32)
    pointer = jnp.where(before >= 0, before, slots)
    for step in range(GX.bit_length()):
        pointer = jnp.take(pointer, pointer, axis=0)
    sort_key = pointer * GX + rank
    order = jnp.argsort(sort_key)
    inverse_order = jnp.argsort(order)
    return (order, inverse_order)


def shift_down(values):
    return jnp.concatenate([jnp.zeros_like(values[:1]), values[:-1]], 0)


def shift_up(values):
    return jnp.concatenate([values[1:], jnp.zeros_like(values[:1])], 0)


def compose_maps(first_map, second_map):
    e00, e01, e10, e11 = first_map
    l00, l01, l10, l11 = second_map
    n00 = l00 * e00 + l01 * e10
    n01 = l00 * e01 + l01 * e11
    n10 = l10 * e00 + l11 * e10
    n11 = l10 * e01 + l11 * e11
    scale = jnp.abs(n00) + jnp.abs(n01) + jnp.abs(n10) + jnp.abs(n11)
    return (n00 / scale, n01 / scale, n10 / scale, n11 / scale)


def compose_affine(first_map, second_map):
    first_q, first_p = first_map
    second_q, second_p = second_map
    return (first_q * second_q, second_p + second_q * first_p)


def sorted_solve(glow, gup, corner, before, after, order, inverse_order, ends):
    glow = jnp.take(glow, order, axis=0)
    gup = jnp.take(gup, order, axis=0)
    corner = jnp.take(corner, order, axis=0)
    has_b = jnp.take(before, order, axis=0) >= 0
    has_a = jnp.take(after, order, axis=0) >= 0
    arranged = jnp.take(ends, order, axis=0)
    y0 = arranged[:, :, 0]
    y1 = arranged[:, :, 1]
    a00, a01, a10, a11, lq0, lq1, up0, up1 = block_terms(glow, gup, corner)
    maps = (
        -(lq0 * up1 - lq1 * up0),
        a00 * up1 - a10 * up0,
        -(lq0 * a11 - a01 * lq1),
        a00 * a11 - a01 * a10,
    )
    summed = lax.associative_scan(compose_maps, maps, axis=0)
    f1_prev = summed[1] / summed[3]
    fq = shift_down(f1_prev)
    b00 = a00 - lq0 * fq
    b10 = a10 - lq1 * fq
    det = b00 * a11 - a01 * b10
    f0 = (a11 * up0 - a01 * up1) / det
    f1 = (b00 * up1 - b10 * up0) / det
    slope = (-(b00 * lq1 - b10 * lq0) / det)[:, :, None]
    offset = (b00[:, :, None] * y1 - b10[:, :, None] * y0) / det[:, :, None]
    e1 = lax.associative_scan(compose_affine, (slope, offset), axis=0)[1]
    eq = shift_down(e1)
    e0 = (
        a11[:, :, None] * y0 - a01[:, :, None] * y1 - (a11 * lq0 - a01 * lq1)[:, :, None] * eq
    ) / det[:, :, None]
    zp = lax.associative_scan(compose_affine, (-f0[:, :, None], e0), reverse=True, axis=0)[1]
    pn = shift_up(zp)
    zq = e1 - f1[:, :, None] * pn
    low = jnp.where(has_b[:, None, None], zp - shift_down(zq), jnp.zeros_like(zp))
    high = jnp.where(has_a[:, None, None], zq - pn, jnp.zeros_like(zq))
    return jnp.take(jnp.stack([low, high], 2), inverse_order, axis=0)


def correct(local, block, glow, gup, jumps, d):
    axis = 2 + d
    count, edge = (local.shape[0], local.shape[2])
    shape_v = [count, 2, 1, 1, 1]
    shape_v[axis] = edge
    first_col = block[..., 0].reshape(shape_v)
    last_col = block[..., edge - 1].reshape(shape_v)
    plane_shape = lax.index_in_dim(local, 0, axis, False).shape
    low = jnp.expand_dims(jumps[:, :, 0].reshape(plane_shape), axis)
    high = jnp.expand_dims(jumps[:, :, 1].reshape(plane_shape), axis)
    return (
        local
        - glow[:, :, None, None, None] * low * first_col
        - gup[:, :, None, None, None] * high * last_col
    )


def general_body(calcium, buffer, fraction, rates, inverses, neighbors, ranks):
    count, edge = (calcium.shape[0], calcium.shape[1])
    devices = lax.axis_size("bricks")
    square = edge * edge
    per_device = square // devices
    start = lax.axis_index("bricks") * count
    corners = jnp.stack(
        [
            inverses[..., 0, 0],
            inverses[..., edge - 1, 0],
            inverses[..., 0, edge - 1],
            inverses[..., edge - 1, edge - 1],
        ],
        -1,
    )
    rate_all, corner_all = (
        lax.all_gather(rates, "bricks", axis=0, tiled=True),
        lax.all_gather(corners, "bricks", axis=0, tiled=True),
    )
    couple_all = coupling(rate_all, neighbors)
    couple = lax.dynamic_slice_in_dim(couple_all, start, count, 0)
    field = jnp.stack([calcium, buffer], 1).reshape(count, 2, edge, edge, edge)
    planes = end_planes(field).reshape(count, 3, 2, 2, devices, per_device)
    lined = lookup(
        lax.all_to_all(planes, "bricks", split_axis=4, concat_axis=0, tiled=True),
        neighbors[:, 0],
        neighbors[:, 1],
    )
    halos = lax.all_to_all(lined, "bricks", split_axis=0, concat_axis=4, tiled=True).reshape(
        count, 3, 2, 2, square
    )
    lams = [
        operator(
            field, d, rates[:, d], couple[:, d, 0], couple[:, d, 1], halos[:, d, 0], halos[:, d, 1]
        )
        for d in range(3)
    ]
    rhs = field + lams[0] + 2.0 * lams[1] + 2.0 * lams[2] + reaction(field, fraction)

    def solve(right, d):
        block = inverses[:, d]
        local = apply_inverse(block, right, d)
        ends = line_ends(local, d).reshape(count, 2, 2, devices, per_device)
        order, inverse_order = chain_order(neighbors[d, 0], ranks[d])
        chain_fn = partial(
            sorted_solve,
            couple_all[:, d, 0],
            couple_all[:, d, 1],
            corner_all[:, d],
            neighbors[d, 0],
            neighbors[d, 1],
            order,
            inverse_order,
        )
        lined_jumps = chain_fn(
            lax.all_to_all(ends, "bricks", split_axis=3, concat_axis=0, tiled=True)[:, :, :, 0]
        )[:, :, :, None]
        jumps = lax.all_to_all(
            lined_jumps, "bricks", split_axis=0, concat_axis=3, tiled=True
        ).reshape(count, 2, 2, square)
        return correct(local, block, couple[:, d, 0], couple[:, d, 1], jumps, d)

    first = solve(rhs, 0)
    second = solve(first - lams[1], 1)
    third = solve(second - lams[2], 2)
    result = third.reshape(count, 2, edge, edge * edge)
    return (result[:, 0], result[:, 1])


LANES = 128


ROWS = 5


def cosine_basis(edge):
    wave = np.arange(edge)[:, None]
    place = np.arange(edge)[None, :]
    basis = np.sqrt(2.0 / edge) * np.cos(np.pi * wave * (place + 0.5) / edge)
    basis[0] = math.sqrt(1.0 / edge)
    eigen = 2.0 - 2.0 * np.cos(np.pi * np.arange(edge) / edge)
    return basis, eigen


def parts_of(x):
    high = x.astype(jnp.bfloat16)
    rest = x - high.astype(jnp.float32)
    middle = rest.astype(jnp.bfloat16)
    return high, middle, (rest - middle.astype(jnp.float32)).astype(jnp.bfloat16)


LEFT = (0, 0, 0, 1, 1, 2)
RIGHT = (0, 1, 2, 0, 1, 0)


def left_of(x):
    parts = [part.astype(jnp.float32) for part in parts_of(x)]
    return jnp.concatenate([parts[p] for p in LEFT], 1).astype(jnp.bfloat16)


def right_of(x, axis=0):
    parts = parts_of(x)
    return jnp.concatenate([parts[p] for p in RIGHT], axis)


def exact_of(x):
    return jnp.concatenate(parts_of(x), 1)


def dot(a, b):
    return jnp.dot(a, b, preferred_element_type=jnp.float32)


def dot_lanes(a, b):
    return lax.dot_general(a, b, (((1,), (1,)), ((), ())), preferred_element_type=jnp.float32)


def host_parts(x):
    parts = []
    for _ in range(3):
        parts.append(x.astype(jnp.bfloat16).astype(np.float64))
        x = x - parts[-1]
    return parts


def host_left(x):
    parts = host_parts(x)
    return np.concatenate([parts[p] for p in LEFT], 1)


def host_right(x):
    parts = host_parts(x)
    return np.concatenate([parts[p] for p in RIGHT], 0)


def lane_of(shape):
    return lax.broadcasted_iota(jnp.int32, shape, len(shape) - 1)


def swap_blocks(four):
    x0, x1, x2, x3 = four
    lane = lane_of(x0.shape)
    low = (lane & 64) == 0
    y0, y2 = jnp.where(low, x0, pltpu.roll(x2, 64, 1)), jnp.where(low, pltpu.roll(x0, 64, 1), x2)
    y1, y3 = jnp.where(low, x1, pltpu.roll(x3, 64, 1)), jnp.where(low, pltpu.roll(x1, 64, 1), x3)
    even = (lane & 32) == 0
    z0, z1 = jnp.where(even, y0, pltpu.roll(y1, 32, 1)), jnp.where(even, pltpu.roll(y0, 96, 1), y1)
    z2, z3 = jnp.where(even, y2, pltpu.roll(y3, 32, 1)), jnp.where(even, pltpu.roll(y2, 96, 1), y3)
    return [z0, z1, z2, z3]


def swap_rows(source, base, scratch, at, edge):
    tiles = edge // 4
    for c in range(tiles):
        rows = [source[pl.ds(base + edge * c + g, tiles, stride=4), :] for g in range(4)]
        for t4, row in enumerate(swap_blocks(rows)):
            scratch[pl.ds(at + 4 * c + t4, tiles, stride=edge), :] = row


def tile_rows(x, edge):
    tiles = edge // 4
    return jnp.concatenate([x[:, LANES * c : LANES * (c + 1)] for c in range(tiles)], 0)


def wide(ref, at, edge):
    tiles = edge // 4
    return jnp.concatenate([ref[pl.ds(at + edge * c, edge), :] for c in range(tiles)], 1)


def swap_inner(refs, edge):
    tiles = edge // 4
    fields = [(ref, b) for ref in refs for b in range(ref.shape[0])]
    whole = [
        exact_of(jnp.concatenate([ref[b, :, LANES * c : LANES * (c + 1)] for ref, b in fields], 0))
        for c in range(tiles)
    ]
    row = lax.broadcasted_iota(jnp.int32, (LANES, LANES), 0)
    lane = lane_of((LANES, LANES))
    for to in range(tiles):
        total = jnp.zeros((len(fields) * edge, LANES), jnp.float32)
        for c in range(tiles):
            hit = ((row & (edge - 1)) == 4 * to + lane // edge) & ((lane & (edge - 1)) == 4 * c + row // edge)
            hit = hit.astype(jnp.float32).astype(jnp.bfloat16)
            total = total + dot(whole[c], jnp.concatenate([hit] * 3, 0))
        for f, (ref, b) in enumerate(fields):
            ref[b, :, LANES * to : LANES * (to + 1)] = total[edge * f : edge * (f + 1)]


def normal_of(near, slot):
    along_j = (near[1, 0, slot] >= 0) | (near[1, 1, slot] >= 0)
    return jnp.where(along_j, 1, 2)


def message_kernel(
    near_in, rates_in, calcium_in, buffer_in, fraction_in, inverses_in, const_in,
    msg, solved,
    near, rates, calcium, buffer, fraction, inverses, const, sems,
):
    count, edge = calcium.shape[0], calcium.shape[1]
    tiles = edge // 4
    size = tiles * edge
    copies = [
        pltpu.make_async_copy(source, target, sems.at[x])
        for x, (source, target) in enumerate(
            (
                (near_in, near),
                (rates_in, rates),
                (calcium_in, calcium),
                (buffer_in, buffer),
                (fraction_in, fraction),
                (inverses_in, inverses),
                (const_in, const),
            )
        )
    ]
    for copy in copies:
        copy.start()
    first_slot = lax.axis_index("bricks") * count
    for copy in copies:
        copy.wait()
    normal = normal_of(near, first_slot)
    closed = 3 - normal

    @pl.when(normal == 1)
    def _():
        swap_inner((calcium, buffer, fraction), edge)

    lane = lane_of((edge, LANES))
    inner = lane & (edge - 1)
    square_row = lax.broadcasted_iota(jnp.int32, (LANES, LANES), 0)
    square_lane = lane_of((LANES, LANES))
    on_block = (square_row // edge) == (square_lane // edge)
    faces_u, faces_y, ends0, ends1 = [], [], [], []
    for b in range(count):
        face = jnp.where(near[normal, 1, first_slot + b] >= 0, edge - 1, 0)
        calc = [calcium[b, :, LANES * c : LANES * (c + 1)] for c in range(tiles)]
        bound = [buffer[b, :, LANES * c : LANES * (c + 1)] for c in range(tiles)]
        alpha = [fraction[b, :, LANES * c : LANES * (c + 1)] for c in range(tiles)]
        bind = [KON * x * (BTOT - y) - KOFF * y for x, y in zip(calc, bound)]
        source_calc = [INFLUX / a - (w + INFLUX) for w, a in zip(bind, alpha)]
        for q, (u, source) in enumerate(((calc, source_calc), (bound, bind))):
            at = size * (2 * b + q)
            rate_t, rate_n = 2.0 * rates[b, q, closed], 2.0 * rates[b, q, normal]
            ahead = [pltpu.roll(x, LANES - edge, 1) for x in u]
            behind = [pltpu.roll(x, edge, 1) for x in u]
            f = []
            for c in range(tiles):
                x = u[c]
                next_t = jnp.where(lane < LANES - edge, ahead[c], ahead[c + 1] if c + 1 < tiles else x)
                last_t = jnp.where(lane >= edge, behind[c], behind[c - 1] if c else x)
                next_n = jnp.where(inner == edge - 1, x, pltpu.roll(x, LANES - 1, 1))
                last_n = jnp.where(inner == 0, x, pltpu.roll(x, 1, 1))
                twice = x + x
                along = rate_t * (next_t + last_t - twice) + rate_n * (next_n + last_n - twice)
                f.append(twice + along + source[c])
            g = dot(left_of(inverses[b, 0, q]), right_of(jnp.concatenate(f, 1)))
            ends0.append(jnp.concatenate([g[0:1, LANES * c : LANES * (c + 1)] for c in range(tiles)], 0))
            ends1.append(jnp.concatenate([g[edge - 1 : edge, LANES * c : LANES * (c + 1)] for c in range(tiles)], 0))
            w = jnp.concatenate([g[:, LANES * c : LANES * (c + 1)] - 2.0 * u[c] for c in range(tiles)], 0)
            sides = [
                jnp.where(on_block, jnp.concatenate([jnp.concatenate([x.astype(jnp.float32)] * 4, 1)] * 4, 0), 0.0)
                for x in parts_of(inverses[b, normal, q])
            ]
            sides = [x.astype(jnp.bfloat16) for x in sides]
            y = dot(right_of(w, 1), jnp.concatenate([sides[p] for p in LEFT], 0))
            solved[pl.ds(at, size), :] = y
            face_u = jnp.zeros((edge, LANES), jnp.float32)
            face_y = jnp.zeros((edge, LANES), jnp.float32)
            for c in range(tiles):
                shift = (c - face) & (LANES - 1)
                face_u = jnp.where(inner == c, pltpu.roll(u[c], shift, 1), face_u)
                face_y = jnp.where(inner == c, pltpu.roll(y[edge * c : edge * (c + 1)], shift, 1), face_y)
            faces_u.append(face_u)
            faces_y.append(face_y)

    stack = jnp.concatenate(swap_blocks(ends0) + swap_blocks(ends1), 0)
    ends_of = const[:, : 6 * edge]
    faces_of = const[:, 2 * LANES :]
    both = dot(ends_of, right_of(jnp.concatenate([stack[:edge], stack[edge:]], 1)))
    part_u = dot_lanes(faces_of, right_of(jnp.concatenate(faces_u, 0), 1))
    part_y = dot_lanes(faces_of, right_of(jnp.concatenate(faces_y, 0), 1))
    fields = swap_blocks([both[:, :LANES], both[:, LANES:], part_u, part_y])
    for x, part in enumerate(fields):
        msg[pl.ds(x, edge, stride=ROWS), :] = part
    row = jnp.zeros((edge, LANES), jnp.float32)
    for b in range(count):
        for q in range(2):
            for x, rate in enumerate((rates[b, q, 0], rates[b, q, closed], rates[b, q, normal])):
                row = jnp.where(lane == (2 * b + q) * edge + x, rate, row)
    msg[pl.ds(4, edge, stride=ROWS), :] = row


def local_kernel(
    near_in, solved_in, inverses_in,
    base, pick, flags, edges,
    near, table, solved, inverses, work, other, sems,
):
    count, edge = inverses.shape[0], inverses.shape[3]
    tiles = edge // 4
    size = tiles * edge
    slots = near.shape[2]
    copies = [
        pltpu.make_async_copy(source, target, sems.at[x])
        for x, (source, target) in enumerate(
            (
                (near_in, near),
                (near_in, table),
                (solved_in, solved),
                (inverses_in, inverses),
            )
        )
    ]
    for copy in copies:
        copy.start()
    for copy in copies[:2]:
        copy.wait()
    normal = normal_of(near, 0)
    closed = 3 - normal
    up = near[normal, 1, 0] >= 0
    touch = up | (near[normal, 0, 0] >= 0)

    lane = lane_of((8, LANES))
    back = jnp.broadcast_to(table[0, 0:1, :], (8, slots))
    back = jnp.concatenate([back] * (LANES // slots), 1)
    pointer = jnp.where(back >= 0, back, lane & (slots - 1))
    place = jnp.where(back >= 0, 1, 0)

    def pull(values, index):
        return jnp.take_along_axis(values, index, axis=1, mode="promise_in_bounds")

    reach = 1
    while reach < edge:
        place = place + pull(place, pointer)
        pointer = pull(pointer, pointer)
        reach *= 2
    chain = jnp.where(pointer == pointer[:, 0:1], 0, edge) + place
    goal = pull(chain, (lane & (edge - 1)) * count + lane // (2 * edge)) + 2 * (lane & edge)
    hit = lax.broadcasted_iota(jnp.int32, (LANES, LANES), 0) == goal[0:1]
    pick[...] = hit.astype(jnp.float32).T
    face = jnp.where(((lane & edge) == 0) == up, edge - 1, 0).astype(jnp.float32)
    depth = lax.broadcasted_iota(jnp.int32, (8, LANES), 0)
    angle = jnp.full((8, LANES), lax.axis_index("bricks")).astype(jnp.float32) * (0.5 * math.pi / edge)
    half = jnp.sin(angle)
    flags[...] = jnp.where(
        depth == 0,
        face,
        jnp.where(
            depth == 1,
            jnp.where(touch, 1.0, 0.0),
            jnp.where(depth == 2, jnp.where(normal == 2, 1.0, 0.0), 4.0 * half * half),
        ),
    )

    for copy in copies[2:]:
        copy.wait()
    first_slot = lax.axis_index("bricks") * count
    for b in range(count):
        face = jnp.where(near[normal, 1, first_slot + b] >= 0, edge - 1, 0)
        for q in range(2):
            x = 2 * b + q
            at = size * x
            swap_rows(solved, at, other, 0, edge)
            whole = dot(left_of(inverses[b, closed, q]), right_of(wide(other, 0, edge)))
            for c in range(tiles):
                other[pl.ds(edge * c, edge), :] = whole[:, LANES * c : LANES * (c + 1)]
            swap_rows(other, 0, work, 0, edge)
            base[pl.ds(at, size), :] = work[...]
            row_n = jnp.concatenate([inverses[b, normal, q, pl.ds(face, 1), :]] * 4, 1)
            edges[x, 0] = jnp.broadcast_to(inverses[b, 0, q, :, 0:1], (edge, LANES))
            edges[x, 1] = jnp.broadcast_to(inverses[b, 0, q, :, edge - 1 : edge], (edge, LANES))
            edges[x, 2] = jnp.broadcast_to(row_n, (edge, LANES))


def owner_kernel(recv, pick, flags, const, out):
    edge = const.shape[0]
    turned = const[:, : 6 * edge].astype(jnp.bfloat16)
    basis = const[:, 2 * LANES : 2 * LANES + 6 * edge].astype(jnp.bfloat16)
    lam, v_first, v_last = (const[:, LANES * x : LANES * (x + 1)] for x in (4, 5, 6))
    face, touch, normal_2, my_lam = flags[0:1], flags[1:2], flags[2:3], flags[3:4]

    hit = pick[...].astype(jnp.bfloat16)
    data = jnp.concatenate([recv[pl.ds(x, edge, stride=ROWS), :] for x in range(4)], 0).T
    tail = recv[pl.ds(4, edge, stride=ROWS), :]
    tail = jnp.concatenate([tail] + [pltpu.roll(tail, LANES - edge * x, 1) for x in range(1, 4)], 0).T[:16]
    parts = dot(exact_of(jnp.concatenate([tail, data], 0)), jnp.concatenate([hit] * 3, 0))
    rate_0, rate_t, rate_n = parts[0:1], parts[1:2], parts[2:3]
    y0, y1, face_u, face_y = (parts[16 + edge * x : 16 + edge * (x + 1)] for x in range(4))

    lane = lane_of((1, LANES))
    place = lane & (edge - 1)
    first_row = (lane & edge) == 0

    def partner(x):
        return jnp.where(first_row, pltpu.roll(x, LANES - edge, 1), pltpu.roll(x, edge, 1))

    def after(x, s=1):
        return pltpu.roll(x, LANES - s, 1)

    def before(x, s=1):
        return pltpu.roll(x, s, 1)

    damp_0 = 1.0 / (1.0 + lam * rate_0)
    damp_n = 1.0 / (1.0 + lam * rate_n)
    damp_t = 1.0 / (1.0 + my_lam * rate_t)
    other_n = partner(rate_n)
    g = jnp.where(touch > 0.5, 2.0 * rate_n * other_n / (rate_n + other_n), 0.0)
    cross = 2.0 * g * (partner(face_u) - face_u)
    near_c = jnp.sum(damp_0 * v_first * v_first, 0, keepdims=True)
    far_c = jnp.sum(damp_0 * v_first * v_last, 0, keepdims=True)
    end_n = jnp.sum(damp_n * v_first * v_first, 0, keepdims=True)
    open_face = place < edge - 1
    right = jnp.where(open_face, y1 - after(y0), 0.0)
    both = dot(basis, right_of(jnp.concatenate([cross, right], 1)))
    damped = damp_0 * both[:, :LANES]
    pieces = dot(turned, right_of(jnp.concatenate([damped, damp_0 * v_first, damp_0 * v_last], 1)))
    spread, col_0, col_1 = (pieces[:, LANES * x : LANES * (x + 1)] for x in range(3))
    v_face = jnp.where(face < 0.5, v_first, v_last)
    at_first = v_face * jnp.sum(v_first * damped, 0, keepdims=True)
    at_last = v_face * jnp.sum(v_last * damped, 0, keepdims=True)
    right = both[:, LANES:] + jnp.where(open_face, at_last - after(at_first), 0.0)

    inv_rate = 1.0 / rate_0
    diag = jnp.where(open_face, 0.5 * (inv_rate + after(inv_rate)) + near_c + after(near_c), 1.0)
    lower = jnp.where(open_face & (place > 0), -far_c, 0.0)
    upper = jnp.where(place < edge - 2, -after(far_c), 0.0)
    step = 1
    while step < edge:
        inverse = 1.0 / diag
        back = -lower * before(inverse, step)
        fore = -upper * after(inverse, step)
        diag = diag + back * before(upper, step) + fore * after(lower, step)
        right = right + back * before(right, step) + fore * after(right, step)
        lower = back * before(lower, step)
        upper = fore * after(upper, step)
        step *= 2
    flux_up = right / diag
    flux_down = jnp.where(place > 0, before(flux_up), 0.0)

    weight_down = jnp.sum(damp_n * v_face * flux_down, 0, keepdims=True)
    weight_up = jnp.sum(damp_n * v_face * flux_up, 0, keepdims=True)
    ends = face_y + end_n * spread + col_0 * weight_down - col_1 * weight_up
    ends = jnp.where(normal_2 > 0.5, damp_t, 1.0) * ends
    jump = g / (1.0 + g * (end_n + partner(end_n))) * (ends - partner(ends))
    face_out = jnp.where(normal_2 > 0.5, damp_t * spread - jump, damp_t * (spread - jump))
    damp_nt = damp_n * damp_t
    lines = dot(turned, right_of(jnp.concatenate([damp_nt * flux_down, damp_nt * flux_up], 1)))
    packed = jnp.concatenate(
        [lines[:, :LANES], lines[:, LANES:], face_out, jnp.zeros((edge, LANES), jnp.float32)], 0
    )
    reply = dot_lanes(jnp.concatenate([hit] * 3, 1), exact_of(packed))
    kinds = swap_blocks([reply[edge * x : edge * (x + 1)] for x in range(4)])
    for x in range(3):
        out[pl.ds(x, edge, stride=3), :] = kinds[x]


def update_kernel(
    recv, base, edges, flags, calcium, buffer, const,
    calcium_out, buffer_out,
    calcium_next, buffer_next, work, sems,
):
    count, edge = calcium.shape[0], calcium.shape[1]
    tiles = edge // 4
    size = tiles * edge
    swapped = flags[2, 0] < 0.5
    old = jnp.where(flags[2:3] < 0.5, 0.0, 1.0)
    low, high, face_part = (recv[pl.ds(x, edge, stride=3), :] for x in range(3))
    parts = [part.astype(jnp.float32) for part in parts_of(face_part)]
    turn = jnp.concatenate([parts[p] for p in LEFT] + [jnp.zeros_like(parts[0])] * 2, 0)
    turn = turn.T[:, : 6 * edge].astype(jnp.bfloat16)
    face_wide = dot(turn, const[:, 2 * LANES :])
    lines = dot(const[:edge, : 6 * edge], right_of(jnp.concatenate([low, high], 1)))
    rows = []
    for e in range(2):
        work[pl.ds(edge * e, edge), :] = lines[:, LANES * e : LANES * (e + 1)]
        rows.append(swap_blocks([work[pl.ds(edge * e + t4, tiles, stride=4), :] for t4 in range(4)]))

    stores = [
        pltpu.make_async_copy(source.at[b], to.at[b], sems.at[2 * b + q])
        for b in range(count)
        for q, (source, to) in enumerate(((calcium_next, calcium_out), (buffer_next, buffer_out)))
    ]
    for b in range(count):
        for q, (ref, now) in enumerate(((calcium_next, calcium), (buffer_next, buffer))):
            x = 2 * b + q
            at = size * x
            col_0, col_1, row_n = edges[x, 0], edges[x, 1], edges[x, 2]
            for c in range(tiles):
                part = slice(LANES * c, LANES * (c + 1))
                ref[b, :, part] = (
                    (base[pl.ds(at + edge * c, edge), :] + old * now[b, :, part])
                    + face_wide[edge * x : edge * (x + 1), part] * row_n
                    + (col_0 * rows[0][x][c : c + 1] - col_1 * rows[1][x][c : c + 1])
                )
            stores[x].start()
    for store in stores:
        store.wait()

    @pl.when(swapped)
    def _():
        swap_inner((calcium_next, buffer_next), edge)
        calcium_next[...] = calcium_next[...] + calcium[...]
        buffer_next[...] = buffer_next[...] + buffer[...]
        for store in stores:
            store.start()
        for store in stores:
            store.wait()


def fast_body(calcium, buffer, fraction, rates, inverses, neighbors, ranks):
    count, edge = calcium.shape[0], calcium.shape[1]
    devices = lax.axis_size("bricks")
    tiles = edge // 4
    size = tiles * edge
    f32 = jnp.float32
    basis, eigen = cosine_basis(edge)
    place = np.arange(edge)
    ends_of = np.zeros((edge, edge))
    ends_of[:, (place % 4) * tiles + place // 4] = basis
    faces_of = np.zeros((edge, LANES))
    faces_of[:, (place % 4) * edge + place // 4] = basis
    pad = lambda x: np.pad(x, ((0, 0), (0, 2 * LANES - x.shape[1])))
    message_const = np.concatenate([pad(host_left(ends_of)), host_left(faces_of)], 1)
    lanes_of = lambda x: np.tile(x[:, None], (1, LANES))
    owner_const = np.concatenate(
        [pad(host_left(basis.T)), pad(host_left(basis))]
        + [lanes_of(x) for x in (eigen, basis[:, 0], basis[:, -1])],
        1,
    )
    expand = host_right(np.repeat(basis, edge, 1))
    back_const = np.pad(pad(host_left(basis.T)), ((0, 5 * edge), (0, 0)))
    update_const = np.concatenate([back_const, expand], 1)
    smem = pl.BlockSpec(memory_space=pltpu.SMEM)
    vmem = pl.BlockSpec(memory_space=pltpu.VMEM)
    hbm = pl.BlockSpec(memory_space=pltpu.HBM)
    params = pltpu.CompilerParams(vmem_limit_bytes=48 * 2**20)
    const = lambda x: jnp.asarray(x, f32)
    field = jax.ShapeDtypeStruct(calcium.shape, f32)
    tall = jax.ShapeDtypeStruct((2 * count * size, LANES), f32)

    stay = lambda x: pltpu.with_memory_space_constraint(x, pltpu.HBM)
    msg, solved = pl.pallas_call(
        message_kernel,
        out_shape=(jax.ShapeDtypeStruct((devices * ROWS, LANES), f32), tall),
        in_specs=[hbm] * 7,
        out_specs=(vmem, vmem),
        scratch_shapes=[
            pltpu.SMEM(neighbors.shape, jnp.int32),
            pltpu.SMEM((count, 2, 3), f32),
            pltpu.VMEM(calcium.shape, f32),
            pltpu.VMEM(calcium.shape, f32),
            pltpu.VMEM(fraction.shape, f32),
            pltpu.VMEM(inverses.shape, f32),
            pltpu.VMEM(message_const.shape, jnp.bfloat16),
            pltpu.SemaphoreType.DMA((7,)),
        ],
        compiler_params=pltpu.CompilerParams(vmem_limit_bytes=48 * 2**20),
        name="message",
    )(*(stay(x) for x in (neighbors, rates.transpose(0, 2, 1), calcium, buffer, fraction, inverses, jnp.asarray(message_const, jnp.bfloat16))))
    recv = lax.all_to_all(msg.reshape(devices * ROWS, 1, LANES), "bricks", 0, 0, tiled=True).reshape(devices * ROWS, LANES)
    base, pick, flags, edges = pl.pallas_call(
        local_kernel,
        out_shape=(
            tall,
            jax.ShapeDtypeStruct((LANES, LANES), f32),
            jax.ShapeDtypeStruct((8, LANES), f32),
            jax.ShapeDtypeStruct((2 * count, 3, edge, LANES), f32),
        ),
        in_specs=[hbm] * 3,
        out_specs=(vmem,) * 4,
        scratch_shapes=[
            pltpu.SMEM(neighbors.shape, jnp.int32),
            pltpu.VMEM(neighbors.shape, jnp.int32),
            pltpu.VMEM(tall.shape, f32),
            pltpu.VMEM(inverses.shape, f32),
            pltpu.VMEM((size, LANES), f32),
            pltpu.VMEM((size, LANES), f32),
            pltpu.SemaphoreType.DMA((4,)),
        ],
        compiler_params=pltpu.CompilerParams(vmem_limit_bytes=48 * 2**20),
        cost_estimate=pl.CostEstimate(flops=2 * 10**7, bytes_accessed=4 * 10**6, transcendentals=0),
        name="local_solution",
    )(neighbors, solved, inverses)
    reply = pl.pallas_call(
        owner_kernel,
        out_shape=jax.ShapeDtypeStruct((devices * 3, LANES), f32),
        in_specs=[vmem] * 4,
        out_specs=vmem,
        compiler_params=params,
        name="chain_and_face_solves",
    )(recv, pick, flags, const(owner_const))
    back = lax.all_to_all(reply.reshape(devices * 3, 1, LANES), "bricks", 0, 0, tiled=True)
    return pl.pallas_call(
        update_kernel,
        out_shape=(field, field),
        in_specs=[vmem] * 7,
        out_specs=(hbm, hbm),
        scratch_shapes=[
            pltpu.VMEM(calcium.shape, f32),
            pltpu.VMEM(buffer.shape, f32),
            pltpu.VMEM((2 * edge, LANES), f32),
            pltpu.SemaphoreType.DMA((2 * count,)),
        ],
        compiler_params=params,
        name="rank_three_update",
    )(back.reshape(devices * 3, LANES), base, edges, flags, calcium, buffer, jnp.asarray(update_const, jnp.bfloat16))


def body(calcium, buffer, fraction, rates, inverses, neighbors, ranks):
    count, edge = calcium.shape[0], calcium.shape[1]
    devices = lax.axis_size("bricks")
    if edge == GX and devices == edge and count == 2 and 4 * edge == LANES:
        return fast_body(calcium, buffer, fraction, rates, inverses, neighbors, ranks)
    return general_body(calcium, buffer, fraction, rates, inverses, neighbors, ranks)


def solution(mesh):
    in_specs = (
        P("bricks", None, None),
        P("bricks", None, None),
        P("bricks", None, None),
        P("bricks", None, None),
        P("bricks", None, None, None, None),
        P(),
        P(),
    )
    out_specs = (P("bricks", None, None), P("bricks", None, None))
    return jax.shard_map(body, mesh=mesh, in_specs=in_specs, out_specs=out_specs, check_vma=False)
```

```python
from functools import partial
import math

import jax
import jax.numpy as jnp
import numpy as np
from jax import lax
from jax.experimental import pallas as pl
from jax.experimental.pallas import tpu as pltpu
from jax.sharding import PartitionSpec as P

GX = 32


KON = 0.5
KOFF = 0.3
BTOT = 2.0
INFLUX = 0.1


def fetch(table, index):
    rows = jnp.take(table, jnp.maximum(index, 0), axis=0)
    has = (index >= 0).reshape((-1,) + (1,) * (rows.ndim - 1))
    return jnp.where(has, rows, jnp.zeros_like(rows))


def lookup(planes, before, after):
    sides = []
    for d in range(3):
        lower = fetch(planes[:, d, 1], before[d])
        upper = fetch(planes[:, d, 0], after[d])
        sides.append(jnp.stack([lower, upper], 1))
    return jnp.stack(sides, 1)


def coupling(rate_all, neighbors):
    per_dim = []
    for d in range(3):
        mine = rate_all[:, d]
        sides = []
        for side in range(2):
            other = fetch(mine, neighbors[d, side])
            has = (neighbors[d, side] >= 0)[:, None]
            sides.append(jnp.where(has, 2.0 * mine * other / (mine + other), jnp.zeros_like(mine)))
        per_dim.append(jnp.stack(sides, 1))
    return jnp.stack(per_dim, 1)


def end_planes(field):
    count, edge = (field.shape[0], field.shape[2])
    per_dim = []
    for d in range(3):
        first = lax.index_in_dim(field, 0, 2 + d, False).reshape(count, 2, edge * edge)
        last = lax.index_in_dim(field, edge - 1, 2 + d, False).reshape(count, 2, edge * edge)
        per_dim.append(jnp.stack([first, last], 1))
    return jnp.stack(per_dim, 1)


def operator(field, d, rate, glow, gup, hlow, hup):
    axis = 2 + d
    edge = field.shape[axis]
    plane_shape = lax.index_in_dim(field, 0, axis, False).shape
    lower_face = jnp.expand_dims(hlow.reshape(plane_shape), axis)
    upper_face = jnp.expand_dims(hup.reshape(plane_shape), axis)
    upper = jnp.concatenate([lax.slice_in_dim(field, 1, edge, axis=axis), upper_face], axis)
    lower = jnp.concatenate([lower_face, lax.slice_in_dim(field, 0, edge - 1, axis=axis)], axis)
    place = lax.broadcasted_iota(jnp.int32, field.shape, axis)
    inner = rate[:, :, None, None, None]
    c_up = jnp.where(place == edge - 1, gup[:, :, None, None, None], inner)
    c_down = jnp.where(place == 0, glow[:, :, None, None, None], inner)
    return c_up * (upper - field) + c_down * (lower - field)


def reaction(field, fraction):
    count, edge = (field.shape[0], field.shape[2])
    alpha = fraction.reshape(count, edge, edge, edge)
    calc, bound = (field[:, 0], field[:, 1])
    bind = KON * calc * (BTOT - bound) - KOFF * bound
    return jnp.stack([-bind + INFLUX * (1.0 - alpha) / alpha, bind], 1)


def apply_inverse(block, field, d):
    forms = ["psab,psbjk->psajk", "psab,psibk->psiak", "psab,psijb->psija"]
    return jnp.einsum(forms[d], block, field, precision=lax.Precision.HIGHEST)


def line_ends(field, d):
    count, edge = (field.shape[0], field.shape[2])
    first = lax.index_in_dim(field, 0, 2 + d, False).reshape(count, 2, edge * edge)
    last = lax.index_in_dim(field, edge - 1, 2 + d, False).reshape(count, 2, edge * edge)
    return jnp.stack([first, last], 2)


def block_terms(glow, gup, corner):
    v_first, v_last, w_first, w_last = (
        corner[..., 0],
        corner[..., 1],
        corner[..., 2],
        corner[..., 3],
    )
    a00 = 1.0 + glow * v_first
    a01 = gup * w_first
    a10 = glow * v_last
    a11 = 1.0 + gup * w_last
    lq0 = -glow * v_first
    lq1 = -glow * v_last
    up0 = -gup * w_first
    up1 = -gup * w_last
    return (a00, a01, a10, a11, lq0, lq1, up0, up1)


def chain_order(before, rank):
    slots = jnp.arange(before.shape[0], dtype=jnp.int32)
    pointer = jnp.where(before >= 0, before, slots)
    for step in range(GX.bit_length()):
        pointer = jnp.take(pointer, pointer, axis=0)
    sort_key = pointer * GX + rank
    order = jnp.argsort(sort_key)
    inverse_order = jnp.argsort(order)
    return (order, inverse_order)


def shift_down(values):
    return jnp.concatenate([jnp.zeros_like(values[:1]), values[:-1]], 0)


def shift_up(values):
    return jnp.concatenate([values[1:], jnp.zeros_like(values[:1])], 0)


def compose_maps(first_map, second_map):
    e00, e01, e10, e11 = first_map
    l00, l01, l10, l11 = second_map
    n00 = l00 * e00 + l01 * e10
    n01 = l00 * e01 + l01 * e11
    n10 = l10 * e00 + l11 * e10
    n11 = l10 * e01 + l11 * e11
    scale = jnp.abs(n00) + jnp.abs(n01) + jnp.abs(n10) + jnp.abs(n11)
    return (n00 / scale, n01 / scale, n10 / scale, n11 / scale)


def compose_affine(first_map, second_map):
    first_q, first_p = first_map
    second_q, second_p = second_map
    return (first_q * second_q, second_p + second_q * first_p)


def sorted_solve(glow, gup, corner, before, after, order, inverse_order, ends):
    glow = jnp.take(glow, order, axis=0)
    gup = jnp.take(gup, order, axis=0)
    corner = jnp.take(corner, order, axis=0)
    has_b = jnp.take(before, order, axis=0) >= 0
    has_a = jnp.take(after, order, axis=0) >= 0
    arranged = jnp.take(ends, order, axis=0)
    y0 = arranged[:, :, 0]
    y1 = arranged[:, :, 1]
    a00, a01, a10, a11, lq0, lq1, up0, up1 = block_terms(glow, gup, corner)
    maps = (
        -(lq0 * up1 - lq1 * up0),
        a00 * up1 - a10 * up0,
        -(lq0 * a11 - a01 * lq1),
        a00 * a11 - a01 * a10,
    )
    summed = lax.associative_scan(compose_maps, maps, axis=0)
    f1_prev = summed[1] / summed[3]
    fq = shift_down(f1_prev)
    b00 = a00 - lq0 * fq
    b10 = a10 - lq1 * fq
    det = b00 * a11 - a01 * b10
    f0 = (a11 * up0 - a01 * up1) / det
    f1 = (b00 * up1 - b10 * up0) / det
    slope = (-(b00 * lq1 - b10 * lq0) / det)[:, :, None]
    offset = (b00[:, :, None] * y1 - b10[:, :, None] * y0) / det[:, :, None]
    e1 = lax.associative_scan(compose_affine, (slope, offset), axis=0)[1]
    eq = shift_down(e1)
    e0 = (
        a11[:, :, None] * y0 - a01[:, :, None] * y1 - (a11 * lq0 - a01 * lq1)[:, :, None] * eq
    ) / det[:, :, None]
    zp = lax.associative_scan(compose_affine, (-f0[:, :, None], e0), reverse=True, axis=0)[1]
    pn = shift_up(zp)
    zq = e1 - f1[:, :, None] * pn
    low = jnp.where(has_b[:, None, None], zp - shift_down(zq), jnp.zeros_like(zp))
    high = jnp.where(has_a[:, None, None], zq - pn, jnp.zeros_like(zq))
    return jnp.take(jnp.stack([low, high], 2), inverse_order, axis=0)


def correct(local, block, glow, gup, jumps, d):
    axis = 2 + d
    count, edge = (local.shape[0], local.shape[2])
    shape_v = [count, 2, 1, 1, 1]
    shape_v[axis] = edge
    first_col = block[..., 0].reshape(shape_v)
    last_col = block[..., edge - 1].reshape(shape_v)
    plane_shape = lax.index_in_dim(local, 0, axis, False).shape
    low = jnp.expand_dims(jumps[:, :, 0].reshape(plane_shape), axis)
    high = jnp.expand_dims(jumps[:, :, 1].reshape(plane_shape), axis)
    return (
        local
        - glow[:, :, None, None, None] * low * first_col
        - gup[:, :, None, None, None] * high * last_col
    )


def general_body(calcium, buffer, fraction, rates, inverses, neighbors, ranks):
    count, edge = (calcium.shape[0], calcium.shape[1])
    devices = lax.axis_size("bricks")
    square = edge * edge
    per_device = square // devices
    start = lax.axis_index("bricks") * count
    corners = jnp.stack(
        [
            inverses[..., 0, 0],
            inverses[..., edge - 1, 0],
            inverses[..., 0, edge - 1],
            inverses[..., edge - 1, edge - 1],
        ],
        -1,
    )
    rate_all, corner_all = (
        lax.all_gather(rates, "bricks", axis=0, tiled=True),
        lax.all_gather(corners, "bricks", axis=0, tiled=True),
    )
    couple_all = coupling(rate_all, neighbors)
    couple = lax.dynamic_slice_in_dim(couple_all, start, count, 0)
    field = jnp.stack([calcium, buffer], 1).reshape(count, 2, edge, edge, edge)
    planes = end_planes(field).reshape(count, 3, 2, 2, devices, per_device)
    lined = lookup(
        lax.all_to_all(planes, "bricks", split_axis=4, concat_axis=0, tiled=True),
        neighbors[:, 0],
        neighbors[:, 1],
    )
    halos = lax.all_to_all(lined, "bricks", split_axis=0, concat_axis=4, tiled=True).reshape(
        count, 3, 2, 2, square
    )
    lams = [
        operator(
            field, d, rates[:, d], couple[:, d, 0], couple[:, d, 1], halos[:, d, 0], halos[:, d, 1]
        )
        for d in range(3)
    ]
    rhs = field + lams[0] + 2.0 * lams[1] + 2.0 * lams[2] + reaction(field, fraction)

    def solve(right, d):
        block = inverses[:, d]
        local = apply_inverse(block, right, d)
        ends = line_ends(local, d).reshape(count, 2, 2, devices, per_device)
        order, inverse_order = chain_order(neighbors[d, 0], ranks[d])
        chain_fn = partial(
            sorted_solve,
            couple_all[:, d, 0],
            couple_all[:, d, 1],
            corner_all[:, d],
            neighbors[d, 0],
            neighbors[d, 1],
            order,
            inverse_order,
        )
        lined_jumps = chain_fn(
            lax.all_to_all(ends, "bricks", split_axis=3, concat_axis=0, tiled=True)[:, :, :, 0]
        )[:, :, :, None]
        jumps = lax.all_to_all(
            lined_jumps, "bricks", split_axis=0, concat_axis=3, tiled=True
        ).reshape(count, 2, 2, square)
        return correct(local, block, couple[:, d, 0], couple[:, d, 1], jumps, d)

    first = solve(rhs, 0)
    second = solve(first - lams[1], 1)
    third = solve(second - lams[2], 2)
    result = third.reshape(count, 2, edge, edge * edge)
    return (result[:, 0], result[:, 1])


LANES = 128


ROWS = 5


def cosine_basis(edge):
    wave = np.arange(edge)[:, None]
    place = np.arange(edge)[None, :]
    basis = np.sqrt(2.0 / edge) * np.cos(np.pi * wave * (place + 0.5) / edge)
    basis[0] = math.sqrt(1.0 / edge)
    eigen = 2.0 - 2.0 * np.cos(np.pi * np.arange(edge) / edge)
    return basis, eigen


def parts_of(x):
    high = x.astype(jnp.bfloat16).astype(jnp.float32)
    rest = x - high
    middle = rest.astype(jnp.bfloat16).astype(jnp.float32)
    return high, middle, rest - middle


LEFT = (0, 0, 0, 1, 1, 2)
RIGHT = (0, 1, 2, 0, 1, 0)


def left_of(x):
    parts = parts_of(x)
    return jnp.concatenate([parts[p] for p in LEFT], 1)


def right_of(x, axis=0):
    parts = parts_of(x)
    return jnp.concatenate([parts[p] for p in RIGHT], axis)


def exact_of(x):
    return jnp.concatenate(parts_of(x), 1)


def dot(a, b):
    return jnp.dot(a, b, preferred_element_type=jnp.float32)


def dot_lanes(a, b):
    return lax.dot_general(a, b, (((1,), (1,)), ((), ())), preferred_element_type=jnp.float32)


def host_parts(x):
    parts = []
    for _ in range(3):
        parts.append(x.astype(jnp.bfloat16).astype(np.float64))
        x = x - parts[-1]
    return parts


def host_left(x):
    parts = host_parts(x)
    return np.concatenate([parts[p] for p in LEFT], 1)


def host_right(x):
    parts = host_parts(x)
    return np.concatenate([parts[p] for p in RIGHT], 0)


def lane_of(shape):
    return lax.broadcasted_iota(jnp.int32, shape, len(shape) - 1)


def swap_blocks(four):
    x0, x1, x2, x3 = four
    lane = lane_of(x0.shape)
    low = (lane & 64) == 0
    y0, y2 = jnp.where(low, x0, pltpu.roll(x2, 64, 1)), jnp.where(low, pltpu.roll(x0, 64, 1), x2)
    y1, y3 = jnp.where(low, x1, pltpu.roll(x3, 64, 1)), jnp.where(low, pltpu.roll(x1, 64, 1), x3)
    even = (lane & 32) == 0
    z0, z1 = jnp.where(even, y0, pltpu.roll(y1, 32, 1)), jnp.where(even, pltpu.roll(y0, 96, 1), y1)
    z2, z3 = jnp.where(even, y2, pltpu.roll(y3, 32, 1)), jnp.where(even, pltpu.roll(y2, 96, 1), y3)
    return [z0, z1, z2, z3]


def swap_rows(source, base, scratch, at, edge):
    tiles = edge // 4
    for c in range(tiles):
        rows = [source[pl.ds(base + edge * c + g, tiles, stride=4), :] for g in range(4)]
        for t4, row in enumerate(swap_blocks(rows)):
            scratch[pl.ds(at + 4 * c + t4, tiles, stride=edge), :] = row


def tile_rows(x, edge):
    tiles = edge // 4
    return jnp.concatenate([x[:, LANES * c : LANES * (c + 1)] for c in range(tiles)], 0)


def wide(ref, at, edge):
    tiles = edge // 4
    return jnp.concatenate([ref[pl.ds(at + edge * c, edge), :] for c in range(tiles)], 1)


def swap_inner(refs, edge):
    tiles = edge // 4
    fields = [(ref, b) for ref in refs for b in range(ref.shape[0])]
    whole = [
        exact_of(jnp.concatenate([ref[b, :, LANES * c : LANES * (c + 1)] for ref, b in fields], 0))
        for c in range(tiles)
    ]
    row = lax.broadcasted_iota(jnp.int32, (LANES, LANES), 0)
    lane = lane_of((LANES, LANES))
    for to in range(tiles):
        total = jnp.zeros((len(fields) * edge, LANES), jnp.float32)
        for c in range(tiles):
            hit = ((row & (edge - 1)) == 4 * to + lane // edge) & ((lane & (edge - 1)) == 4 * c + row // edge)
            hit = hit.astype(jnp.float32)
            total = total + dot(whole[c], jnp.concatenate([hit] * 3, 0))
        for f, (ref, b) in enumerate(fields):
            ref[b, :, LANES * to : LANES * (to + 1)] = total[edge * f : edge * (f + 1)]


def normal_of(near, slot):
    along_j = (near[1, 0, slot] >= 0) | (near[1, 1, slot] >= 0)
    return jnp.where(along_j, 1, 2)


def message_kernel(
    near_in, rates_in, calcium_in, buffer_in, fraction_in, inverses_in, const_in,
    msg, solved,
    near, rates, calcium, buffer, fraction, inverses, const, sems,
):
    count, edge = calcium.shape[0], calcium.shape[1]
    tiles = edge // 4
    size = tiles * edge
    copies = [
        pltpu.make_async_copy(source, target, sems.at[x])
        for x, (source, target) in enumerate(
            (
                (near_in, near),
                (rates_in, rates),
                (calcium_in, calcium),
                (buffer_in, buffer),
                (fraction_in, fraction),
                (inverses_in, inverses),
                (const_in, const),
            )
        )
    ]
    for copy in copies:
        copy.start()
    first_slot = lax.axis_index("bricks") * count
    for copy in copies:
        copy.wait()
    normal = normal_of(near, first_slot)
    closed = 3 - normal

    @pl.when(normal == 1)
    def _():
        swap_inner((calcium, buffer, fraction), edge)

    lane = lane_of((edge, LANES))
    inner = lane & (edge - 1)
    square_row = lax.broadcasted_iota(jnp.int32, (LANES, LANES), 0)
    square_lane = lane_of((LANES, LANES))
    on_block = (square_row // edge) == (square_lane // edge)
    faces_u, faces_y, ends0, ends1 = [], [], [], []
    for b in range(count):
        face = jnp.where(near[normal, 1, first_slot + b] >= 0, edge - 1, 0)
        calc = [calcium[b, :, LANES * c : LANES * (c + 1)] for c in range(tiles)]
        bound = [buffer[b, :, LANES * c : LANES * (c + 1)] for c in range(tiles)]
        alpha = [fraction[b, :, LANES * c : LANES * (c + 1)] for c in range(tiles)]
        bind = [KON * x * (BTOT - y) - KOFF * y for x, y in zip(calc, bound)]
        source_calc = [INFLUX / a - (w + INFLUX) for w, a in zip(bind, alpha)]
        for q, (u, source) in enumerate(((calc, source_calc), (bound, bind))):
            at = size * (2 * b + q)
            rate_t, rate_n = 2.0 * rates[b, q, closed], 2.0 * rates[b, q, normal]
            ahead = [pltpu.roll(x, LANES - edge, 1) for x in u]
            behind = [pltpu.roll(x, edge, 1) for x in u]
            f = []
            for c in range(tiles):
                x = u[c]
                next_t = jnp.where(lane < LANES - edge, ahead[c], ahead[c + 1] if c + 1 < tiles else x)
                last_t = jnp.where(lane >= edge, behind[c], behind[c - 1] if c else x)
                next_n = jnp.where(inner == edge - 1, x, pltpu.roll(x, LANES - 1, 1))
                last_n = jnp.where(inner == 0, x, pltpu.roll(x, 1, 1))
                twice = x + x
                along = rate_t * (next_t + last_t - twice) + rate_n * (next_n + last_n - twice)
                f.append(twice + along + source[c])
            g = dot(left_of(inverses[b, 0, q]), right_of(jnp.concatenate(f, 1)))
            ends0.append(jnp.concatenate([g[0:1, LANES * c : LANES * (c + 1)] for c in range(tiles)], 0))
            ends1.append(jnp.concatenate([g[edge - 1 : edge, LANES * c : LANES * (c + 1)] for c in range(tiles)], 0))
            w = jnp.concatenate([g[:, LANES * c : LANES * (c + 1)] - 2.0 * u[c] for c in range(tiles)], 0)
            sides = [
                jnp.where(on_block, jnp.concatenate([jnp.concatenate([x.astype(jnp.float32)] * 4, 1)] * 4, 0), 0.0)
                for x in parts_of(inverses[b, normal, q])
            ]
            y = dot(right_of(w, 1), jnp.concatenate([sides[p] for p in LEFT], 0))
            solved[pl.ds(at, size), :] = y
            face_u = jnp.zeros((edge, LANES), jnp.float32)
            face_y = jnp.zeros((edge, LANES), jnp.float32)
            for c in range(tiles):
                shift = (c - face) & (LANES - 1)
                face_u = jnp.where(inner == c, pltpu.roll(u[c], shift, 1), face_u)
                face_y = jnp.where(inner == c, pltpu.roll(y[edge * c : edge * (c + 1)], shift, 1), face_y)
            faces_u.append(face_u)
            faces_y.append(face_y)

    stack = jnp.concatenate(swap_blocks(ends0) + swap_blocks(ends1), 0)
    ends_of = const[:, : 6 * edge].astype(jnp.float32)
    faces_of = const[:, 2 * LANES :].astype(jnp.float32)
    both = dot(ends_of, right_of(jnp.concatenate([stack[:edge], stack[edge:]], 1)))
    part_u = dot_lanes(faces_of, right_of(jnp.concatenate(faces_u, 0), 1))
    part_y = dot_lanes(faces_of, right_of(jnp.concatenate(faces_y, 0), 1))
    fields = swap_blocks([both[:, :LANES], both[:, LANES:], part_u, part_y])
    for x, part in enumerate(fields):
        msg[pl.ds(x, edge, stride=ROWS), :] = part
    row = jnp.zeros((edge, LANES), jnp.float32)
    for b in range(count):
        for q in range(2):
            for x, rate in enumerate((rates[b, q, 0], rates[b, q, closed], rates[b, q, normal])):
                row = jnp.where(lane == (2 * b + q) * edge + x, rate, row)
    msg[pl.ds(4, edge, stride=ROWS), :] = row


def local_kernel(
    near_in, solved_in, inverses_in,
    base, pick, flags, edges,
    near, table, solved, inverses, work, other, sems,
):
    count, edge = inverses.shape[0], inverses.shape[3]
    tiles = edge // 4
    size = tiles * edge
    slots = near.shape[2]
    copies = [
        pltpu.make_async_copy(source, target, sems.at[x])
        for x, (source, target) in enumerate(
            (
                (near_in, near),
                (near_in, table),
                (solved_in, solved),
                (inverses_in, inverses),
            )
        )
    ]
    for copy in copies:
        copy.start()
    for copy in copies[:2]:
        copy.wait()
    normal = normal_of(near, 0)
    closed = 3 - normal
    up = near[normal, 1, 0] >= 0
    touch = up | (near[normal, 0, 0] >= 0)

    lane = lane_of((8, LANES))
    back = jnp.broadcast_to(table[0, 0:1, :], (8, slots))
    back = jnp.concatenate([back] * (LANES // slots), 1)
    pointer = jnp.where(back >= 0, back, lane & (slots - 1))
    place = jnp.where(back >= 0, 1, 0)

    def pull(values, index):
        return jnp.take_along_axis(values, index, axis=1, mode="promise_in_bounds")

    reach = 1
    while reach < edge:
        place = place + pull(place, pointer)
        pointer = pull(pointer, pointer)
        reach *= 2
    chain = jnp.where(pointer == pointer[:, 0:1], 0, edge) + place
    goal = pull(chain, (lane & (edge - 1)) * count + lane // (2 * edge)) + 2 * (lane & edge)
    hit = lax.broadcasted_iota(jnp.int32, (LANES, LANES), 0) == goal[0:1]
    pick[...] = hit.astype(jnp.float32).T
    face = jnp.where(((lane & edge) == 0) == up, edge - 1, 0).astype(jnp.float32)
    depth = lax.broadcasted_iota(jnp.int32, (8, LANES), 0)
    angle = jnp.full((8, LANES), lax.axis_index("bricks")).astype(jnp.float32) * (0.5 * math.pi / edge)
    half = jnp.sin(angle)
    flags[...] = jnp.where(
        depth == 0,
        face,
        jnp.where(
            depth == 1,
            jnp.where(touch, 1.0, 0.0),
            jnp.where(depth == 2, jnp.where(normal == 2, 1.0, 0.0), 4.0 * half * half),
        ),
    )

    for copy in copies[2:]:
        copy.wait()
    first_slot = lax.axis_index("bricks") * count
    for b in range(count):
        face = jnp.where(near[normal, 1, first_slot + b] >= 0, edge - 1, 0)
        for q in range(2):
            x = 2 * b + q
            at = size * x
            swap_rows(solved, at, other, 0, edge)
            whole = dot(left_of(inverses[b, closed, q]), right_of(wide(other, 0, edge)))
            for c in range(tiles):
                other[pl.ds(edge * c, edge), :] = whole[:, LANES * c : LANES * (c + 1)]
            swap_rows(other, 0, work, 0, edge)
            base[pl.ds(at, size), :] = work[...]
            row_n = jnp.concatenate([inverses[b, normal, q, pl.ds(face, 1), :]] * 4, 1)
            edges[x, 0] = jnp.broadcast_to(inverses[b, 0, q, :, 0:1], (edge, LANES))
            edges[x, 1] = jnp.broadcast_to(inverses[b, 0, q, :, edge - 1 : edge], (edge, LANES))
            edges[x, 2] = jnp.broadcast_to(row_n, (edge, LANES))


def owner_kernel(recv, pick, flags, const, out):
    edge = const.shape[0]
    turned = const[:, : 6 * edge]
    basis = const[:, 2 * LANES : 2 * LANES + 6 * edge]
    lam, v_first, v_last = (const[:, LANES * x : LANES * (x + 1)] for x in (4, 5, 6))
    face, touch, normal_2, my_lam = flags[0:1], flags[1:2], flags[2:3], flags[3:4]

    hit = pick[...]
    data = jnp.concatenate([recv[pl.ds(x, edge, stride=ROWS), :] for x in range(4)], 0).T
    tail = recv[pl.ds(4, edge, stride=ROWS), :]
    tail = jnp.concatenate([tail] + [pltpu.roll(tail, LANES - edge * x, 1) for x in range(1, 4)], 0).T[:16]
    parts = dot(exact_of(jnp.concatenate([tail, data], 0)), jnp.concatenate([hit] * 3, 0))
    rate_0, rate_t, rate_n = parts[0:1], parts[1:2], parts[2:3]
    y0, y1, face_u, face_y = (parts[16 + edge * x : 16 + edge * (x + 1)] for x in range(4))

    lane = lane_of((1, LANES))
    place = lane & (edge - 1)
    first_row = (lane & edge) == 0

    def partner(x):
        return jnp.where(first_row, pltpu.roll(x, LANES - edge, 1), pltpu.roll(x, edge, 1))

    def after(x, s=1):
        return pltpu.roll(x, LANES - s, 1)

    def before(x, s=1):
        return pltpu.roll(x, s, 1)

    damp_0 = 1.0 / (1.0 + lam * rate_0)
    damp_n = 1.0 / (1.0 + lam * rate_n)
    damp_t = 1.0 / (1.0 + my_lam * rate_t)
    other_n = partner(rate_n)
    g = jnp.where(touch > 0.5, 2.0 * rate_n * other_n / (rate_n + other_n), 0.0)
    cross = 2.0 * g * (partner(face_u) - face_u)
    near_c = jnp.sum(damp_0 * v_first * v_first, 0, keepdims=True)
    far_c = jnp.sum(damp_0 * v_first * v_last, 0, keepdims=True)
    end_n = jnp.sum(damp_n * v_first * v_first, 0, keepdims=True)
    open_face = place < edge - 1
    right = jnp.where(open_face, y1 - after(y0), 0.0)
    both = dot(basis, right_of(jnp.concatenate([cross, right], 1)))
    damped = damp_0 * both[:, :LANES]
    pieces = dot(turned, right_of(jnp.concatenate([damped, damp_0 * v_first, damp_0 * v_last], 1)))
    spread, col_0, col_1 = (pieces[:, LANES * x : LANES * (x + 1)] for x in range(3))
    v_face = jnp.where(face < 0.5, v_first, v_last)
    at_first = v_face * jnp.sum(v_first * damped, 0, keepdims=True)
    at_last = v_face * jnp.sum(v_last * damped, 0, keepdims=True)
    right = both[:, LANES:] + jnp.where(open_face, at_last - after(at_first), 0.0)

    inv_rate = 1.0 / rate_0
    diag = jnp.where(open_face, 0.5 * (inv_rate + after(inv_rate)) + near_c + after(near_c), 1.0)
    lower = jnp.where(open_face & (place > 0), -far_c, 0.0)
    upper = jnp.where(place < edge - 2, -after(far_c), 0.0)
    step = 1
    while step < edge:
        inverse = 1.0 / diag
        back = -lower * before(inverse, step)
        fore = -upper * after(inverse, step)
        diag = diag + back * before(upper, step) + fore * after(lower, step)
        right = right + back * before(right, step) + fore * after(right, step)
        lower = back * before(lower, step)
        upper = fore * after(upper, step)
        step *= 2
    flux_up = right / diag
    flux_down = jnp.where(place > 0, before(flux_up), 0.0)

    weight_down = jnp.sum(damp_n * v_face * flux_down, 0, keepdims=True)
    weight_up = jnp.sum(damp_n * v_face * flux_up, 0, keepdims=True)
    ends = face_y + end_n * spread + col_0 * weight_down - col_1 * weight_up
    ends = jnp.where(normal_2 > 0.5, damp_t, 1.0) * ends
    jump = g / (1.0 + g * (end_n + partner(end_n))) * (ends - partner(ends))
    face_out = jnp.where(normal_2 > 0.5, damp_t * spread - jump, damp_t * (spread - jump))
    damp_nt = damp_n * damp_t
    lines = dot(turned, right_of(jnp.concatenate([damp_nt * flux_down, damp_nt * flux_up], 1)))
    packed = jnp.concatenate(
        [lines[:, :LANES], lines[:, LANES:], face_out, jnp.zeros((edge, LANES), jnp.float32)], 0
    )
    reply = dot_lanes(jnp.concatenate([hit] * 3, 1), exact_of(packed))
    kinds = swap_blocks([reply[edge * x : edge * (x + 1)] for x in range(4)])
    for x in range(3):
        out[pl.ds(x, edge, stride=3), :] = kinds[x]


def update_kernel(
    recv, base, edges, flags, calcium, buffer, const,
    calcium_out, buffer_out,
    calcium_next, buffer_next, work, sems,
):
    count, edge = calcium.shape[0], calcium.shape[1]
    tiles = edge // 4
    size = tiles * edge
    swapped = flags[2, 0] < 0.5
    old = jnp.where(flags[2:3] < 0.5, 0.0, 1.0)
    low, high, face_part = (recv[pl.ds(x, edge, stride=3), :] for x in range(3))
    parts = [part.astype(jnp.float32) for part in parts_of(face_part)]
    turn = jnp.concatenate([parts[p] for p in LEFT] + [jnp.zeros_like(parts[0])] * 2, 0)
    turn = turn.T[:, : 6 * edge]
    face_wide = dot(turn, const[:, 2 * LANES :].astype(jnp.float32))
    lines = dot(const[:edge, : 6 * edge].astype(jnp.float32), right_of(jnp.concatenate([low, high], 1)))
    rows = []
    for e in range(2):
        work[pl.ds(edge * e, edge), :] = lines[:, LANES * e : LANES * (e + 1)]
        rows.append(swap_blocks([work[pl.ds(edge * e + t4, tiles, stride=4), :] for t4 in range(4)]))

    stores = [
        pltpu.make_async_copy(source.at[b], to.at[b], sems.at[2 * b + q])
        for b in range(count)
        for q, (source, to) in enumerate(((calcium_next, calcium_out), (buffer_next, buffer_out)))
    ]
    for b in range(count):
        for q, (ref, now) in enumerate(((calcium_next, calcium), (buffer_next, buffer))):
            x = 2 * b + q
            at = size * x
            col_0, col_1, row_n = edges[x, 0], edges[x, 1], edges[x, 2]
            for c in range(tiles):
                part = slice(LANES * c, LANES * (c + 1))
                ref[b, :, part] = (
                    (base[pl.ds(at + edge * c, edge), :] + old * now[b, :, part])
                    + face_wide[edge * x : edge * (x + 1), part] * row_n
                    + (col_0 * rows[0][x][c : c + 1] - col_1 * rows[1][x][c : c + 1])
                )
            stores[x].start()
    for store in stores:
        store.wait()

    @pl.when(swapped)
    def _():
        swap_inner((calcium_next, buffer_next), edge)
        calcium_next[...] = calcium_next[...] + calcium[...]
        buffer_next[...] = buffer_next[...] + buffer[...]
        for store in stores:
            store.start()
        for store in stores:
            store.wait()


def fast_body(calcium, buffer, fraction, rates, inverses, neighbors, ranks):
    count, edge = calcium.shape[0], calcium.shape[1]
    devices = lax.axis_size("bricks")
    tiles = edge // 4
    size = tiles * edge
    f32 = jnp.float32
    basis, eigen = cosine_basis(edge)
    place = np.arange(edge)
    ends_of = np.zeros((edge, edge))
    ends_of[:, (place % 4) * tiles + place // 4] = basis
    faces_of = np.zeros((edge, LANES))
    faces_of[:, (place % 4) * edge + place // 4] = basis
    pad = lambda x: np.pad(x, ((0, 0), (0, 2 * LANES - x.shape[1])))
    message_const = np.concatenate([pad(host_left(ends_of)), host_left(faces_of)], 1)
    lanes_of = lambda x: np.tile(x[:, None], (1, LANES))
    owner_const = np.concatenate(
        [pad(host_left(basis.T)), pad(host_left(basis))]
        + [lanes_of(x) for x in (eigen, basis[:, 0], basis[:, -1])],
        1,
    )
    expand = host_right(np.repeat(basis, edge, 1))
    back_const = np.pad(pad(host_left(basis.T)), ((0, 5 * edge), (0, 0)))
    update_const = np.concatenate([back_const, expand], 1)
    smem = pl.BlockSpec(memory_space=pltpu.SMEM)
    vmem = pl.BlockSpec(memory_space=pltpu.VMEM)
    hbm = pl.BlockSpec(memory_space=pltpu.HBM)
    params = pltpu.CompilerParams(vmem_limit_bytes=48 * 2**20)
    const = lambda x: jnp.asarray(x, f32)
    field = jax.ShapeDtypeStruct(calcium.shape, f32)
    tall = jax.ShapeDtypeStruct((2 * count * size, LANES), f32)

    stay = lambda x: pltpu.with_memory_space_constraint(x, pltpu.HBM)
    msg, solved = pl.pallas_call(
        message_kernel,
        out_shape=(jax.ShapeDtypeStruct((devices * ROWS, LANES), f32), tall),
        in_specs=[hbm] * 7,
        out_specs=(vmem, vmem),
        scratch_shapes=[
            pltpu.SMEM(neighbors.shape, jnp.int32),
            pltpu.SMEM((count, 2, 3), f32),
            pltpu.VMEM(calcium.shape, f32),
            pltpu.VMEM(calcium.shape, f32),
            pltpu.VMEM(fraction.shape, f32),
            pltpu.VMEM(inverses.shape, f32),
            pltpu.VMEM(message_const.shape, jnp.bfloat16),
            pltpu.SemaphoreType.DMA((7,)),
        ],
        compiler_params=pltpu.CompilerParams(vmem_limit_bytes=48 * 2**20),
        name="message",
    )(*(stay(x) for x in (neighbors, rates.transpose(0, 2, 1), calcium, buffer, fraction, inverses, jnp.asarray(message_const, jnp.bfloat16))))
    recv = lax.all_to_all(msg.reshape(devices * ROWS, 1, LANES), "bricks", 0, 0, tiled=True).reshape(devices * ROWS, LANES)
    base, pick, flags, edges = pl.pallas_call(
        local_kernel,
        out_shape=(
            tall,
            jax.ShapeDtypeStruct((LANES, LANES), f32),
            jax.ShapeDtypeStruct((8, LANES), f32),
            jax.ShapeDtypeStruct((2 * count, 3, edge, LANES), f32),
        ),
        in_specs=[hbm] * 3,
        out_specs=(vmem,) * 4,
        scratch_shapes=[
            pltpu.SMEM(neighbors.shape, jnp.int32),
            pltpu.VMEM(neighbors.shape, jnp.int32),
            pltpu.VMEM(tall.shape, f32),
            pltpu.VMEM(inverses.shape, f32),
            pltpu.VMEM((size, LANES), f32),
            pltpu.VMEM((size, LANES), f32),
            pltpu.SemaphoreType.DMA((4,)),
        ],
        compiler_params=pltpu.CompilerParams(vmem_limit_bytes=48 * 2**20),
        cost_estimate=pl.CostEstimate(flops=2 * 10**7, bytes_accessed=4 * 10**6, transcendentals=0),
        name="local_solution",
    )(neighbors, solved, inverses)
    reply = pl.pallas_call(
        owner_kernel,
        out_shape=jax.ShapeDtypeStruct((devices * 3, LANES), f32),
        in_specs=[vmem] * 4,
        out_specs=vmem,
        compiler_params=params,
        name="chain_and_face_solves",
    )(recv, pick, flags, const(owner_const))
    back = lax.all_to_all(reply.reshape(devices * 3, 1, LANES), "bricks", 0, 0, tiled=True)
    return pl.pallas_call(
        update_kernel,
        out_shape=(field, field),
        in_specs=[vmem] * 7,
        out_specs=(hbm, hbm),
        scratch_shapes=[
            pltpu.VMEM(calcium.shape, f32),
            pltpu.VMEM(buffer.shape, f32),
            pltpu.VMEM((2 * edge, LANES), f32),
            pltpu.SemaphoreType.DMA((2 * count,)),
        ],
        compiler_params=params,
        name="rank_three_update",
    )(back.reshape(devices * 3, LANES), base, edges, flags, calcium, buffer, jnp.asarray(update_const, jnp.bfloat16))


def body(calcium, buffer, fraction, rates, inverses, neighbors, ranks):
    count, edge = calcium.shape[0], calcium.shape[1]
    devices = lax.axis_size("bricks")
    if edge == GX and devices == edge and count == 2 and 4 * edge == LANES:
        return fast_body(calcium, buffer, fraction, rates, inverses, neighbors, ranks)
    return general_body(calcium, buffer, fraction, rates, inverses, neighbors, ranks)


def solution(mesh):
    in_specs = (
        P("bricks", None, None),
        P("bricks", None, None),
        P("bricks", None, None),
        P("bricks", None, None),
        P("bricks", None, None, None, None),
        P(),
        P(),
    )
    out_specs = (P("bricks", None, None), P("bricks", None, None))
    return jax.shard_map(body, mesh=mesh, in_specs=in_specs, out_specs=out_specs, check_vma=False)
```

```python
from functools import partial
import math

import jax
import jax.numpy as jnp
import numpy as np
from jax import lax
from jax.experimental import pallas as pl
from jax.experimental.pallas import tpu as pltpu
from jax.sharding import PartitionSpec as P

GX = 32


KON = 0.5
KOFF = 0.3
BTOT = 2.0
INFLUX = 0.1


def fetch(table, index):
    rows = jnp.take(table, jnp.maximum(index, 0), axis=0)
    has = (index >= 0).reshape((-1,) + (1,) * (rows.ndim - 1))
    return jnp.where(has, rows, jnp.zeros_like(rows))


def lookup(planes, before, after):
    sides = []
    for d in range(3):
        lower = fetch(planes[:, d, 1], before[d])
        upper = fetch(planes[:, d, 0], after[d])
        sides.append(jnp.stack([lower, upper], 1))
    return jnp.stack(sides, 1)


def coupling(rate_all, neighbors):
    per_dim = []
    for d in range(3):
        mine = rate_all[:, d]
        sides = []
        for side in range(2):
            other = fetch(mine, neighbors[d, side])
            has = (neighbors[d, side] >= 0)[:, None]
            sides.append(jnp.where(has, 2.0 * mine * other / (mine + other), jnp.zeros_like(mine)))
        per_dim.append(jnp.stack(sides, 1))
    return jnp.stack(per_dim, 1)


def end_planes(field):
    count, edge = (field.shape[0], field.shape[2])
    per_dim = []
    for d in range(3):
        first = lax.index_in_dim(field, 0, 2 + d, False).reshape(count, 2, edge * edge)
        last = lax.index_in_dim(field, edge - 1, 2 + d, False).reshape(count, 2, edge * edge)
        per_dim.append(jnp.stack([first, last], 1))
    return jnp.stack(per_dim, 1)


def operator(field, d, rate, glow, gup, hlow, hup):
    axis = 2 + d
    edge = field.shape[axis]
    plane_shape = lax.index_in_dim(field, 0, axis, False).shape
    lower_face = jnp.expand_dims(hlow.reshape(plane_shape), axis)
    upper_face = jnp.expand_dims(hup.reshape(plane_shape), axis)
    upper = jnp.concatenate([lax.slice_in_dim(field, 1, edge, axis=axis), upper_face], axis)
    lower = jnp.concatenate([lower_face, lax.slice_in_dim(field, 0, edge - 1, axis=axis)], axis)
    place = lax.broadcasted_iota(jnp.int32, field.shape, axis)
    inner = rate[:, :, None, None, None]
    c_up = jnp.where(place == edge - 1, gup[:, :, None, None, None], inner)
    c_down = jnp.where(place == 0, glow[:, :, None, None, None], inner)
    return c_up * (upper - field) + c_down * (lower - field)


def reaction(field, fraction):
    count, edge = (field.shape[0], field.shape[2])
    alpha = fraction.reshape(count, edge, edge, edge)
    calc, bound = (field[:, 0], field[:, 1])
    bind = KON * calc * (BTOT - bound) - KOFF * bound
    return jnp.stack([-bind + INFLUX * (1.0 - alpha) / alpha, bind], 1)


def apply_inverse(block, field, d):
    forms = ["psab,psbjk->psajk", "psab,psibk->psiak", "psab,psijb->psija"]
    return jnp.einsum(forms[d], block, field, precision=lax.Precision.HIGHEST)


def line_ends(field, d):
    count, edge = (field.shape[0], field.shape[2])
    first = lax.index_in_dim(field, 0, 2 + d, False).reshape(count, 2, edge * edge)
    last = lax.index_in_dim(field, edge - 1, 2 + d, False).reshape(count, 2, edge * edge)
    return jnp.stack([first, last], 2)


def block_terms(glow, gup, corner):
    v_first, v_last, w_first, w_last = (
        corner[..., 0],
        corner[..., 1],
        corner[..., 2],
        corner[..., 3],
    )
    a00 = 1.0 + glow * v_first
    a01 = gup * w_first
    a10 = glow * v_last
    a11 = 1.0 + gup * w_last
    lq0 = -glow * v_first
    lq1 = -glow * v_last
    up0 = -gup * w_first
    up1 = -gup * w_last
    return (a00, a01, a10, a11, lq0, lq1, up0, up1)


def chain_order(before, rank):
    slots = jnp.arange(before.shape[0], dtype=jnp.int32)
    pointer = jnp.where(before >= 0, before, slots)
    for step in range(GX.bit_length()):
        pointer = jnp.take(pointer, pointer, axis=0)
    sort_key = pointer * GX + rank
    order = jnp.argsort(sort_key)
    inverse_order = jnp.argsort(order)
    return (order, inverse_order)


def shift_down(values):
    return jnp.concatenate([jnp.zeros_like(values[:1]), values[:-1]], 0)


def shift_up(values):
    return jnp.concatenate([values[1:], jnp.zeros_like(values[:1])], 0)


def compose_maps(first_map, second_map):
    e00, e01, e10, e11 = first_map
    l00, l01, l10, l11 = second_map
    n00 = l00 * e00 + l01 * e10
    n01 = l00 * e01 + l01 * e11
    n10 = l10 * e00 + l11 * e10
    n11 = l10 * e01 + l11 * e11
    scale = jnp.abs(n00) + jnp.abs(n01) + jnp.abs(n10) + jnp.abs(n11)
    return (n00 / scale, n01 / scale, n10 / scale, n11 / scale)


def compose_affine(first_map, second_map):
    first_q, first_p = first_map
    second_q, second_p = second_map
    return (first_q * second_q, second_p + second_q * first_p)


def sorted_solve(glow, gup, corner, before, after, order, inverse_order, ends):
    glow = jnp.take(glow, order, axis=0)
    gup = jnp.take(gup, order, axis=0)
    corner = jnp.take(corner, order, axis=0)
    has_b = jnp.take(before, order, axis=0) >= 0
    has_a = jnp.take(after, order, axis=0) >= 0
    arranged = jnp.take(ends, order, axis=0)
    y0 = arranged[:, :, 0]
    y1 = arranged[:, :, 1]
    a00, a01, a10, a11, lq0, lq1, up0, up1 = block_terms(glow, gup, corner)
    maps = (
        -(lq0 * up1 - lq1 * up0),
        a00 * up1 - a10 * up0,
        -(lq0 * a11 - a01 * lq1),
        a00 * a11 - a01 * a10,
    )
    summed = lax.associative_scan(compose_maps, maps, axis=0)
    f1_prev = summed[1] / summed[3]
    fq = shift_down(f1_prev)
    b00 = a00 - lq0 * fq
    b10 = a10 - lq1 * fq
    det = b00 * a11 - a01 * b10
    f0 = (a11 * up0 - a01 * up1) / det
    f1 = (b00 * up1 - b10 * up0) / det
    slope = (-(b00 * lq1 - b10 * lq0) / det)[:, :, None]
    offset = (b00[:, :, None] * y1 - b10[:, :, None] * y0) / det[:, :, None]
    e1 = lax.associative_scan(compose_affine, (slope, offset), axis=0)[1]
    eq = shift_down(e1)
    e0 = (
        a11[:, :, None] * y0 - a01[:, :, None] * y1 - (a11 * lq0 - a01 * lq1)[:, :, None] * eq
    ) / det[:, :, None]
    zp = lax.associative_scan(compose_affine, (-f0[:, :, None], e0), reverse=True, axis=0)[1]
    pn = shift_up(zp)
    zq = e1 - f1[:, :, None] * pn
    low = jnp.where(has_b[:, None, None], zp - shift_down(zq), jnp.zeros_like(zp))
    high = jnp.where(has_a[:, None, None], zq - pn, jnp.zeros_like(zq))
    return jnp.take(jnp.stack([low, high], 2), inverse_order, axis=0)


def correct(local, block, glow, gup, jumps, d):
    axis = 2 + d
    count, edge = (local.shape[0], local.shape[2])
    shape_v = [count, 2, 1, 1, 1]
    shape_v[axis] = edge
    first_col = block[..., 0].reshape(shape_v)
    last_col = block[..., edge - 1].reshape(shape_v)
    plane_shape = lax.index_in_dim(local, 0, axis, False).shape
    low = jnp.expand_dims(jumps[:, :, 0].reshape(plane_shape), axis)
    high = jnp.expand_dims(jumps[:, :, 1].reshape(plane_shape), axis)
    return (
        local
        - glow[:, :, None, None, None] * low * first_col
        - gup[:, :, None, None, None] * high * last_col
    )


def general_body(calcium, buffer, fraction, rates, inverses, neighbors, ranks):
    count, edge = (calcium.shape[0], calcium.shape[1])
    devices = lax.axis_size("bricks")
    square = edge * edge
    per_device = square // devices
    start = lax.axis_index("bricks") * count
    corners = jnp.stack(
        [
            inverses[..., 0, 0],
            inverses[..., edge - 1, 0],
            inverses[..., 0, edge - 1],
            inverses[..., edge - 1, edge - 1],
        ],
        -1,
    )
    rate_all, corner_all = (
        lax.all_gather(rates, "bricks", axis=0, tiled=True),
        lax.all_gather(corners, "bricks", axis=0, tiled=True),
    )
    couple_all = coupling(rate_all, neighbors)
    couple = lax.dynamic_slice_in_dim(couple_all, start, count, 0)
    field = jnp.stack([calcium, buffer], 1).reshape(count, 2, edge, edge, edge)
    planes = end_planes(field).reshape(count, 3, 2, 2, devices, per_device)
    lined = lookup(
        lax.all_to_all(planes, "bricks", split_axis=4, concat_axis=0, tiled=True),
        neighbors[:, 0],
        neighbors[:, 1],
    )
    halos = lax.all_to_all(lined, "bricks", split_axis=0, concat_axis=4, tiled=True).reshape(
        count, 3, 2, 2, square
    )
    lams = [
        operator(
            field, d, rates[:, d], couple[:, d, 0], couple[:, d, 1], halos[:, d, 0], halos[:, d, 1]
        )
        for d in range(3)
    ]
    rhs = field + lams[0] + 2.0 * lams[1] + 2.0 * lams[2] + reaction(field, fraction)

    def solve(right, d):
        block = inverses[:, d]
        local = apply_inverse(block, right, d)
        ends = line_ends(local, d).reshape(count, 2, 2, devices, per_device)
        order, inverse_order = chain_order(neighbors[d, 0], ranks[d])
        chain_fn = partial(
            sorted_solve,
            couple_all[:, d, 0],
            couple_all[:, d, 1],
            corner_all[:, d],
            neighbors[d, 0],
            neighbors[d, 1],
            order,
            inverse_order,
        )
        lined_jumps = chain_fn(
            lax.all_to_all(ends, "bricks", split_axis=3, concat_axis=0, tiled=True)[:, :, :, 0]
        )[:, :, :, None]
        jumps = lax.all_to_all(
            lined_jumps, "bricks", split_axis=0, concat_axis=3, tiled=True
        ).reshape(count, 2, 2, square)
        return correct(local, block, couple[:, d, 0], couple[:, d, 1], jumps, d)

    first = solve(rhs, 0)
    second = solve(first - lams[1], 1)
    third = solve(second - lams[2], 2)
    result = third.reshape(count, 2, edge, edge * edge)
    return (result[:, 0], result[:, 1])


LANES = 128


ROWS = 5


def cosine_basis(edge):
    wave = np.arange(edge)[:, None]
    place = np.arange(edge)[None, :]
    basis = np.sqrt(2.0 / edge) * np.cos(np.pi * wave * (place + 0.5) / edge)
    basis[0] = math.sqrt(1.0 / edge)
    eigen = 2.0 - 2.0 * np.cos(np.pi * np.arange(edge) / edge)
    return basis, eigen


def parts_of(x):
    high = x.astype(jnp.bfloat16).astype(jnp.float32)
    rest = x - high
    middle = rest.astype(jnp.bfloat16).astype(jnp.float32)
    return high, middle, rest - middle


LEFT = (0, 0, 0, 1, 1, 2)
RIGHT = (0, 1, 2, 0, 1, 0)


def left_of(x):
    parts = parts_of(x)
    return jnp.concatenate([parts[p] for p in LEFT], 1)


def right_of(x, axis=0):
    parts = parts_of(x)
    return jnp.concatenate([parts[p] for p in RIGHT], axis)


def exact_of(x):
    return jnp.concatenate(parts_of(x), 1)


def dot(a, b):
    return jnp.dot(a, b, preferred_element_type=jnp.float32)


def dot_lanes(a, b):
    return lax.dot_general(a, b, (((1,), (1,)), ((), ())), preferred_element_type=jnp.float32)


def host_parts(x):
    parts = []
    for _ in range(3):
        parts.append(x.astype(jnp.bfloat16).astype(np.float64))
        x = x - parts[-1]
    return parts


def host_left(x):
    parts = host_parts(x)
    return np.concatenate([parts[p] for p in LEFT], 1)


def host_right(x):
    parts = host_parts(x)
    return np.concatenate([parts[p] for p in RIGHT], 0)


def lane_of(shape):
    return lax.broadcasted_iota(jnp.int32, shape, len(shape) - 1)


def swap_blocks(four):
    x0, x1, x2, x3 = four
    lane = lane_of(x0.shape)
    low = (lane & 64) == 0
    y0, y2 = jnp.where(low, x0, pltpu.roll(x2, 64, 1)), jnp.where(low, pltpu.roll(x0, 64, 1), x2)
    y1, y3 = jnp.where(low, x1, pltpu.roll(x3, 64, 1)), jnp.where(low, pltpu.roll(x1, 64, 1), x3)
    even = (lane & 32) == 0
    z0, z1 = jnp.where(even, y0, pltpu.roll(y1, 32, 1)), jnp.where(even, pltpu.roll(y0, 96, 1), y1)
    z2, z3 = jnp.where(even, y2, pltpu.roll(y3, 32, 1)), jnp.where(even, pltpu.roll(y2, 96, 1), y3)
    return [z0, z1, z2, z3]


def swap_rows(source, base, scratch, at, edge):
    tiles = edge // 4
    for c in range(tiles):
        rows = [source[pl.ds(base + edge * c + g, tiles, stride=4), :] for g in range(4)]
        for t4, row in enumerate(swap_blocks(rows)):
            scratch[pl.ds(at + 4 * c + t4, tiles, stride=edge), :] = row


def tile_rows(x, edge):
    tiles = edge // 4
    return jnp.concatenate([x[:, LANES * c : LANES * (c + 1)] for c in range(tiles)], 0)


def wide(ref, at, edge):
    tiles = edge // 4
    return jnp.concatenate([ref[pl.ds(at + edge * c, edge), :] for c in range(tiles)], 1)


def swap_inner(refs, edge):
    tiles = edge // 4
    fields = [(ref, b) for ref in refs for b in range(ref.shape[0])]
    whole = [
        exact_of(jnp.concatenate([ref[b, :, LANES * c : LANES * (c + 1)] for ref, b in fields], 0))
        for c in range(tiles)
    ]
    row = lax.broadcasted_iota(jnp.int32, (LANES, LANES), 0)
    lane = lane_of((LANES, LANES))
    for to in range(tiles):
        total = jnp.zeros((len(fields) * edge, LANES), jnp.float32)
        for c in range(tiles):
            hit = ((row & (edge - 1)) == 4 * to + lane // edge) & ((lane & (edge - 1)) == 4 * c + row // edge)
            hit = hit.astype(jnp.float32)
            total = total + dot(whole[c], jnp.concatenate([hit] * 3, 0))
        for f, (ref, b) in enumerate(fields):
            ref[b, :, LANES * to : LANES * (to + 1)] = total[edge * f : edge * (f + 1)]


def normal_of(near, slot):
    along_j = (near[1, 0, slot] >= 0) | (near[1, 1, slot] >= 0)
    return jnp.where(along_j, 1, 2)


def message_kernel(
    near_in, rates_in, calcium_in, buffer_in, fraction_in, inverses_in, const_in,
    msg, solved,
    near, rates, calcium, buffer, fraction, inverses, const, sems,
):
    count, edge = calcium.shape[0], calcium.shape[1]
    tiles = edge // 4
    size = tiles * edge
    copies = [
        pltpu.make_async_copy(source, target, sems.at[x])
        for x, (source, target) in enumerate(
            (
                (near_in, near),
                (rates_in, rates),
                (calcium_in, calcium),
                (buffer_in, buffer),
                (fraction_in, fraction),
                (inverses_in, inverses),
                (const_in, const),
            )
        )
    ]
    for copy in copies:
        copy.start()
    first_slot = lax.axis_index("bricks") * count
    for copy in copies:
        copy.wait()
    normal = normal_of(near, first_slot)
    closed = 3 - normal

    @pl.when(normal == 1)
    def _():
        swap_inner((calcium, buffer, fraction), edge)

    lane = lane_of((edge, LANES))
    inner = lane & (edge - 1)
    square_row = lax.broadcasted_iota(jnp.int32, (LANES, LANES), 0)
    square_lane = lane_of((LANES, LANES))
    on_block = (square_row // edge) == (square_lane // edge)
    faces_u, faces_y, ends0, ends1 = [], [], [], []
    for b in range(count):
        face = jnp.where(near[normal, 1, first_slot + b] >= 0, edge - 1, 0)
        calc = [calcium[b, :, LANES * c : LANES * (c + 1)] for c in range(tiles)]
        bound = [buffer[b, :, LANES * c : LANES * (c + 1)] for c in range(tiles)]
        alpha = [fraction[b, :, LANES * c : LANES * (c + 1)] for c in range(tiles)]
        bind = [KON * x * (BTOT - y) - KOFF * y for x, y in zip(calc, bound)]
        source_calc = [INFLUX / a - (w + INFLUX) for w, a in zip(bind, alpha)]
        for q, (u, source) in enumerate(((calc, source_calc), (bound, bind))):
            at = size * (2 * b + q)
            rate_t, rate_n = 2.0 * rates[b, q, closed], 2.0 * rates[b, q, normal]
            ahead = [pltpu.roll(x, LANES - edge, 1) for x in u]
            behind = [pltpu.roll(x, edge, 1) for x in u]
            f = []
            for c in range(tiles):
                x = u[c]
                next_t = jnp.where(lane < LANES - edge, ahead[c], ahead[c + 1] if c + 1 < tiles else x)
                last_t = jnp.where(lane >= edge, behind[c], behind[c - 1] if c else x)
                next_n = jnp.where(inner == edge - 1, x, pltpu.roll(x, LANES - 1, 1))
                last_n = jnp.where(inner == 0, x, pltpu.roll(x, 1, 1))
                twice = x + x
                along = rate_t * (next_t + last_t - twice) + rate_n * (next_n + last_n - twice)
                f.append(twice + along + source[c])
            g = dot(left_of(inverses[b, 0, q]), right_of(jnp.concatenate(f, 1)))
            ends0.append(jnp.concatenate([g[0:1, LANES * c : LANES * (c + 1)] for c in range(tiles)], 0))
            ends1.append(jnp.concatenate([g[edge - 1 : edge, LANES * c : LANES * (c + 1)] for c in range(tiles)], 0))
            w = jnp.concatenate([g[:, LANES * c : LANES * (c + 1)] - 2.0 * u[c] for c in range(tiles)], 0)
            sides = [
                jnp.where(on_block, jnp.concatenate([jnp.concatenate([x.astype(jnp.float32)] * 4, 1)] * 4, 0), 0.0)
                for x in parts_of(inverses[b, normal, q])
            ]
            y = dot(right_of(w, 1), jnp.concatenate([sides[p] for p in LEFT], 0))
            solved[pl.ds(at, size), :] = y
            face_u = jnp.zeros((edge, LANES), jnp.float32)
            face_y = jnp.zeros((edge, LANES), jnp.float32)
            for c in range(tiles):
                shift = (c - face) & (LANES - 1)
                face_u = jnp.where(inner == c, pltpu.roll(u[c], shift, 1), face_u)
                face_y = jnp.where(inner == c, pltpu.roll(y[edge * c : edge * (c + 1)], shift, 1), face_y)
            faces_u.append(face_u)
            faces_y.append(face_y)

    stack = jnp.concatenate(swap_blocks(ends0) + swap_blocks(ends1), 0)
    ends_of = const[:, : 6 * edge].astype(jnp.float32)
    faces_of = const[:, 2 * LANES :].astype(jnp.float32)
    both = dot(ends_of, right_of(jnp.concatenate([stack[:edge], stack[edge:]], 1)))
    part_u = dot_lanes(faces_of, right_of(jnp.concatenate(faces_u, 0), 1))
    part_y = dot_lanes(faces_of, right_of(jnp.concatenate(faces_y, 0), 1))
    fields = swap_blocks([both[:, :LANES], both[:, LANES:], part_u, part_y])
    for x, part in enumerate(fields):
        msg[pl.ds(x, edge, stride=ROWS), :] = part
    row = jnp.zeros((edge, LANES), jnp.float32)
    for b in range(count):
        for q in range(2):
            for x, rate in enumerate((rates[b, q, 0], rates[b, q, closed], rates[b, q, normal])):
                row = jnp.where(lane == (2 * b + q) * edge + x, rate, row)
    msg[pl.ds(4, edge, stride=ROWS), :] = row


def local_kernel(
    near_in, solved_in, inverses_in,
    base, pick, flags, edges,
    near, table, solved, inverses, work, other, sems,
):
    count, edge = inverses.shape[0], inverses.shape[3]
    tiles = edge // 4
    size = tiles * edge
    slots = near.shape[2]
    copies = [
        pltpu.make_async_copy(source, target, sems.at[x])
        for x, (source, target) in enumerate(
            (
                (near_in, near),
                (near_in, table),
                (solved_in, solved),
                (inverses_in, inverses),
            )
        )
    ]
    for copy in copies:
        copy.start()
    for copy in copies[:2]:
        copy.wait()
    normal = normal_of(near, 0)
    closed = 3 - normal
    up = near[normal, 1, 0] >= 0
    touch = up | (near[normal, 0, 0] >= 0)

    lane = lane_of((8, LANES))
    back = jnp.broadcast_to(table[0, 0:1, :], (8, slots))
    back = jnp.concatenate([back] * (LANES // slots), 1)
    pointer = jnp.where(back >= 0, back, lane & (slots - 1))
    place = jnp.where(back >= 0, 1, 0)

    def pull(values, index):
        return jnp.take_along_axis(values, index, axis=1, mode="promise_in_bounds")

    reach = 1
    while reach < edge:
        place = place + pull(place, pointer)
        pointer = pull(pointer, pointer)
        reach *= 2
    chain = jnp.where(pointer == pointer[:, 0:1], 0, edge) + place
    goal = pull(chain, (lane & (edge - 1)) * count + lane // (2 * edge)) + 2 * (lane & edge)
    hit = lax.broadcasted_iota(jnp.int32, (LANES, LANES), 0) == goal[0:1]
    pick[...] = hit.astype(jnp.float32).T
    face = jnp.where(((lane & edge) == 0) == up, edge - 1, 0).astype(jnp.float32)
    depth = lax.broadcasted_iota(jnp.int32, (8, LANES), 0)
    angle = jnp.full((8, LANES), lax.axis_index("bricks")).astype(jnp.float32) * (0.5 * math.pi / edge)
    half = jnp.sin(angle)
    flags[...] = jnp.where(
        depth == 0,
        face,
        jnp.where(
            depth == 1,
            jnp.where(touch, 1.0, 0.0),
            jnp.where(depth == 2, jnp.where(normal == 2, 1.0, 0.0), 4.0 * half * half),
        ),
    )

    for copy in copies[2:]:
        copy.wait()
    first_slot = lax.axis_index("bricks") * count
    for b in range(count):
        face = jnp.where(near[normal, 1, first_slot + b] >= 0, edge - 1, 0)
        for q in range(2):
            x = 2 * b + q
            at = size * x
            swap_rows(solved, at, other, 0, edge)
            whole = dot(left_of(inverses[b, closed, q]), right_of(wide(other, 0, edge)))
            for c in range(tiles):
                other[pl.ds(edge * c, edge), :] = whole[:, LANES * c : LANES * (c + 1)]
            swap_rows(other, 0, work, 0, edge)
            base[pl.ds(at, size), :] = work[...]
            row_n = jnp.concatenate([inverses[b, normal, q, pl.ds(face, 1), :]] * 4, 1)
            edges[x, 0] = jnp.broadcast_to(inverses[b, 0, q, :, 0:1], (edge, LANES))
            edges[x, 1] = jnp.broadcast_to(inverses[b, 0, q, :, edge - 1 : edge], (edge, LANES))
            edges[x, 2] = jnp.broadcast_to(row_n, (edge, LANES))


def owner_kernel(recv, pick, flags, const, out):
    edge = const.shape[0]
    turned = const[:, : 6 * edge]
    basis = const[:, 2 * LANES : 2 * LANES + 6 * edge]
    lam, v_first, v_last = (const[:, LANES * x : LANES * (x + 1)] for x in (4, 5, 6))
    face, touch, normal_2, my_lam = flags[0:1], flags[1:2], flags[2:3], flags[3:4]

    hit = pick[...]
    data = jnp.concatenate([recv[pl.ds(x, edge, stride=ROWS), :] for x in range(4)], 0).T
    tail = recv[pl.ds(4, edge, stride=ROWS), :]
    tail = jnp.concatenate([tail] + [pltpu.roll(tail, LANES - edge * x, 1) for x in range(1, 4)], 0).T[:16]
    hits = jnp.concatenate([hit] * 3, 0)
    params = dot(exact_of(tail), hits)
    rate_0, rate_t, rate_n = params[0:1], params[1:2], params[2:3]
    parts = dot(exact_of(data), hits)
    y0, y1, face_u, face_y = (parts[edge * x : edge * (x + 1)] for x in range(4))

    lane = lane_of((1, LANES))
    place = lane & (edge - 1)
    first_row = (lane & edge) == 0

    def partner(x):
        return jnp.where(first_row, pltpu.roll(x, LANES - edge, 1), pltpu.roll(x, edge, 1))

    def after(x, s=1):
        return pltpu.roll(x, LANES - s, 1)

    def before(x, s=1):
        return pltpu.roll(x, s, 1)

    damp_0 = 1.0 / (1.0 + lam * rate_0)
    damp_n = 1.0 / (1.0 + lam * rate_n)
    damp_t = 1.0 / (1.0 + my_lam * rate_t)
    other_n = partner(rate_n)
    g = jnp.where(touch > 0.5, 2.0 * rate_n * other_n / (rate_n + other_n), 0.0)
    cross = partner(face_u) - face_u
    near_c = jnp.sum(damp_0 * v_first * v_first, 0, keepdims=True)
    far_c = jnp.sum(damp_0 * v_first * v_last, 0, keepdims=True)
    end_n = jnp.sum(damp_n * v_first * v_first, 0, keepdims=True)
    open_face = place < edge - 1
    right = jnp.where(open_face, y1 - after(y0), 0.0)
    both = dot(basis, right_of(jnp.concatenate([cross, right], 1)))
    damped = damp_0 * (2.0 * g) * both[:, :LANES]
    pieces = dot(turned, right_of(jnp.concatenate([damped, damp_0 * v_first, damp_0 * v_last], 1)))
    spread, col_0, col_1 = (pieces[:, LANES * x : LANES * (x + 1)] for x in range(3))
    v_face = jnp.where(face < 0.5, v_first, v_last)
    at_first = v_face * jnp.sum(v_first * damped, 0, keepdims=True)
    at_last = v_face * jnp.sum(v_last * damped, 0, keepdims=True)
    right = both[:, LANES:] + jnp.where(open_face, at_last - after(at_first), 0.0)

    inv_rate = 1.0 / rate_0
    diag = jnp.where(open_face, 0.5 * (inv_rate + after(inv_rate)) + near_c + after(near_c), 1.0)
    lower = jnp.where(open_face & (place > 0), -far_c, 0.0)
    upper = jnp.where(place < edge - 2, -after(far_c), 0.0)
    def shift(x, by):
        return x if by == 0 else pltpu.roll(x, -by % LANES, 1)

    def reduced(near_by, at, s):
        (dm, lm, um, rm), (d, l, u, r), (dp, lp, up, rp) = (near_by[at + x * s] for x in (-1, 0, 1))
        back, fore = -l / dm, -u / dp
        return d + back * um + fore * lp, back * lm, fore * up, r + back * rm + fore * rp

    system = (diag, lower, upper, right)
    step, total = 1, (edge - 1).bit_length()
    for levels in (3, total - 3):
        reach = 2**levels - 1
        rows_by = {x * step: tuple(shift(y, x * step) for y in system) for x in range(-reach, reach + 1)}
        for level in range(levels):
            reach = 2**levels - 2 ** (level + 1)
            now = step * 2**level
            rows_by = {
                x * step: reduced(rows_by, x * step, now)
                for x in range(-reach, reach + 1, 2 ** (level + 1))
            }
        system = rows_by[0]
        step *= 2**levels
    diag, lower, upper, right = system
    flux_up = right / diag
    flux_down = jnp.where(place > 0, before(flux_up), 0.0)

    weight_down = jnp.sum(damp_n * v_face * flux_down, 0, keepdims=True)
    weight_up = jnp.sum(damp_n * v_face * flux_up, 0, keepdims=True)
    ends = face_y + end_n * spread + col_0 * weight_down - col_1 * weight_up
    ends = jnp.where(normal_2 > 0.5, damp_t, 1.0) * ends
    jump = g / (1.0 + g * (end_n + partner(end_n))) * (ends - partner(ends))
    face_out = jnp.where(normal_2 > 0.5, damp_t * spread - jump, damp_t * (spread - jump))
    damp_nt = damp_n * damp_t
    lines = dot(turned, right_of(jnp.concatenate([damp_nt * flux_down, damp_nt * flux_up], 1)))
    packed = jnp.concatenate(
        [lines[:, :LANES], lines[:, LANES:], face_out, jnp.zeros((edge, LANES), jnp.float32)], 0
    )
    reply = dot_lanes(jnp.concatenate([hit] * 3, 1), exact_of(packed))
    kinds = swap_blocks([reply[edge * x : edge * (x + 1)] for x in range(4)])
    for x in range(3):
        out[pl.ds(x, edge, stride=3), :] = kinds[x]


def update_kernel(
    recv, base, edges, flags, calcium, buffer, const,
    calcium_out, buffer_out,
    calcium_next, buffer_next, work, sems,
):
    count, edge = calcium.shape[0], calcium.shape[1]
    tiles = edge // 4
    size = tiles * edge
    swapped = flags[2, 0] < 0.5
    old = jnp.where(flags[2:3] < 0.5, 0.0, 1.0)
    low, high, face_part = (recv[pl.ds(x, edge, stride=3), :] for x in range(3))
    parts = [part.astype(jnp.float32) for part in parts_of(face_part)]
    turn = jnp.concatenate([parts[p] for p in LEFT] + [jnp.zeros_like(parts[0])] * 2, 0)
    turn = turn.T[:, : 6 * edge]
    face_wide = dot(turn, const[:, 2 * LANES :].astype(jnp.float32))
    lines = dot(const[:edge, : 6 * edge].astype(jnp.float32), right_of(jnp.concatenate([low, high], 1)))
    rows = []
    for e in range(2):
        work[pl.ds(edge * e, edge), :] = lines[:, LANES * e : LANES * (e + 1)]
        rows.append(swap_blocks([work[pl.ds(edge * e + t4, tiles, stride=4), :] for t4 in range(4)]))

    stores = [
        pltpu.make_async_copy(source.at[b], to.at[b], sems.at[2 * b + q])
        for b in range(count)
        for q, (source, to) in enumerate(((calcium_next, calcium_out), (buffer_next, buffer_out)))
    ]
    for b in range(count):
        for q, (ref, now) in enumerate(((calcium_next, calcium), (buffer_next, buffer))):
            x = 2 * b + q
            at = size * x
            col_0, col_1, row_n = edges[x, 0], edges[x, 1], edges[x, 2]
            for c in range(tiles):
                part = slice(LANES * c, LANES * (c + 1))
                ref[b, :, part] = (
                    (base[pl.ds(at + edge * c, edge), :] + old * now[b, :, part])
                    + face_wide[edge * x : edge * (x + 1), part] * row_n
                    + (col_0 * rows[0][x][c : c + 1] - col_1 * rows[1][x][c : c + 1])
                )
            stores[x].start()
    for store in stores:
        store.wait()

    @pl.when(swapped)
    def _():
        swap_inner((calcium_next, buffer_next), edge)
        calcium_next[...] = calcium_next[...] + calcium[...]
        buffer_next[...] = buffer_next[...] + buffer[...]
        for store in stores:
            store.start()
        for store in stores:
            store.wait()


def fast_body(calcium, buffer, fraction, rates, inverses, neighbors, ranks):
    count, edge = calcium.shape[0], calcium.shape[1]
    devices = lax.axis_size("bricks")
    tiles = edge // 4
    size = tiles * edge
    f32 = jnp.float32
    basis, eigen = cosine_basis(edge)
    place = np.arange(edge)
    ends_of = np.zeros((edge, edge))
    ends_of[:, (place % 4) * tiles + place // 4] = basis
    faces_of = np.zeros((edge, LANES))
    faces_of[:, (place % 4) * edge + place // 4] = basis
    pad = lambda x: np.pad(x, ((0, 0), (0, 2 * LANES - x.shape[1])))
    message_const = np.concatenate([pad(host_left(ends_of)), host_left(faces_of)], 1)
    lanes_of = lambda x: np.tile(x[:, None], (1, LANES))
    owner_const = np.concatenate(
        [pad(host_left(basis.T)), pad(host_left(basis))]
        + [lanes_of(x) for x in (eigen, basis[:, 0], basis[:, -1])],
        1,
    )
    expand = host_right(np.repeat(basis, edge, 1))
    back_const = np.pad(pad(host_left(basis.T)), ((0, 5 * edge), (0, 0)))
    update_const = np.concatenate([back_const, expand], 1)
    smem = pl.BlockSpec(memory_space=pltpu.SMEM)
    vmem = pl.BlockSpec(memory_space=pltpu.VMEM)
    hbm = pl.BlockSpec(memory_space=pltpu.HBM)
    params = pltpu.CompilerParams(vmem_limit_bytes=48 * 2**20)
    const = lambda x: jnp.asarray(x, f32)
    field = jax.ShapeDtypeStruct(calcium.shape, f32)
    tall = jax.ShapeDtypeStruct((2 * count * size, LANES), f32)

    stay = lambda x: pltpu.with_memory_space_constraint(x, pltpu.HBM)
    msg, solved = pl.pallas_call(
        message_kernel,
        out_shape=(jax.ShapeDtypeStruct((devices * ROWS, LANES), f32), tall),
        in_specs=[hbm] * 7,
        out_specs=(vmem, vmem),
        scratch_shapes=[
            pltpu.SMEM(neighbors.shape, jnp.int32),
            pltpu.SMEM((count, 2, 3), f32),
            pltpu.VMEM(calcium.shape, f32),
            pltpu.VMEM(calcium.shape, f32),
            pltpu.VMEM(fraction.shape, f32),
            pltpu.VMEM(inverses.shape, f32),
            pltpu.VMEM(message_const.shape, jnp.bfloat16),
            pltpu.SemaphoreType.DMA((7,)),
        ],
        compiler_params=pltpu.CompilerParams(vmem_limit_bytes=48 * 2**20),
        name="message",
    )(*(stay(x) for x in (neighbors, rates.transpose(0, 2, 1), calcium, buffer, fraction, inverses, jnp.asarray(message_const, jnp.bfloat16))))
    recv = lax.all_to_all(msg.reshape(devices * ROWS, 1, LANES), "bricks", 0, 0, tiled=True).reshape(devices * ROWS, LANES)
    base, pick, flags, edges = pl.pallas_call(
        local_kernel,
        out_shape=(
            tall,
            jax.ShapeDtypeStruct((LANES, LANES), f32),
            jax.ShapeDtypeStruct((8, LANES), f32),
            jax.ShapeDtypeStruct((2 * count, 3, edge, LANES), f32),
        ),
        in_specs=[hbm] * 3,
        out_specs=(vmem,) * 4,
        scratch_shapes=[
            pltpu.SMEM(neighbors.shape, jnp.int32),
            pltpu.VMEM(neighbors.shape, jnp.int32),
            pltpu.VMEM(tall.shape, f32),
            pltpu.VMEM(inverses.shape, f32),
            pltpu.VMEM((size, LANES), f32),
            pltpu.VMEM((size, LANES), f32),
            pltpu.SemaphoreType.DMA((4,)),
        ],
        compiler_params=pltpu.CompilerParams(vmem_limit_bytes=48 * 2**20),
        cost_estimate=pl.CostEstimate(flops=2 * 10**7, bytes_accessed=4 * 10**6, transcendentals=0),
        name="local_solution",
    )(neighbors, solved, inverses)
    reply = pl.pallas_call(
        owner_kernel,
        out_shape=jax.ShapeDtypeStruct((devices * 3, LANES), f32),
        in_specs=[vmem] * 4,
        out_specs=vmem,
        compiler_params=params,
        name="chain_and_face_solves",
    )(recv, pick, flags, const(owner_const))
    back = lax.all_to_all(reply.reshape(devices * 3, 1, LANES), "bricks", 0, 0, tiled=True)
    return pl.pallas_call(
        update_kernel,
        out_shape=(field, field),
        in_specs=[vmem] * 7,
        out_specs=(hbm, hbm),
        scratch_shapes=[
            pltpu.VMEM(calcium.shape, f32),
            pltpu.VMEM(buffer.shape, f32),
            pltpu.VMEM((2 * edge, LANES), f32),
            pltpu.SemaphoreType.DMA((2 * count,)),
        ],
        compiler_params=params,
        name="rank_three_update",
    )(back.reshape(devices * 3, LANES), base, edges, flags, calcium, buffer, jnp.asarray(update_const, jnp.bfloat16))


def body(calcium, buffer, fraction, rates, inverses, neighbors, ranks):
    count, edge = calcium.shape[0], calcium.shape[1]
    devices = lax.axis_size("bricks")
    if edge == GX and devices == edge and count == 2 and 4 * edge == LANES:
        return fast_body(calcium, buffer, fraction, rates, inverses, neighbors, ranks)
    return general_body(calcium, buffer, fraction, rates, inverses, neighbors, ranks)


def solution(mesh):
    in_specs = (
        P("bricks", None, None),
        P("bricks", None, None),
        P("bricks", None, None),
        P("bricks", None, None),
        P("bricks", None, None, None, None),
        P(),
        P(),
    )
    out_specs = (P("bricks", None, None), P("bricks", None, None))
    return jax.shard_map(body, mesh=mesh, in_specs=in_specs, out_specs=out_specs, check_vma=False)
```

```python
from functools import partial
import math

import jax
import jax.numpy as jnp
import numpy as np
from jax import lax
from jax.experimental import pallas as pl
from jax.experimental.pallas import tpu as pltpu
from jax.sharding import PartitionSpec as P

GX = 32


KON = 0.5
KOFF = 0.3
BTOT = 2.0
INFLUX = 0.1


def fetch(table, index):
    rows = jnp.take(table, jnp.maximum(index, 0), axis=0)
    has = (index >= 0).reshape((-1,) + (1,) * (rows.ndim - 1))
    return jnp.where(has, rows, jnp.zeros_like(rows))


def lookup(planes, before, after):
    sides = []
    for d in range(3):
        lower = fetch(planes[:, d, 1], before[d])
        upper = fetch(planes[:, d, 0], after[d])
        sides.append(jnp.stack([lower, upper], 1))
    return jnp.stack(sides, 1)


def coupling(rate_all, neighbors):
    per_dim = []
    for d in range(3):
        mine = rate_all[:, d]
        sides = []
        for side in range(2):
            other = fetch(mine, neighbors[d, side])
            has = (neighbors[d, side] >= 0)[:, None]
            sides.append(jnp.where(has, 2.0 * mine * other / (mine + other), jnp.zeros_like(mine)))
        per_dim.append(jnp.stack(sides, 1))
    return jnp.stack(per_dim, 1)


def end_planes(field):
    count, edge = (field.shape[0], field.shape[2])
    per_dim = []
    for d in range(3):
        first = lax.index_in_dim(field, 0, 2 + d, False).reshape(count, 2, edge * edge)
        last = lax.index_in_dim(field, edge - 1, 2 + d, False).reshape(count, 2, edge * edge)
        per_dim.append(jnp.stack([first, last], 1))
    return jnp.stack(per_dim, 1)


def operator(field, d, rate, glow, gup, hlow, hup):
    axis = 2 + d
    edge = field.shape[axis]
    plane_shape = lax.index_in_dim(field, 0, axis, False).shape
    lower_face = jnp.expand_dims(hlow.reshape(plane_shape), axis)
    upper_face = jnp.expand_dims(hup.reshape(plane_shape), axis)
    upper = jnp.concatenate([lax.slice_in_dim(field, 1, edge, axis=axis), upper_face], axis)
    lower = jnp.concatenate([lower_face, lax.slice_in_dim(field, 0, edge - 1, axis=axis)], axis)
    place = lax.broadcasted_iota(jnp.int32, field.shape, axis)
    inner = rate[:, :, None, None, None]
    c_up = jnp.where(place == edge - 1, gup[:, :, None, None, None], inner)
    c_down = jnp.where(place == 0, glow[:, :, None, None, None], inner)
    return c_up * (upper - field) + c_down * (lower - field)


def reaction(field, fraction):
    count, edge = (field.shape[0], field.shape[2])
    alpha = fraction.reshape(count, edge, edge, edge)
    calc, bound = (field[:, 0], field[:, 1])
    bind = KON * calc * (BTOT - bound) - KOFF * bound
    return jnp.stack([-bind + INFLUX * (1.0 - alpha) / alpha, bind], 1)


def apply_inverse(block, field, d):
    forms = ["psab,psbjk->psajk", "psab,psibk->psiak", "psab,psijb->psija"]
    return jnp.einsum(forms[d], block, field, precision=lax.Precision.HIGHEST)


def line_ends(field, d):
    count, edge = (field.shape[0], field.shape[2])
    first = lax.index_in_dim(field, 0, 2 + d, False).reshape(count, 2, edge * edge)
    last = lax.index_in_dim(field, edge - 1, 2 + d, False).reshape(count, 2, edge * edge)
    return jnp.stack([first, last], 2)


def block_terms(glow, gup, corner):
    v_first, v_last, w_first, w_last = (
        corner[..., 0],
        corner[..., 1],
        corner[..., 2],
        corner[..., 3],
    )
    a00 = 1.0 + glow * v_first
    a01 = gup * w_first
    a10 = glow * v_last
    a11 = 1.0 + gup * w_last
    lq0 = -glow * v_first
    lq1 = -glow * v_last
    up0 = -gup * w_first
    up1 = -gup * w_last
    return (a00, a01, a10, a11, lq0, lq1, up0, up1)


def chain_order(before, rank):
    slots = jnp.arange(before.shape[0], dtype=jnp.int32)
    pointer = jnp.where(before >= 0, before, slots)
    for step in range(GX.bit_length()):
        pointer = jnp.take(pointer, pointer, axis=0)
    sort_key = pointer * GX + rank
    order = jnp.argsort(sort_key)
    inverse_order = jnp.argsort(order)
    return (order, inverse_order)


def shift_down(values):
    return jnp.concatenate([jnp.zeros_like(values[:1]), values[:-1]], 0)


def shift_up(values):
    return jnp.concatenate([values[1:], jnp.zeros_like(values[:1])], 0)


def compose_maps(first_map, second_map):
    e00, e01, e10, e11 = first_map
    l00, l01, l10, l11 = second_map
    n00 = l00 * e00 + l01 * e10
    n01 = l00 * e01 + l01 * e11
    n10 = l10 * e00 + l11 * e10
    n11 = l10 * e01 + l11 * e11
    scale = jnp.abs(n00) + jnp.abs(n01) + jnp.abs(n10) + jnp.abs(n11)
    return (n00 / scale, n01 / scale, n10 / scale, n11 / scale)


def compose_affine(first_map, second_map):
    first_q, first_p = first_map
    second_q, second_p = second_map
    return (first_q * second_q, second_p + second_q * first_p)


def sorted_solve(glow, gup, corner, before, after, order, inverse_order, ends):
    glow = jnp.take(glow, order, axis=0)
    gup = jnp.take(gup, order, axis=0)
    corner = jnp.take(corner, order, axis=0)
    has_b = jnp.take(before, order, axis=0) >= 0
    has_a = jnp.take(after, order, axis=0) >= 0
    arranged = jnp.take(ends, order, axis=0)
    y0 = arranged[:, :, 0]
    y1 = arranged[:, :, 1]
    a00, a01, a10, a11, lq0, lq1, up0, up1 = block_terms(glow, gup, corner)
    maps = (
        -(lq0 * up1 - lq1 * up0),
        a00 * up1 - a10 * up0,
        -(lq0 * a11 - a01 * lq1),
        a00 * a11 - a01 * a10,
    )
    summed = lax.associative_scan(compose_maps, maps, axis=0)
    f1_prev = summed[1] / summed[3]
    fq = shift_down(f1_prev)
    b00 = a00 - lq0 * fq
    b10 = a10 - lq1 * fq
    det = b00 * a11 - a01 * b10
    f0 = (a11 * up0 - a01 * up1) / det
    f1 = (b00 * up1 - b10 * up0) / det
    slope = (-(b00 * lq1 - b10 * lq0) / det)[:, :, None]
    offset = (b00[:, :, None] * y1 - b10[:, :, None] * y0) / det[:, :, None]
    e1 = lax.associative_scan(compose_affine, (slope, offset), axis=0)[1]
    eq = shift_down(e1)
    e0 = (
        a11[:, :, None] * y0 - a01[:, :, None] * y1 - (a11 * lq0 - a01 * lq1)[:, :, None] * eq
    ) / det[:, :, None]
    zp = lax.associative_scan(compose_affine, (-f0[:, :, None], e0), reverse=True, axis=0)[1]
    pn = shift_up(zp)
    zq = e1 - f1[:, :, None] * pn
    low = jnp.where(has_b[:, None, None], zp - shift_down(zq), jnp.zeros_like(zp))
    high = jnp.where(has_a[:, None, None], zq - pn, jnp.zeros_like(zq))
    return jnp.take(jnp.stack([low, high], 2), inverse_order, axis=0)


def correct(local, block, glow, gup, jumps, d):
    axis = 2 + d
    count, edge = (local.shape[0], local.shape[2])
    shape_v = [count, 2, 1, 1, 1]
    shape_v[axis] = edge
    first_col = block[..., 0].reshape(shape_v)
    last_col = block[..., edge - 1].reshape(shape_v)
    plane_shape = lax.index_in_dim(local, 0, axis, False).shape
    low = jnp.expand_dims(jumps[:, :, 0].reshape(plane_shape), axis)
    high = jnp.expand_dims(jumps[:, :, 1].reshape(plane_shape), axis)
    return (
        local
        - glow[:, :, None, None, None] * low * first_col
        - gup[:, :, None, None, None] * high * last_col
    )


def general_body(calcium, buffer, fraction, rates, inverses, neighbors, ranks):
    count, edge = (calcium.shape[0], calcium.shape[1])
    devices = lax.axis_size("bricks")
    square = edge * edge
    per_device = square // devices
    start = lax.axis_index("bricks") * count
    corners = jnp.stack(
        [
            inverses[..., 0, 0],
            inverses[..., edge - 1, 0],
            inverses[..., 0, edge - 1],
            inverses[..., edge - 1, edge - 1],
        ],
        -1,
    )
    rate_all, corner_all = (
        lax.all_gather(rates, "bricks", axis=0, tiled=True),
        lax.all_gather(corners, "bricks", axis=0, tiled=True),
    )
    couple_all = coupling(rate_all, neighbors)
    couple = lax.dynamic_slice_in_dim(couple_all, start, count, 0)
    field = jnp.stack([calcium, buffer], 1).reshape(count, 2, edge, edge, edge)
    planes = end_planes(field).reshape(count, 3, 2, 2, devices, per_device)
    lined = lookup(
        lax.all_to_all(planes, "bricks", split_axis=4, concat_axis=0, tiled=True),
        neighbors[:, 0],
        neighbors[:, 1],
    )
    halos = lax.all_to_all(lined, "bricks", split_axis=0, concat_axis=4, tiled=True).reshape(
        count, 3, 2, 2, square
    )
    lams = [
        operator(
            field, d, rates[:, d], couple[:, d, 0], couple[:, d, 1], halos[:, d, 0], halos[:, d, 1]
        )
        for d in range(3)
    ]
    rhs = field + lams[0] + 2.0 * lams[1] + 2.0 * lams[2] + reaction(field, fraction)

    def solve(right, d):
        block = inverses[:, d]
        local = apply_inverse(block, right, d)
        ends = line_ends(local, d).reshape(count, 2, 2, devices, per_device)
        order, inverse_order = chain_order(neighbors[d, 0], ranks[d])
        chain_fn = partial(
            sorted_solve,
            couple_all[:, d, 0],
            couple_all[:, d, 1],
            corner_all[:, d],
            neighbors[d, 0],
            neighbors[d, 1],
            order,
            inverse_order,
        )
        lined_jumps = chain_fn(
            lax.all_to_all(ends, "bricks", split_axis=3, concat_axis=0, tiled=True)[:, :, :, 0]
        )[:, :, :, None]
        jumps = lax.all_to_all(
            lined_jumps, "bricks", split_axis=0, concat_axis=3, tiled=True
        ).reshape(count, 2, 2, square)
        return correct(local, block, couple[:, d, 0], couple[:, d, 1], jumps, d)

    first = solve(rhs, 0)
    second = solve(first - lams[1], 1)
    third = solve(second - lams[2], 2)
    result = third.reshape(count, 2, edge, edge * edge)
    return (result[:, 0], result[:, 1])


LANES = 128


ROWS = 5


def cosine_basis(edge):
    wave = np.arange(edge)[:, None]
    place = np.arange(edge)[None, :]
    basis = np.sqrt(2.0 / edge) * np.cos(np.pi * wave * (place + 0.5) / edge)
    basis[0] = math.sqrt(1.0 / edge)
    eigen = 2.0 - 2.0 * np.cos(np.pi * np.arange(edge) / edge)
    return basis, eigen


def parts_of(x):
    high = x.astype(jnp.bfloat16).astype(jnp.float32)
    rest = x - high
    middle = rest.astype(jnp.bfloat16).astype(jnp.float32)
    return high, middle, rest - middle


LEFT = (0, 0, 0, 1, 1, 2)
RIGHT = (0, 1, 2, 0, 1, 0)


def left_of(x):
    parts = parts_of(x)
    return jnp.concatenate([parts[p] for p in LEFT], 1)


def right_of(x, axis=0):
    parts = parts_of(x)
    return jnp.concatenate([parts[p] for p in RIGHT], axis)


def exact_of(x):
    return jnp.concatenate(parts_of(x), 1)


def dot(a, b):
    return jnp.dot(a, b, preferred_element_type=jnp.float32)


def dot_lanes(a, b):
    return lax.dot_general(a, b, (((1,), (1,)), ((), ())), preferred_element_type=jnp.float32)


def host_parts(x):
    parts = []
    for _ in range(3):
        parts.append(x.astype(jnp.bfloat16).astype(np.float64))
        x = x - parts[-1]
    return parts


def host_left(x):
    parts = host_parts(x)
    return np.concatenate([parts[p] for p in LEFT], 1)


def host_right(x):
    parts = host_parts(x)
    return np.concatenate([parts[p] for p in RIGHT], 0)


def lane_of(shape):
    return lax.broadcasted_iota(jnp.int32, shape, len(shape) - 1)


def swap_blocks(four):
    x0, x1, x2, x3 = four
    lane = lane_of(x0.shape)
    low = (lane & 64) == 0
    y0, y2 = jnp.where(low, x0, pltpu.roll(x2, 64, 1)), jnp.where(low, pltpu.roll(x0, 64, 1), x2)
    y1, y3 = jnp.where(low, x1, pltpu.roll(x3, 64, 1)), jnp.where(low, pltpu.roll(x1, 64, 1), x3)
    even = (lane & 32) == 0
    z0, z1 = jnp.where(even, y0, pltpu.roll(y1, 32, 1)), jnp.where(even, pltpu.roll(y0, 96, 1), y1)
    z2, z3 = jnp.where(even, y2, pltpu.roll(y3, 32, 1)), jnp.where(even, pltpu.roll(y2, 96, 1), y3)
    return [z0, z1, z2, z3]


def swap_rows(source, base, scratch, at, edge):
    tiles = edge // 4
    for c in range(tiles):
        rows = [source[pl.ds(base + edge * c + g, tiles, stride=4), :] for g in range(4)]
        for t4, row in enumerate(swap_blocks(rows)):
            scratch[pl.ds(at + 4 * c + t4, tiles, stride=edge), :] = row


def tile_rows(x, edge):
    tiles = edge // 4
    return jnp.concatenate([x[:, LANES * c : LANES * (c + 1)] for c in range(tiles)], 0)


def wide(ref, at, edge):
    tiles = edge // 4
    return jnp.concatenate([ref[pl.ds(at + edge * c, edge), :] for c in range(tiles)], 1)


def swap_inner(refs, edge):
    tiles = edge // 4
    fields = [(ref, b) for ref in refs for b in range(ref.shape[0])]
    whole = [
        exact_of(jnp.concatenate([ref[b, :, LANES * c : LANES * (c + 1)] for ref, b in fields], 0))
        for c in range(tiles)
    ]
    row = lax.broadcasted_iota(jnp.int32, (LANES, LANES), 0)
    lane = lane_of((LANES, LANES))
    for to in range(tiles):
        total = jnp.zeros((len(fields) * edge, LANES), jnp.float32)
        for c in range(tiles):
            hit = ((row & (edge - 1)) == 4 * to + lane // edge) & ((lane & (edge - 1)) == 4 * c + row // edge)
            hit = hit.astype(jnp.float32)
            total = total + dot(whole[c], jnp.concatenate([hit] * 3, 0))
        for f, (ref, b) in enumerate(fields):
            ref[b, :, LANES * to : LANES * (to + 1)] = total[edge * f : edge * (f + 1)]


def normal_of(near, slot):
    along_j = (near[1, 0, slot] >= 0) | (near[1, 1, slot] >= 0)
    return jnp.where(along_j, 1, 2)


def message_kernel(
    near_in, rates_in, calcium_in, buffer_in, fraction_in, inverses_in, const_in,
    msg, solved,
    near, rates, calcium, buffer, fraction, inverses, const, sems,
):
    count, edge = calcium.shape[0], calcium.shape[1]
    tiles = edge // 4
    size = tiles * edge
    copies = [
        pltpu.make_async_copy(source, target, sems.at[x])
        for x, (source, target) in enumerate(
            (
                (near_in, near),
                (rates_in, rates),
                (calcium_in, calcium),
                (buffer_in, buffer),
                (fraction_in, fraction),
                (inverses_in, inverses),
                (const_in, const),
            )
        )
    ]
    for copy in copies:
        copy.start()
    first_slot = lax.axis_index("bricks") * count
    for copy in copies:
        copy.wait()
    normal = normal_of(near, first_slot)
    closed = 3 - normal

    @pl.when(normal == 1)
    def _():
        swap_inner((calcium, buffer, fraction), edge)

    lane = lane_of((edge, LANES))
    inner = lane & (edge - 1)
    square_row = lax.broadcasted_iota(jnp.int32, (LANES, LANES), 0)
    square_lane = lane_of((LANES, LANES))
    on_block = (square_row // edge) == (square_lane // edge)
    faces_u, faces_y, ends0, ends1 = [], [], [], []
    for b in range(count):
        face = jnp.where(near[normal, 1, first_slot + b] >= 0, edge - 1, 0)
        calc = [calcium[b, :, LANES * c : LANES * (c + 1)] for c in range(tiles)]
        bound = [buffer[b, :, LANES * c : LANES * (c + 1)] for c in range(tiles)]
        alpha = [fraction[b, :, LANES * c : LANES * (c + 1)] for c in range(tiles)]
        bind = [KON * x * (BTOT - y) - KOFF * y for x, y in zip(calc, bound)]
        source_calc = [INFLUX / a - (w + INFLUX) for w, a in zip(bind, alpha)]
        for q, (u, source) in enumerate(((calc, source_calc), (bound, bind))):
            at = size * (2 * b + q)
            rate_t, rate_n = 2.0 * rates[b, q, closed], 2.0 * rates[b, q, normal]
            ahead = [pltpu.roll(x, LANES - edge, 1) for x in u]
            behind = [pltpu.roll(x, edge, 1) for x in u]
            f = []
            for c in range(tiles):
                x = u[c]
                next_t = jnp.where(lane < LANES - edge, ahead[c], ahead[c + 1] if c + 1 < tiles else x)
                last_t = jnp.where(lane >= edge, behind[c], behind[c - 1] if c else x)
                next_n = jnp.where(inner == edge - 1, x, pltpu.roll(x, LANES - 1, 1))
                last_n = jnp.where(inner == 0, x, pltpu.roll(x, 1, 1))
                twice = x + x
                along = rate_t * (next_t + last_t - twice) + rate_n * (next_n + last_n - twice)
                f.append(twice + along + source[c])
            g = dot(left_of(inverses[b, 0, q]), right_of(jnp.concatenate(f, 1)))
            ends0.append(jnp.concatenate([g[0:1, LANES * c : LANES * (c + 1)] for c in range(tiles)], 0))
            ends1.append(jnp.concatenate([g[edge - 1 : edge, LANES * c : LANES * (c + 1)] for c in range(tiles)], 0))
            w = jnp.concatenate([g[:, LANES * c : LANES * (c + 1)] - 2.0 * u[c] for c in range(tiles)], 0)
            sides = [
                jnp.where(on_block, jnp.concatenate([jnp.concatenate([x.astype(jnp.float32)] * 4, 1)] * 4, 0), 0.0)
                for x in parts_of(inverses[b, normal, q])
            ]
            y = dot(right_of(w, 1), jnp.concatenate([sides[p] for p in LEFT], 0))
            solved[pl.ds(at, size), :] = y
            face_u = jnp.zeros((edge, LANES), jnp.float32)
            face_y = jnp.zeros((edge, LANES), jnp.float32)
            for c in range(tiles):
                shift = (c - face) & (LANES - 1)
                face_u = jnp.where(inner == c, pltpu.roll(u[c], shift, 1), face_u)
                face_y = jnp.where(inner == c, pltpu.roll(y[edge * c : edge * (c + 1)], shift, 1), face_y)
            faces_u.append(face_u)
            faces_y.append(face_y)

    stack = jnp.concatenate(swap_blocks(ends0) + swap_blocks(ends1), 0)
    ends_of = const[:, : 6 * edge].astype(jnp.float32)
    faces_of = const[:, 2 * LANES :].astype(jnp.float32)
    both = dot(ends_of, right_of(jnp.concatenate([stack[:edge], stack[edge:]], 1)))
    part_u = dot_lanes(faces_of, right_of(jnp.concatenate(faces_u, 0), 1))
    part_y = dot_lanes(faces_of, right_of(jnp.concatenate(faces_y, 0), 1))
    fields = swap_blocks([both[:, :LANES], both[:, LANES:], part_u, part_y])
    for x, part in enumerate(fields):
        msg[pl.ds(x, edge, stride=ROWS), :] = part
    row = jnp.zeros((edge, LANES), jnp.float32)
    for b in range(count):
        for q in range(2):
            for x, rate in enumerate((rates[b, q, 0], rates[b, q, closed], rates[b, q, normal])):
                row = jnp.where(lane == (2 * b + q) * edge + x, rate, row)
    msg[pl.ds(4, edge, stride=ROWS), :] = row


def local_kernel(
    near_in, solved_in, inverses_in,
    base, pick, flags, edges,
    near, table, solved, inverses, work, other, sems,
):
    count, edge = inverses.shape[0], inverses.shape[3]
    tiles = edge // 4
    size = tiles * edge
    slots = near.shape[2]
    copies = [
        pltpu.make_async_copy(source, target, sems.at[x])
        for x, (source, target) in enumerate(
            (
                (near_in, near),
                (near_in, table),
                (solved_in, solved),
                (inverses_in, inverses),
            )
        )
    ]
    for copy in copies:
        copy.start()
    for copy in copies[:2]:
        copy.wait()
    normal = normal_of(near, 0)
    closed = 3 - normal
    up = near[normal, 1, 0] >= 0
    touch = up | (near[normal, 0, 0] >= 0)

    lane = lane_of((8, LANES))
    back = jnp.broadcast_to(table[0, 0:1, :], (8, slots))
    back = jnp.concatenate([back] * (LANES // slots), 1)
    pointer = jnp.where(back >= 0, back, lane & (slots - 1))
    place = jnp.where(back >= 0, 1, 0)

    def pull(values, index):
        return jnp.take_along_axis(values, index, axis=1, mode="promise_in_bounds")

    reach = 1
    while reach < edge:
        place = place + pull(place, pointer)
        pointer = pull(pointer, pointer)
        reach *= 2
    chain = jnp.where(pointer == pointer[:, 0:1], 0, edge) + place
    goal = pull(chain, (lane & (edge - 1)) * count + lane // (2 * edge)) + 2 * (lane & edge)
    hit = lax.broadcasted_iota(jnp.int32, (LANES, LANES), 0) == goal[0:1]
    pick[...] = hit.astype(jnp.float32).T
    face = jnp.where(((lane & edge) == 0) == up, edge - 1, 0).astype(jnp.float32)
    depth = lax.broadcasted_iota(jnp.int32, (8, LANES), 0)
    angle = jnp.full((8, LANES), lax.axis_index("bricks")).astype(jnp.float32) * (0.5 * math.pi / edge)
    half = jnp.sin(angle)
    flags[...] = jnp.where(
        depth == 0,
        face,
        jnp.where(
            depth == 1,
            jnp.where(touch, 1.0, 0.0),
            jnp.where(depth == 2, jnp.where(normal == 2, 1.0, 0.0), 4.0 * half * half),
        ),
    )

    for copy in copies[2:]:
        copy.wait()
    first_slot = lax.axis_index("bricks") * count
    for b in range(count):
        face = jnp.where(near[normal, 1, first_slot + b] >= 0, edge - 1, 0)
        for q in range(2):
            x = 2 * b + q
            at = size * x
            swap_rows(solved, at, other, 0, edge)
            whole = dot(left_of(inverses[b, closed, q]), right_of(wide(other, 0, edge)))
            for c in range(tiles):
                other[pl.ds(edge * c, edge), :] = whole[:, LANES * c : LANES * (c + 1)]
            swap_rows(other, 0, work, 0, edge)
            base[pl.ds(at, size), :] = work[...]
            row_n = jnp.concatenate([inverses[b, normal, q, pl.ds(face, 1), :]] * 4, 1)
            edges[x, 0] = jnp.broadcast_to(inverses[b, 0, q, :, 0:1], (edge, LANES))
            edges[x, 1] = jnp.broadcast_to(inverses[b, 0, q, :, edge - 1 : edge], (edge, LANES))
            edges[x, 2] = jnp.broadcast_to(row_n, (edge, LANES))


def owner_kernel(recv, pick, flags, const, out):
    edge = const.shape[0]
    turned = const[:, : 6 * edge]
    basis = const[:, 2 * LANES : 2 * LANES + 6 * edge]
    lam, v_first, v_last = (const[:, LANES * x : LANES * (x + 1)] for x in (4, 5, 6))
    face, touch, normal_2, my_lam = flags[0:1], flags[1:2], flags[2:3], flags[3:4]

    hit = pick[...]
    data = jnp.concatenate([recv[pl.ds(x, edge, stride=ROWS), :] for x in range(4)], 0).T
    tail = recv[pl.ds(4, edge, stride=ROWS), :]
    tail = jnp.concatenate([tail] + [pltpu.roll(tail, LANES - edge * x, 1) for x in range(1, 4)], 0).T[:16]
    hits = jnp.concatenate([hit] * 3, 0)
    params = dot(exact_of(tail), hits)
    rate_0, rate_t, rate_n = params[0:1], params[1:2], params[2:3]
    parts = dot(exact_of(data), hits)
    y0, y1, face_u, face_y = (parts[edge * x : edge * (x + 1)] for x in range(4))

    lane = lane_of((1, LANES))
    place = lane & (edge - 1)
    first_row = (lane & edge) == 0

    def partner(x):
        return jnp.where(first_row, pltpu.roll(x, LANES - edge, 1), pltpu.roll(x, edge, 1))

    def after(x, s=1):
        return pltpu.roll(x, LANES - s, 1)

    def before(x, s=1):
        return pltpu.roll(x, s, 1)

    damp_0 = 1.0 / (1.0 + lam * rate_0)
    damp_n = 1.0 / (1.0 + lam * rate_n)
    damp_t = 1.0 / (1.0 + my_lam * rate_t)
    other_n = partner(rate_n)
    g = jnp.where(touch > 0.5, 2.0 * rate_n * other_n / (rate_n + other_n), 0.0)
    cross = partner(face_u) - face_u
    near_c = jnp.sum(damp_0 * v_first * v_first, 0, keepdims=True)
    far_c = jnp.sum(damp_0 * v_first * v_last, 0, keepdims=True)
    end_n = jnp.sum(damp_n * v_first * v_first, 0, keepdims=True)
    open_face = place < edge - 1
    right = jnp.where(open_face, y1 - after(y0), 0.0)
    both = dot(basis, right_of(jnp.concatenate([cross, right], 1)))
    damped = damp_0 * (2.0 * g) * both[:, :LANES]
    pieces = dot(turned, right_of(jnp.concatenate([damped, damp_0 * v_first, damp_0 * v_last], 1)))
    spread, col_0, col_1 = (pieces[:, LANES * x : LANES * (x + 1)] for x in range(3))
    v_face = jnp.where(face < 0.5, v_first, v_last)
    at_first = v_face * jnp.sum(v_first * damped, 0, keepdims=True)
    at_last = v_face * jnp.sum(v_last * damped, 0, keepdims=True)
    right = both[:, LANES:] + jnp.where(open_face, at_last - after(at_first), 0.0)

    inv_rate = 1.0 / rate_0
    diag = jnp.where(open_face, 0.5 * (inv_rate + after(inv_rate)) + near_c + after(near_c), 1.0)
    lower = jnp.where(open_face & (place > 0), -far_c, 0.0)
    upper = jnp.where(place < edge - 2, -after(far_c), 0.0)
    def shift(x, by):
        return x if by == 0 else pltpu.roll(x, -by % LANES, 1)

    def reduced(near_by, at, s):
        (dm, lm, um, rm), (d, l, u, r), (dp, lp, up, rp) = (near_by[at + x * s] for x in (-1, 0, 1))
        back, fore = -l / dm, -u / dp
        return d + back * um + fore * lp, back * lm, fore * up, r + back * rm + fore * rp

    system = (diag, lower, upper, right)
    step, total = 1, (edge - 1).bit_length()
    for levels in (3, total - 3):
        reach = 2**levels - 1
        rows_by = {x * step: tuple(shift(y, x * step) for y in system) for x in range(-reach, reach + 1)}
        for level in range(levels):
            reach = 2**levels - 2 ** (level + 1)
            now = step * 2**level
            rows_by = {
                x * step: reduced(rows_by, x * step, now)
                for x in range(-reach, reach + 1, 2 ** (level + 1))
            }
        system = rows_by[0]
        step *= 2**levels
    diag, lower, upper, right = system
    flux_up = right / diag
    flux_down = jnp.where(place > 0, before(flux_up), 0.0)

    weight_down = jnp.sum(damp_n * v_face * flux_down, 0, keepdims=True)
    weight_up = jnp.sum(damp_n * v_face * flux_up, 0, keepdims=True)
    ends = face_y + end_n * spread + col_0 * weight_down - col_1 * weight_up
    ends = jnp.where(normal_2 > 0.5, damp_t, 1.0) * ends
    jump = g / (1.0 + g * (end_n + partner(end_n))) * (ends - partner(ends))
    face_out = jnp.where(normal_2 > 0.5, damp_t * spread - jump, damp_t * (spread - jump))
    damp_nt = damp_n * damp_t
    lines = dot(turned, right_of(jnp.concatenate([damp_nt * flux_down, damp_nt * flux_up], 1)))
    packed = jnp.concatenate(
        [lines[:, :LANES], lines[:, LANES:], face_out, jnp.zeros((edge, LANES), jnp.float32)], 0
    )
    reply = dot_lanes(jnp.concatenate([hit] * 3, 1), exact_of(packed))
    kinds = swap_blocks([reply[edge * x : edge * (x + 1)] for x in range(4)])
    for x in range(3):
        out[pl.ds(x, edge, stride=3), :] = kinds[x]


def update_kernel(
    recv, base, edges, flags, calcium, buffer, const,
    calcium_out, buffer_out,
    calcium_next, buffer_next, work, sems,
):
    count, edge = calcium.shape[0], calcium.shape[1]
    tiles = edge // 4
    size = tiles * edge
    swapped = flags[2, 0] < 0.5
    old = jnp.where(flags[2:3] < 0.5, 0.0, 1.0)
    low, high, face_part = (recv[pl.ds(x, edge, stride=3), :] for x in range(3))
    parts = [part.astype(jnp.float32) for part in parts_of(face_part)]
    turn = jnp.concatenate([parts[p] for p in LEFT] + [jnp.zeros_like(parts[0])] * 2, 0)
    turn = turn.T[:, : 6 * edge]
    face_wide = dot(turn, const[:, 2 * LANES :].astype(jnp.float32))
    lines = dot(const[:edge, : 6 * edge].astype(jnp.float32), right_of(jnp.concatenate([low, high], 1)))
    rows = []
    for e in range(2):
        work[pl.ds(edge * e, edge), :] = lines[:, LANES * e : LANES * (e + 1)]
        rows.append(swap_blocks([work[pl.ds(edge * e + t4, tiles, stride=4), :] for t4 in range(4)]))

    stores = [
        pltpu.make_async_copy(source.at[b], to.at[b], sems.at[2 * b + q])
        for b in range(count)
        for q, (source, to) in enumerate(((calcium_next, calcium_out), (buffer_next, buffer_out)))
    ]
    for b in range(count):
        for q, (ref, now) in enumerate(((calcium_next, calcium), (buffer_next, buffer))):
            x = 2 * b + q
            at = size * x
            col_0, col_1, row_n = edges[x, 0], edges[x, 1], edges[x, 2]
            for c in range(tiles):
                part = slice(LANES * c, LANES * (c + 1))
                ref[b, :, part] = (
                    (base[pl.ds(at + edge * c, edge), :] + old * now[b, :, part])
                    + face_wide[edge * x : edge * (x + 1), part] * row_n
                    + (col_0 * rows[0][x][c : c + 1] - col_1 * rows[1][x][c : c + 1])
                )
        stores[2 * b].start()
        stores[2 * b + 1].start()
    for store in stores:
        store.wait()

    @pl.when(swapped)
    def _():
        swap_inner((calcium_next, buffer_next), edge)
        calcium_next[...] = calcium_next[...] + calcium[...]
        buffer_next[...] = buffer_next[...] + buffer[...]
        for store in stores:
            store.start()
        for store in stores:
            store.wait()


def fast_body(calcium, buffer, fraction, rates, inverses, neighbors, ranks):
    count, edge = calcium.shape[0], calcium.shape[1]
    devices = lax.axis_size("bricks")
    tiles = edge // 4
    size = tiles * edge
    f32 = jnp.float32
    basis, eigen = cosine_basis(edge)
    place = np.arange(edge)
    ends_of = np.zeros((edge, edge))
    ends_of[:, (place % 4) * tiles + place // 4] = basis
    faces_of = np.zeros((edge, LANES))
    faces_of[:, (place % 4) * edge + place // 4] = basis
    pad = lambda x: np.pad(x, ((0, 0), (0, 2 * LANES - x.shape[1])))
    message_const = np.concatenate([pad(host_left(ends_of)), host_left(faces_of)], 1)
    lanes_of = lambda x: np.tile(x[:, None], (1, LANES))
    owner_const = np.concatenate(
        [pad(host_left(basis.T)), pad(host_left(basis))]
        + [lanes_of(x) for x in (eigen, basis[:, 0], basis[:, -1])],
        1,
    )
    expand = host_right(np.repeat(basis, edge, 1))
    back_const = np.pad(pad(host_left(basis.T)), ((0, 5 * edge), (0, 0)))
    update_const = np.concatenate([back_const, expand], 1)
    smem = pl.BlockSpec(memory_space=pltpu.SMEM)
    vmem = pl.BlockSpec(memory_space=pltpu.VMEM)
    hbm = pl.BlockSpec(memory_space=pltpu.HBM)
    params = pltpu.CompilerParams(vmem_limit_bytes=48 * 2**20)
    const = lambda x: jnp.asarray(x, f32)
    field = jax.ShapeDtypeStruct(calcium.shape, f32)
    tall = jax.ShapeDtypeStruct((2 * count * size, LANES), f32)

    stay = lambda x: pltpu.with_memory_space_constraint(x, pltpu.HBM)
    msg, solved = pl.pallas_call(
        message_kernel,
        out_shape=(jax.ShapeDtypeStruct((devices * ROWS, LANES), f32), tall),
        in_specs=[hbm] * 7,
        out_specs=(vmem, vmem),
        scratch_shapes=[
            pltpu.SMEM(neighbors.shape, jnp.int32),
            pltpu.SMEM((count, 2, 3), f32),
            pltpu.VMEM(calcium.shape, f32),
            pltpu.VMEM(calcium.shape, f32),
            pltpu.VMEM(fraction.shape, f32),
            pltpu.VMEM(inverses.shape, f32),
            pltpu.VMEM(message_const.shape, jnp.bfloat16),
            pltpu.SemaphoreType.DMA((7,)),
        ],
        compiler_params=pltpu.CompilerParams(vmem_limit_bytes=48 * 2**20),
        name="message",
    )(*(stay(x) for x in (neighbors, rates.transpose(0, 2, 1), calcium, buffer, fraction, inverses, jnp.asarray(message_const, jnp.bfloat16))))
    recv = lax.all_to_all(msg.reshape(devices * ROWS, 1, LANES), "bricks", 0, 0, tiled=True).reshape(devices * ROWS, LANES)
    base, pick, flags, edges = pl.pallas_call(
        local_kernel,
        out_shape=(
            tall,
            jax.ShapeDtypeStruct((LANES, LANES), f32),
            jax.ShapeDtypeStruct((8, LANES), f32),
            jax.ShapeDtypeStruct((2 * count, 3, edge, LANES), f32),
        ),
        in_specs=[hbm] * 3,
        out_specs=(vmem,) * 4,
        scratch_shapes=[
            pltpu.SMEM(neighbors.shape, jnp.int32),
            pltpu.VMEM(neighbors.shape, jnp.int32),
            pltpu.VMEM(tall.shape, f32),
            pltpu.VMEM(inverses.shape, f32),
            pltpu.VMEM((size, LANES), f32),
            pltpu.VMEM((size, LANES), f32),
            pltpu.SemaphoreType.DMA((4,)),
        ],
        compiler_params=pltpu.CompilerParams(vmem_limit_bytes=48 * 2**20),
        cost_estimate=pl.CostEstimate(flops=2 * 10**7, bytes_accessed=4 * 10**6, transcendentals=0),
        name="local_solution",
    )(neighbors, solved, inverses)
    reply = pl.pallas_call(
        owner_kernel,
        out_shape=jax.ShapeDtypeStruct((devices * 3, LANES), f32),
        in_specs=[vmem] * 4,
        out_specs=vmem,
        compiler_params=params,
        name="chain_and_face_solves",
    )(recv, pick, flags, const(owner_const))
    back = lax.all_to_all(reply.reshape(devices * 3, 1, LANES), "bricks", 0, 0, tiled=True)
    return pl.pallas_call(
        update_kernel,
        out_shape=(field, field),
        in_specs=[vmem] * 7,
        out_specs=(hbm, hbm),
        scratch_shapes=[
            pltpu.VMEM(calcium.shape, f32),
            pltpu.VMEM(buffer.shape, f32),
            pltpu.VMEM((2 * edge, LANES), f32),
            pltpu.SemaphoreType.DMA((2 * count,)),
        ],
        compiler_params=params,
        name="rank_three_update",
    )(back.reshape(devices * 3, LANES), base, edges, flags, calcium, buffer, jnp.asarray(update_const, jnp.bfloat16))


def body(calcium, buffer, fraction, rates, inverses, neighbors, ranks):
    count, edge = calcium.shape[0], calcium.shape[1]
    devices = lax.axis_size("bricks")
    if edge == GX and devices == edge and count == 2 and 4 * edge == LANES:
        return fast_body(calcium, buffer, fraction, rates, inverses, neighbors, ranks)
    return general_body(calcium, buffer, fraction, rates, inverses, neighbors, ranks)


def solution(mesh):
    in_specs = (
        P("bricks", None, None),
        P("bricks", None, None),
        P("bricks", None, None),
        P("bricks", None, None),
        P("bricks", None, None, None, None),
        P(),
        P(),
    )
    out_specs = (P("bricks", None, None), P("bricks", None, None))
    return jax.shard_map(body, mesh=mesh, in_specs=in_specs, out_specs=out_specs, check_vma=False)
```

```python
from functools import partial
import math

import jax
import jax.numpy as jnp
import numpy as np
from jax import lax
from jax.experimental import pallas as pl
from jax.experimental.pallas import tpu as pltpu
from jax.sharding import PartitionSpec as P

GX = 32


KON = 0.5
KOFF = 0.3
BTOT = 2.0
INFLUX = 0.1


def fetch(table, index):
    rows = jnp.take(table, jnp.maximum(index, 0), axis=0)
    has = (index >= 0).reshape((-1,) + (1,) * (rows.ndim - 1))
    return jnp.where(has, rows, jnp.zeros_like(rows))


def lookup(planes, before, after):
    sides = []
    for d in range(3):
        lower = fetch(planes[:, d, 1], before[d])
        upper = fetch(planes[:, d, 0], after[d])
        sides.append(jnp.stack([lower, upper], 1))
    return jnp.stack(sides, 1)


def coupling(rate_all, neighbors):
    per_dim = []
    for d in range(3):
        mine = rate_all[:, d]
        sides = []
        for side in range(2):
            other = fetch(mine, neighbors[d, side])
            has = (neighbors[d, side] >= 0)[:, None]
            sides.append(jnp.where(has, 2.0 * mine * other / (mine + other), jnp.zeros_like(mine)))
        per_dim.append(jnp.stack(sides, 1))
    return jnp.stack(per_dim, 1)


def end_planes(field):
    count, edge = (field.shape[0], field.shape[2])
    per_dim = []
    for d in range(3):
        first = lax.index_in_dim(field, 0, 2 + d, False).reshape(count, 2, edge * edge)
        last = lax.index_in_dim(field, edge - 1, 2 + d, False).reshape(count, 2, edge * edge)
        per_dim.append(jnp.stack([first, last], 1))
    return jnp.stack(per_dim, 1)


def operator(field, d, rate, glow, gup, hlow, hup):
    axis = 2 + d
    edge = field.shape[axis]
    plane_shape = lax.index_in_dim(field, 0, axis, False).shape
    lower_face = jnp.expand_dims(hlow.reshape(plane_shape), axis)
    upper_face = jnp.expand_dims(hup.reshape(plane_shape), axis)
    upper = jnp.concatenate([lax.slice_in_dim(field, 1, edge, axis=axis), upper_face], axis)
    lower = jnp.concatenate([lower_face, lax.slice_in_dim(field, 0, edge - 1, axis=axis)], axis)
    place = lax.broadcasted_iota(jnp.int32, field.shape, axis)
    inner = rate[:, :, None, None, None]
    c_up = jnp.where(place == edge - 1, gup[:, :, None, None, None], inner)
    c_down = jnp.where(place == 0, glow[:, :, None, None, None], inner)
    return c_up * (upper - field) + c_down * (lower - field)


def reaction(field, fraction):
    count, edge = (field.shape[0], field.shape[2])
    alpha = fraction.reshape(count, edge, edge, edge)
    calc, bound = (field[:, 0], field[:, 1])
    bind = KON * calc * (BTOT - bound) - KOFF * bound
    return jnp.stack([-bind + INFLUX * (1.0 - alpha) / alpha, bind], 1)


def apply_inverse(block, field, d):
    forms = ["psab,psbjk->psajk", "psab,psibk->psiak", "psab,psijb->psija"]
    return jnp.einsum(forms[d], block, field, precision=lax.Precision.HIGHEST)


def line_ends(field, d):
    count, edge = (field.shape[0], field.shape[2])
    first = lax.index_in_dim(field, 0, 2 + d, False).reshape(count, 2, edge * edge)
    last = lax.index_in_dim(field, edge - 1, 2 + d, False).reshape(count, 2, edge * edge)
    return jnp.stack([first, last], 2)


def block_terms(glow, gup, corner):
    v_first, v_last, w_first, w_last = (
        corner[..., 0],
        corner[..., 1],
        corner[..., 2],
        corner[..., 3],
    )
    a00 = 1.0 + glow * v_first
    a01 = gup * w_first
    a10 = glow * v_last
    a11 = 1.0 + gup * w_last
    lq0 = -glow * v_first
    lq1 = -glow * v_last
    up0 = -gup * w_first
    up1 = -gup * w_last
    return (a00, a01, a10, a11, lq0, lq1, up0, up1)


def chain_order(before, rank):
    slots = jnp.arange(before.shape[0], dtype=jnp.int32)
    pointer = jnp.where(before >= 0, before, slots)
    for step in range(GX.bit_length()):
        pointer = jnp.take(pointer, pointer, axis=0)
    sort_key = pointer * GX + rank
    order = jnp.argsort(sort_key)
    inverse_order = jnp.argsort(order)
    return (order, inverse_order)


def shift_down(values):
    return jnp.concatenate([jnp.zeros_like(values[:1]), values[:-1]], 0)


def shift_up(values):
    return jnp.concatenate([values[1:], jnp.zeros_like(values[:1])], 0)


def compose_maps(first_map, second_map):
    e00, e01, e10, e11 = first_map
    l00, l01, l10, l11 = second_map
    n00 = l00 * e00 + l01 * e10
    n01 = l00 * e01 + l01 * e11
    n10 = l10 * e00 + l11 * e10
    n11 = l10 * e01 + l11 * e11
    scale = jnp.abs(n00) + jnp.abs(n01) + jnp.abs(n10) + jnp.abs(n11)
    return (n00 / scale, n01 / scale, n10 / scale, n11 / scale)


def compose_affine(first_map, second_map):
    first_q, first_p = first_map
    second_q, second_p = second_map
    return (first_q * second_q, second_p + second_q * first_p)


def sorted_solve(glow, gup, corner, before, after, order, inverse_order, ends):
    glow = jnp.take(glow, order, axis=0)
    gup = jnp.take(gup, order, axis=0)
    corner = jnp.take(corner, order, axis=0)
    has_b = jnp.take(before, order, axis=0) >= 0
    has_a = jnp.take(after, order, axis=0) >= 0
    arranged = jnp.take(ends, order, axis=0)
    y0 = arranged[:, :, 0]
    y1 = arranged[:, :, 1]
    a00, a01, a10, a11, lq0, lq1, up0, up1 = block_terms(glow, gup, corner)
    maps = (
        -(lq0 * up1 - lq1 * up0),
        a00 * up1 - a10 * up0,
        -(lq0 * a11 - a01 * lq1),
        a00 * a11 - a01 * a10,
    )
    summed = lax.associative_scan(compose_maps, maps, axis=0)
    f1_prev = summed[1] / summed[3]
    fq = shift_down(f1_prev)
    b00 = a00 - lq0 * fq
    b10 = a10 - lq1 * fq
    det = b00 * a11 - a01 * b10
    f0 = (a11 * up0 - a01 * up1) / det
    f1 = (b00 * up1 - b10 * up0) / det
    slope = (-(b00 * lq1 - b10 * lq0) / det)[:, :, None]
    offset = (b00[:, :, None] * y1 - b10[:, :, None] * y0) / det[:, :, None]
    e1 = lax.associative_scan(compose_affine, (slope, offset), axis=0)[1]
    eq = shift_down(e1)
    e0 = (
        a11[:, :, None] * y0 - a01[:, :, None] * y1 - (a11 * lq0 - a01 * lq1)[:, :, None] * eq
    ) / det[:, :, None]
    zp = lax.associative_scan(compose_affine, (-f0[:, :, None], e0), reverse=True, axis=0)[1]
    pn = shift_up(zp)
    zq = e1 - f1[:, :, None] * pn
    low = jnp.where(has_b[:, None, None], zp - shift_down(zq), jnp.zeros_like(zp))
    high = jnp.where(has_a[:, None, None], zq - pn, jnp.zeros_like(zq))
    return jnp.take(jnp.stack([low, high], 2), inverse_order, axis=0)


def correct(local, block, glow, gup, jumps, d):
    axis = 2 + d
    count, edge = (local.shape[0], local.shape[2])
    shape_v = [count, 2, 1, 1, 1]
    shape_v[axis] = edge
    first_col = block[..., 0].reshape(shape_v)
    last_col = block[..., edge - 1].reshape(shape_v)
    plane_shape = lax.index_in_dim(local, 0, axis, False).shape
    low = jnp.expand_dims(jumps[:, :, 0].reshape(plane_shape), axis)
    high = jnp.expand_dims(jumps[:, :, 1].reshape(plane_shape), axis)
    return (
        local
        - glow[:, :, None, None, None] * low * first_col
        - gup[:, :, None, None, None] * high * last_col
    )


def general_body(calcium, buffer, fraction, rates, inverses, neighbors, ranks):
    count, edge = (calcium.shape[0], calcium.shape[1])
    devices = lax.axis_size("bricks")
    square = edge * edge
    per_device = square // devices
    start = lax.axis_index("bricks") * count
    corners = jnp.stack(
        [
            inverses[..., 0, 0],
            inverses[..., edge - 1, 0],
            inverses[..., 0, edge - 1],
            inverses[..., edge - 1, edge - 1],
        ],
        -1,
    )
    rate_all, corner_all = (
        lax.all_gather(rates, "bricks", axis=0, tiled=True),
        lax.all_gather(corners, "bricks", axis=0, tiled=True),
    )
    couple_all = coupling(rate_all, neighbors)
    couple = lax.dynamic_slice_in_dim(couple_all, start, count, 0)
    field = jnp.stack([calcium, buffer], 1).reshape(count, 2, edge, edge, edge)
    planes = end_planes(field).reshape(count, 3, 2, 2, devices, per_device)
    lined = lookup(
        lax.all_to_all(planes, "bricks", split_axis=4, concat_axis=0, tiled=True),
        neighbors[:, 0],
        neighbors[:, 1],
    )
    halos = lax.all_to_all(lined, "bricks", split_axis=0, concat_axis=4, tiled=True).reshape(
        count, 3, 2, 2, square
    )
    lams = [
        operator(
            field, d, rates[:, d], couple[:, d, 0], couple[:, d, 1], halos[:, d, 0], halos[:, d, 1]
        )
        for d in range(3)
    ]
    rhs = field + lams[0] + 2.0 * lams[1] + 2.0 * lams[2] + reaction(field, fraction)

    def solve(right, d):
        block = inverses[:, d]
        local = apply_inverse(block, right, d)
        ends = line_ends(local, d).reshape(count, 2, 2, devices, per_device)
        order, inverse_order = chain_order(neighbors[d, 0], ranks[d])
        chain_fn = partial(
            sorted_solve,
            couple_all[:, d, 0],
            couple_all[:, d, 1],
            corner_all[:, d],
            neighbors[d, 0],
            neighbors[d, 1],
            order,
            inverse_order,
        )
        lined_jumps = chain_fn(
            lax.all_to_all(ends, "bricks", split_axis=3, concat_axis=0, tiled=True)[:, :, :, 0]
        )[:, :, :, None]
        jumps = lax.all_to_all(
            lined_jumps, "bricks", split_axis=0, concat_axis=3, tiled=True
        ).reshape(count, 2, 2, square)
        return correct(local, block, couple[:, d, 0], couple[:, d, 1], jumps, d)

    first = solve(rhs, 0)
    second = solve(first - lams[1], 1)
    third = solve(second - lams[2], 2)
    result = third.reshape(count, 2, edge, edge * edge)
    return (result[:, 0], result[:, 1])


LANES = 128


ROWS = 5


def cosine_basis(edge):
    wave = np.arange(edge)[:, None]
    place = np.arange(edge)[None, :]
    basis = np.sqrt(2.0 / edge) * np.cos(np.pi * wave * (place + 0.5) / edge)
    basis[0] = math.sqrt(1.0 / edge)
    eigen = 2.0 - 2.0 * np.cos(np.pi * np.arange(edge) / edge)
    return basis, eigen


def parts_of(x):
    high = x.astype(jnp.bfloat16).astype(jnp.float32)
    rest = x - high
    middle = rest.astype(jnp.bfloat16).astype(jnp.float32)
    return high, middle, rest - middle


LEFT = (0, 0, 0, 1, 1, 2)
RIGHT = (0, 1, 2, 0, 1, 0)


def left_of(x):
    parts = parts_of(x)
    return jnp.concatenate([parts[p] for p in LEFT], 1)


def right_of(x, axis=0):
    parts = parts_of(x)
    return jnp.concatenate([parts[p] for p in RIGHT], axis)


def exact_of(x):
    return jnp.concatenate(parts_of(x), 1)


def dot(a, b):
    return jnp.dot(a, b, preferred_element_type=jnp.float32)


def dot_lanes(a, b):
    return lax.dot_general(a, b, (((1,), (1,)), ((), ())), preferred_element_type=jnp.float32)


def host_parts(x):
    parts = []
    for _ in range(3):
        parts.append(x.astype(jnp.bfloat16).astype(np.float64))
        x = x - parts[-1]
    return parts


def host_left(x):
    parts = host_parts(x)
    return np.concatenate([parts[p] for p in LEFT], 1)


def host_right(x):
    parts = host_parts(x)
    return np.concatenate([parts[p] for p in RIGHT], 0)


def lane_of(shape):
    return lax.broadcasted_iota(jnp.int32, shape, len(shape) - 1)


def swap_blocks(four):
    x0, x1, x2, x3 = four
    lane = lane_of(x0.shape)
    low = (lane & 64) == 0
    y0, y2 = jnp.where(low, x0, pltpu.roll(x2, 64, 1)), jnp.where(low, pltpu.roll(x0, 64, 1), x2)
    y1, y3 = jnp.where(low, x1, pltpu.roll(x3, 64, 1)), jnp.where(low, pltpu.roll(x1, 64, 1), x3)
    even = (lane & 32) == 0
    z0, z1 = jnp.where(even, y0, pltpu.roll(y1, 32, 1)), jnp.where(even, pltpu.roll(y0, 96, 1), y1)
    z2, z3 = jnp.where(even, y2, pltpu.roll(y3, 32, 1)), jnp.where(even, pltpu.roll(y2, 96, 1), y3)
    return [z0, z1, z2, z3]


def swap_rows(source, base, scratch, at, edge):
    tiles = edge // 4
    for c in range(tiles):
        rows = [source[pl.ds(base + edge * c + g, tiles, stride=4), :] for g in range(4)]
        for t4, row in enumerate(swap_blocks(rows)):
            scratch[pl.ds(at + 4 * c + t4, tiles, stride=edge), :] = row


def tile_rows(x, edge):
    tiles = edge // 4
    return jnp.concatenate([x[:, LANES * c : LANES * (c + 1)] for c in range(tiles)], 0)


def wide(ref, at, edge):
    tiles = edge // 4
    return jnp.concatenate([ref[pl.ds(at + edge * c, edge), :] for c in range(tiles)], 1)


def swap_inner(refs, edge):
    tiles = edge // 4
    fields = [(ref, b) for ref in refs for b in range(ref.shape[0])]
    whole = [
        exact_of(jnp.concatenate([ref[b, :, LANES * c : LANES * (c + 1)] for ref, b in fields], 0))
        for c in range(tiles)
    ]
    row = lax.broadcasted_iota(jnp.int32, (LANES, LANES), 0)
    lane = lane_of((LANES, LANES))
    for to in range(tiles):
        total = jnp.zeros((len(fields) * edge, LANES), jnp.float32)
        for c in range(tiles):
            hit = ((row & (edge - 1)) == 4 * to + lane // edge) & ((lane & (edge - 1)) == 4 * c + row // edge)
            hit = hit.astype(jnp.float32)
            total = total + dot(whole[c], jnp.concatenate([hit] * 3, 0))
        for f, (ref, b) in enumerate(fields):
            ref[b, :, LANES * to : LANES * (to + 1)] = total[edge * f : edge * (f + 1)]


def normal_of(near, slot):
    along_j = (near[1, 0, slot] >= 0) | (near[1, 1, slot] >= 0)
    return jnp.where(along_j, 1, 2)


def message_kernel(
    near_in, rates_in, calcium_in, buffer_in, fraction_in, inverses_in, const_in,
    msg, solved,
    near, rates, calcium, buffer, fraction, inverses, const, sems,
):
    count, edge = calcium.shape[0], calcium.shape[1]
    tiles = edge // 4
    size = tiles * edge
    copies = [
        pltpu.make_async_copy(source, target, sems.at[x])
        for x, (source, target) in enumerate(
            (
                (calcium_in, calcium),
                (buffer_in, buffer),
                (fraction_in, fraction),
                (inverses_in, inverses),
                (near_in, near),
                (rates_in, rates),
                (const_in, const),
            )
        )
    ]
    for copy in copies:
        copy.start()
    first_slot = lax.axis_index("bricks") * count
    for copy in copies:
        copy.wait()
    normal = normal_of(near, first_slot)
    closed = 3 - normal

    @pl.when(normal == 1)
    def _():
        swap_inner((calcium, buffer, fraction), edge)

    lane = lane_of((edge, LANES))
    inner = lane & (edge - 1)
    square_row = lax.broadcasted_iota(jnp.int32, (LANES, LANES), 0)
    square_lane = lane_of((LANES, LANES))
    on_block = (square_row // edge) == (square_lane // edge)
    faces_u, faces_y, ends0, ends1 = [], [], [], []
    for b in range(count):
        face = jnp.where(near[normal, 1, first_slot + b] >= 0, edge - 1, 0)
        calc = [calcium[b, :, LANES * c : LANES * (c + 1)] for c in range(tiles)]
        bound = [buffer[b, :, LANES * c : LANES * (c + 1)] for c in range(tiles)]
        alpha = [fraction[b, :, LANES * c : LANES * (c + 1)] for c in range(tiles)]
        bind = [KON * x * (BTOT - y) - KOFF * y for x, y in zip(calc, bound)]
        source_calc = [INFLUX / a - (w + INFLUX) for w, a in zip(bind, alpha)]
        for q, (u, source) in enumerate(((calc, source_calc), (bound, bind))):
            at = size * (2 * b + q)
            rate_t, rate_n = 2.0 * rates[b, q, closed], 2.0 * rates[b, q, normal]
            ahead = [pltpu.roll(x, LANES - edge, 1) for x in u]
            behind = [pltpu.roll(x, edge, 1) for x in u]
            f = []
            for c in range(tiles):
                x = u[c]
                next_t = jnp.where(lane < LANES - edge, ahead[c], ahead[c + 1] if c + 1 < tiles else x)
                last_t = jnp.where(lane >= edge, behind[c], behind[c - 1] if c else x)
                next_n = jnp.where(inner == edge - 1, x, pltpu.roll(x, LANES - 1, 1))
                last_n = jnp.where(inner == 0, x, pltpu.roll(x, 1, 1))
                twice = x + x
                along = rate_t * (next_t + last_t - twice) + rate_n * (next_n + last_n - twice)
                f.append(twice + along + source[c])
            g = dot(left_of(inverses[b, 0, q]), right_of(jnp.concatenate(f, 1)))
            ends0.append(jnp.concatenate([g[0:1, LANES * c : LANES * (c + 1)] for c in range(tiles)], 0))
            ends1.append(jnp.concatenate([g[edge - 1 : edge, LANES * c : LANES * (c + 1)] for c in range(tiles)], 0))
            w = jnp.concatenate([g[:, LANES * c : LANES * (c + 1)] - 2.0 * u[c] for c in range(tiles)], 0)
            sides = [
                jnp.where(on_block, jnp.concatenate([jnp.concatenate([x.astype(jnp.float32)] * 4, 1)] * 4, 0), 0.0)
                for x in parts_of(inverses[b, normal, q])
            ]
            y = dot(right_of(w, 1), jnp.concatenate([sides[p] for p in LEFT], 0))
            solved[pl.ds(at, size), :] = y
            face_u = jnp.zeros((edge, LANES), jnp.float32)
            face_y = jnp.zeros((edge, LANES), jnp.float32)
            for c in range(tiles):
                shift = (c - face) & (LANES - 1)
                face_u = jnp.where(inner == c, pltpu.roll(u[c], shift, 1), face_u)
                face_y = jnp.where(inner == c, pltpu.roll(y[edge * c : edge * (c + 1)], shift, 1), face_y)
            faces_u.append(face_u)
            faces_y.append(face_y)

    stack = jnp.concatenate(swap_blocks(ends0) + swap_blocks(ends1), 0)
    ends_of = const[:, : 6 * edge].astype(jnp.float32)
    faces_of = const[:, 2 * LANES :].astype(jnp.float32)
    both = dot(ends_of, right_of(jnp.concatenate([stack[:edge], stack[edge:]], 1)))
    part_u = dot_lanes(faces_of, right_of(jnp.concatenate(faces_u, 0), 1))
    part_y = dot_lanes(faces_of, right_of(jnp.concatenate(faces_y, 0), 1))
    fields = swap_blocks([both[:, :LANES], both[:, LANES:], part_u, part_y])
    for x, part in enumerate(fields):
        msg[pl.ds(x, edge, stride=ROWS), :] = part
    row = jnp.zeros((edge, LANES), jnp.float32)
    for b in range(count):
        for q in range(2):
            for x, rate in enumerate((rates[b, q, 0], rates[b, q, closed], rates[b, q, normal])):
                row = jnp.where(lane == (2 * b + q) * edge + x, rate, row)
    msg[pl.ds(4, edge, stride=ROWS), :] = row


def local_kernel(
    near_in, solved_in, inverses_in,
    base, pick, flags, edges,
    near, table, solved, inverses, work, other, sems,
):
    count, edge = inverses.shape[0], inverses.shape[3]
    tiles = edge // 4
    size = tiles * edge
    slots = near.shape[2]
    copies = [
        pltpu.make_async_copy(source, target, sems.at[x])
        for x, (source, target) in enumerate(
            (
                (near_in, near),
                (near_in, table),
                (solved_in, solved),
                (inverses_in, inverses),
            )
        )
    ]
    for copy in copies:
        copy.start()
    for copy in copies[:2]:
        copy.wait()
    normal = normal_of(near, 0)
    closed = 3 - normal
    up = near[normal, 1, 0] >= 0
    touch = up | (near[normal, 0, 0] >= 0)

    lane = lane_of((8, LANES))
    back = jnp.broadcast_to(table[0, 0:1, :], (8, slots))
    back = jnp.concatenate([back] * (LANES // slots), 1)
    pointer = jnp.where(back >= 0, back, lane & (slots - 1))
    place = jnp.where(back >= 0, 1, 0)

    def pull(values, index):
        return jnp.take_along_axis(values, index, axis=1, mode="promise_in_bounds")

    reach = 1
    while reach < edge:
        place = place + pull(place, pointer)
        pointer = pull(pointer, pointer)
        reach *= 2
    chain = jnp.where(pointer == pointer[:, 0:1], 0, edge) + place
    goal = pull(chain, (lane & (edge - 1)) * count + lane // (2 * edge)) + 2 * (lane & edge)
    hit = lax.broadcasted_iota(jnp.int32, (LANES, LANES), 0) == goal[0:1]
    pick[...] = hit.astype(jnp.float32).T
    face = jnp.where(((lane & edge) == 0) == up, edge - 1, 0).astype(jnp.float32)
    depth = lax.broadcasted_iota(jnp.int32, (8, LANES), 0)
    angle = jnp.full((8, LANES), lax.axis_index("bricks")).astype(jnp.float32) * (0.5 * math.pi / edge)
    half = jnp.sin(angle)
    flags[...] = jnp.where(
        depth == 0,
        face,
        jnp.where(
            depth == 1,
            jnp.where(touch, 1.0, 0.0),
            jnp.where(depth == 2, jnp.where(normal == 2, 1.0, 0.0), 4.0 * half * half),
        ),
    )

    for copy in copies[2:]:
        copy.wait()
    first_slot = lax.axis_index("bricks") * count
    for b in range(count):
        face = jnp.where(near[normal, 1, first_slot + b] >= 0, edge - 1, 0)
        for q in range(2):
            x = 2 * b + q
            at = size * x
            swap_rows(solved, at, other, 0, edge)
            whole = dot(left_of(inverses[b, closed, q]), right_of(wide(other, 0, edge)))
            for c in range(tiles):
                other[pl.ds(edge * c, edge), :] = whole[:, LANES * c : LANES * (c + 1)]
            swap_rows(other, 0, work, 0, edge)
            base[pl.ds(at, size), :] = work[...]
            row_n = jnp.concatenate([inverses[b, normal, q, pl.ds(face, 1), :]] * 4, 1)
            edges[x, 0] = jnp.broadcast_to(inverses[b, 0, q, :, 0:1], (edge, LANES))
            edges[x, 1] = jnp.broadcast_to(inverses[b, 0, q, :, edge - 1 : edge], (edge, LANES))
            edges[x, 2] = jnp.broadcast_to(row_n, (edge, LANES))


def owner_kernel(recv, pick, flags, const, out):
    edge = const.shape[0]
    turned = const[:, : 6 * edge]
    basis = const[:, 2 * LANES : 2 * LANES + 6 * edge]
    lam, v_first, v_last = (const[:, LANES * x : LANES * (x + 1)] for x in (4, 5, 6))
    face, touch, normal_2, my_lam = flags[0:1], flags[1:2], flags[2:3], flags[3:4]

    hit = pick[...]
    data = jnp.concatenate([recv[pl.ds(x, edge, stride=ROWS), :] for x in range(4)], 0).T
    tail = recv[pl.ds(4, edge, stride=ROWS), :]
    tail = jnp.concatenate([tail] + [pltpu.roll(tail, LANES - edge * x, 1) for x in range(1, 4)], 0).T[:16]
    hits = jnp.concatenate([hit] * 3, 0)
    params = dot(exact_of(tail), hits)
    rate_0, rate_t, rate_n = params[0:1], params[1:2], params[2:3]
    parts = dot(exact_of(data), hits)
    y0, y1, face_u, face_y = (parts[edge * x : edge * (x + 1)] for x in range(4))

    lane = lane_of((1, LANES))
    place = lane & (edge - 1)
    first_row = (lane & edge) == 0

    def partner(x):
        return jnp.where(first_row, pltpu.roll(x, LANES - edge, 1), pltpu.roll(x, edge, 1))

    def after(x, s=1):
        return pltpu.roll(x, LANES - s, 1)

    def before(x, s=1):
        return pltpu.roll(x, s, 1)

    damp_0 = 1.0 / (1.0 + lam * rate_0)
    damp_n = 1.0 / (1.0 + lam * rate_n)
    damp_t = 1.0 / (1.0 + my_lam * rate_t)
    other_n = partner(rate_n)
    g = jnp.where(touch > 0.5, 2.0 * rate_n * other_n / (rate_n + other_n), 0.0)
    cross = partner(face_u) - face_u
    near_c = jnp.sum(damp_0 * v_first * v_first, 0, keepdims=True)
    far_c = jnp.sum(damp_0 * v_first * v_last, 0, keepdims=True)
    end_n = jnp.sum(damp_n * v_first * v_first, 0, keepdims=True)
    open_face = place < edge - 1
    right = jnp.where(open_face, y1 - after(y0), 0.0)
    both = dot(basis, right_of(jnp.concatenate([cross, right], 1)))
    damped = damp_0 * (2.0 * g) * both[:, :LANES]
    pieces = dot(turned, right_of(jnp.concatenate([damped, damp_0 * v_first, damp_0 * v_last], 1)))
    spread, col_0, col_1 = (pieces[:, LANES * x : LANES * (x + 1)] for x in range(3))
    v_face = jnp.where(face < 0.5, v_first, v_last)
    at_first = v_face * jnp.sum(v_first * damped, 0, keepdims=True)
    at_last = v_face * jnp.sum(v_last * damped, 0, keepdims=True)
    right = both[:, LANES:] + jnp.where(open_face, at_last - after(at_first), 0.0)

    inv_rate = 1.0 / rate_0
    diag = jnp.where(open_face, 0.5 * (inv_rate + after(inv_rate)) + near_c + after(near_c), 1.0)
    lower = jnp.where(open_face & (place > 0), -far_c, 0.0)
    upper = jnp.where(place < edge - 2, -after(far_c), 0.0)
    def shift(x, by):
        return x if by == 0 else pltpu.roll(x, -by % LANES, 1)

    def reduced(near_by, at, s):
        (dm, lm, um, rm), (d, l, u, r), (dp, lp, up, rp) = (near_by[at + x * s] for x in (-1, 0, 1))
        back, fore = -l / dm, -u / dp
        return d + back * um + fore * lp, back * lm, fore * up, r + back * rm + fore * rp

    system = (diag, lower, upper, right)
    step, total = 1, (edge - 1).bit_length()
    for levels in (3, total - 3):
        reach = 2**levels - 1
        rows_by = {x * step: tuple(shift(y, x * step) for y in system) for x in range(-reach, reach + 1)}
        for level in range(levels):
            reach = 2**levels - 2 ** (level + 1)
            now = step * 2**level
            rows_by = {
                x * step: reduced(rows_by, x * step, now)
                for x in range(-reach, reach + 1, 2 ** (level + 1))
            }
        system = rows_by[0]
        step *= 2**levels
    diag, lower, upper, right = system
    flux_up = right / diag
    flux_down = jnp.where(place > 0, before(flux_up), 0.0)

    weight_down = jnp.sum(damp_n * v_face * flux_down, 0, keepdims=True)
    weight_up = jnp.sum(damp_n * v_face * flux_up, 0, keepdims=True)
    ends = face_y + end_n * spread + col_0 * weight_down - col_1 * weight_up
    ends = jnp.where(normal_2 > 0.5, damp_t, 1.0) * ends
    jump = g / (1.0 + g * (end_n + partner(end_n))) * (ends - partner(ends))
    face_out = jnp.where(normal_2 > 0.5, damp_t * spread - jump, damp_t * (spread - jump))
    damp_nt = damp_n * damp_t
    lines = dot(turned, right_of(jnp.concatenate([damp_nt * flux_down, damp_nt * flux_up], 1)))
    packed = jnp.concatenate(
        [lines[:, :LANES], lines[:, LANES:], face_out, jnp.zeros((edge, LANES), jnp.float32)], 0
    )
    reply = dot_lanes(jnp.concatenate([hit] * 3, 1), exact_of(packed))
    kinds = swap_blocks([reply[edge * x : edge * (x + 1)] for x in range(4)])
    for x in range(3):
        out[pl.ds(x, edge, stride=3), :] = kinds[x]


def update_kernel(
    recv, base, edges, flags, calcium, buffer, const,
    calcium_out, buffer_out,
    calcium_next, buffer_next, work, sems,
):
    count, edge = calcium.shape[0], calcium.shape[1]
    tiles = edge // 4
    size = tiles * edge
    swapped = flags[2, 0] < 0.5
    old = jnp.where(flags[2:3] < 0.5, 0.0, 1.0)
    low, high, face_part = (recv[pl.ds(x, edge, stride=3), :] for x in range(3))
    parts = [part.astype(jnp.float32) for part in parts_of(face_part)]
    turn = jnp.concatenate([parts[p] for p in LEFT] + [jnp.zeros_like(parts[0])] * 2, 0)
    turn = turn.T[:, : 6 * edge]
    face_wide = dot(turn, const[:, 2 * LANES :].astype(jnp.float32))
    lines = dot(const[:edge, : 6 * edge].astype(jnp.float32), right_of(jnp.concatenate([low, high], 1)))
    rows = []
    for e in range(2):
        work[pl.ds(edge * e, edge), :] = lines[:, LANES * e : LANES * (e + 1)]
        rows.append(swap_blocks([work[pl.ds(edge * e + t4, tiles, stride=4), :] for t4 in range(4)]))

    stores = [
        pltpu.make_async_copy(source.at[b], to.at[b], sems.at[2 * b + q])
        for b in range(count)
        for q, (source, to) in enumerate(((calcium_next, calcium_out), (buffer_next, buffer_out)))
    ]
    for b in range(count):
        for q, (ref, now) in enumerate(((calcium_next, calcium), (buffer_next, buffer))):
            x = 2 * b + q
            at = size * x
            col_0, col_1, row_n = edges[x, 0], edges[x, 1], edges[x, 2]
            for c in range(tiles):
                part = slice(LANES * c, LANES * (c + 1))
                ref[b, :, part] = (
                    (base[pl.ds(at + edge * c, edge), :] + old * now[b, :, part])
                    + face_wide[edge * x : edge * (x + 1), part] * row_n
                    + (col_0 * rows[0][x][c : c + 1] - col_1 * rows[1][x][c : c + 1])
                )
        stores[2 * b].start()
        stores[2 * b + 1].start()
    for store in stores:
        store.wait()

    @pl.when(swapped)
    def _():
        swap_inner((calcium_next, buffer_next), edge)
        calcium_next[...] = calcium_next[...] + calcium[...]
        buffer_next[...] = buffer_next[...] + buffer[...]
        for store in stores:
            store.start()
        for store in stores:
            store.wait()


def fast_body(calcium, buffer, fraction, rates, inverses, neighbors, ranks):
    count, edge = calcium.shape[0], calcium.shape[1]
    devices = lax.axis_size("bricks")
    tiles = edge // 4
    size = tiles * edge
    f32 = jnp.float32
    basis, eigen = cosine_basis(edge)
    place = np.arange(edge)
    ends_of = np.zeros((edge, edge))
    ends_of[:, (place % 4) * tiles + place // 4] = basis
    faces_of = np.zeros((edge, LANES))
    faces_of[:, (place % 4) * edge + place // 4] = basis
    pad = lambda x: np.pad(x, ((0, 0), (0, 2 * LANES - x.shape[1])))
    message_const = np.concatenate([pad(host_left(ends_of)), host_left(faces_of)], 1)
    lanes_of = lambda x: np.tile(x[:, None], (1, LANES))
    owner_const = np.concatenate(
        [pad(host_left(basis.T)), pad(host_left(basis))]
        + [lanes_of(x) for x in (eigen, basis[:, 0], basis[:, -1])],
        1,
    )
    expand = host_right(np.repeat(basis, edge, 1))
    back_const = np.pad(pad(host_left(basis.T)), ((0, 5 * edge), (0, 0)))
    update_const = np.concatenate([back_const, expand], 1)
    smem = pl.BlockSpec(memory_space=pltpu.SMEM)
    vmem = pl.BlockSpec(memory_space=pltpu.VMEM)
    hbm = pl.BlockSpec(memory_space=pltpu.HBM)
    params = pltpu.CompilerParams(vmem_limit_bytes=48 * 2**20)
    const = lambda x: jnp.asarray(x, f32)
    field = jax.ShapeDtypeStruct(calcium.shape, f32)
    tall = jax.ShapeDtypeStruct((2 * count * size, LANES), f32)

    stay = lambda x: pltpu.with_memory_space_constraint(x, pltpu.HBM)
    msg, solved = pl.pallas_call(
        message_kernel,
        out_shape=(jax.ShapeDtypeStruct((devices * ROWS, LANES), f32), tall),
        in_specs=[hbm] * 7,
        out_specs=(vmem, vmem),
        scratch_shapes=[
            pltpu.SMEM(neighbors.shape, jnp.int32),
            pltpu.SMEM((count, 2, 3), f32),
            pltpu.VMEM(calcium.shape, f32),
            pltpu.VMEM(calcium.shape, f32),
            pltpu.VMEM(fraction.shape, f32),
            pltpu.VMEM(inverses.shape, f32),
            pltpu.VMEM(message_const.shape, jnp.bfloat16),
            pltpu.SemaphoreType.DMA((7,)),
        ],
        compiler_params=pltpu.CompilerParams(vmem_limit_bytes=48 * 2**20),
        name="message",
    )(*(stay(x) for x in (neighbors, rates.transpose(0, 2, 1), calcium, buffer, fraction, inverses, jnp.asarray(message_const, jnp.bfloat16))))
    recv = lax.all_to_all(msg.reshape(devices * ROWS, 1, LANES), "bricks", 0, 0, tiled=True).reshape(devices * ROWS, LANES)
    base, pick, flags, edges = pl.pallas_call(
        local_kernel,
        out_shape=(
            tall,
            jax.ShapeDtypeStruct((LANES, LANES), f32),
            jax.ShapeDtypeStruct((8, LANES), f32),
            jax.ShapeDtypeStruct((2 * count, 3, edge, LANES), f32),
        ),
        in_specs=[hbm] * 3,
        out_specs=(vmem,) * 4,
        scratch_shapes=[
            pltpu.SMEM(neighbors.shape, jnp.int32),
            pltpu.VMEM(neighbors.shape, jnp.int32),
            pltpu.VMEM(tall.shape, f32),
            pltpu.VMEM(inverses.shape, f32),
            pltpu.VMEM((size, LANES), f32),
            pltpu.VMEM((size, LANES), f32),
            pltpu.SemaphoreType.DMA((4,)),
        ],
        compiler_params=pltpu.CompilerParams(vmem_limit_bytes=48 * 2**20),
        cost_estimate=pl.CostEstimate(flops=2 * 10**7, bytes_accessed=4 * 10**6, transcendentals=0),
        name="local_solution",
    )(neighbors, solved, inverses)
    reply = pl.pallas_call(
        owner_kernel,
        out_shape=jax.ShapeDtypeStruct((devices * 3, LANES), f32),
        in_specs=[vmem] * 4,
        out_specs=vmem,
        compiler_params=params,
        name="chain_and_face_solves",
    )(recv, pick, flags, const(owner_const))
    back = lax.all_to_all(reply.reshape(devices * 3, 1, LANES), "bricks", 0, 0, tiled=True)
    return pl.pallas_call(
        update_kernel,
        out_shape=(field, field),
        in_specs=[vmem] * 7,
        out_specs=(hbm, hbm),
        scratch_shapes=[
            pltpu.VMEM(calcium.shape, f32),
            pltpu.VMEM(buffer.shape, f32),
            pltpu.VMEM((2 * edge, LANES), f32),
            pltpu.SemaphoreType.DMA((2 * count,)),
        ],
        compiler_params=params,
        name="rank_three_update",
    )(back.reshape(devices * 3, LANES), base, edges, flags, calcium, buffer, jnp.asarray(update_const, jnp.bfloat16))


def body(calcium, buffer, fraction, rates, inverses, neighbors, ranks):
    count, edge = calcium.shape[0], calcium.shape[1]
    devices = lax.axis_size("bricks")
    if edge == GX and devices == edge and count == 2 and 4 * edge == LANES:
        return fast_body(calcium, buffer, fraction, rates, inverses, neighbors, ranks)
    return general_body(calcium, buffer, fraction, rates, inverses, neighbors, ranks)


def solution(mesh):
    in_specs = (
        P("bricks", None, None),
        P("bricks", None, None),
        P("bricks", None, None),
        P("bricks", None, None),
        P("bricks", None, None, None, None),
        P(),
        P(),
    )
    out_specs = (P("bricks", None, None), P("bricks", None, None))
    return jax.shard_map(body, mesh=mesh, in_specs=in_specs, out_specs=out_specs, check_vma=False)
```
